32 devices in a mesh: dp: 16 (over z, y, x), copy: 2 (over core).
Axes of the slice: x: 2, y: 2, z: 4, core: 2. Of those that a mesh axis runs over, the one named last changes fastest.
Arguments:
- patches: bfloat16 [16, 1024, 64], P('dp'), may hold values from -6 to 6
- noise_copies: bfloat16 [2, 16, 1024, 64], P('copy', 'dp'), may hold values from -6 to 6
- image_ids: int32 [16, 1024], P('dp'), may hold values from 0 to 2, never falling along the last dimension, each value on 1 to 512 neighbouring positions
- buffer_flags: int32 [16, 1024], P('dp'), may hold values 0 or 1
- loss_mask: int32 [16, 1024], P('dp'), may hold values 0 or 1
- timesteps: int32 [2, 16, 1024], P('copy', 'dp'), may hold values from 0 to 999
- attend_weight: float32 [8, 768, 768], P(None, ('dp', 'copy'))
- attend_velocity: float32 [8, 768, 768], P(None, ('dp', 'copy')), may hold values from -1.1920929e-06 to 1.1920929e-06
- expand_weight: float32 [4, 3072, 768], P(None, ('dp', 'copy')), may hold values from -0.21875 to 0.21875
- expand_velocity: float32 [4, 3072, 768], P(None, ('dp', 'copy')), may hold values from -1.1920929e-06 to 1.1920929e-06
- dense_weight: float32 [2, 1024, 1024], P(None, ('dp', 'copy')), may hold values from -0.1875 to 0.1875
- dense_velocity: float32 [2, 1024, 1024], P(None, ('dp', 'copy')), may hold values from -1.1920929e-06 to 1.1920929e-06
- modulate_weight: float32 [5120, 1024], P(('dp', 'copy')), may hold values from -0.1875 to 0.1875
- modulate_velocity: float32 [5120, 1024], P(('dp', 'copy')), may hold values from -1.1920929e-06 to 1.1920929e-06
- condition_weight: float32 [1024, 768], P(('dp', 'copy')), may hold values from -0.21875 to 0.21875
- condition_velocity: float32 [1024, 768], P(('dp', 'copy')), may hold values from -1.1920929e-06 to 1.1920929e-06
- encoder_table: float32 [1100, 768], P(None, ('dp', 'copy'))
- encoder_first: float32 [1100, 768], P(None, ('dp', 'copy')), may hold values from -1.1920929e-07 to 1.1920929e-07
- encoder_second: float32 [1100, 768], P(None, ('dp', 'copy')), may hold values from 1.1054302e-15 to 1.7856949e-14
- head_table: float32 [384, 1024], P(None, ('dp', 'copy'))
- head_first: float32 [384, 1024], P(None, ('dp', 'copy')), may hold values from -1.1920929e-07 to 1.1920929e-07
- head_second: float32 [384, 1024], P(None, ('dp', 'copy')), may hold values from 1.1054302e-15 to 1.7856949e-14
Outputs:
- loss_sum: float32 [], replicated
- loss_count: float32 [], replicated
- clip_norm: float32 [], replicated
- attend_master: float32 [8, 768, 768], P(None, ('dp', 'copy'))
- attend_momentum: float32 [8, 768, 768], P(None, ('dp', 'copy'))
- expand_master: float32 [4, 3072, 768], P(None, ('dp', 'copy'))
- expand_momentum: float32 [4, 3072, 768], P(None, ('dp', 'copy'))
- dense_master: float32 [2, 1024, 1024], P(None, ('dp', 'copy'))
- dense_momentum: float32 [2, 1024, 1024], P(None, ('dp', 'copy'))
- modulate_master: float32 [5120, 1024], P(('dp', 'copy'))
- modulate_momentum: float32 [5120, 1024], P(('dp', 'copy'))
- condition_master: float32 [1024, 768], P(('dp', 'copy'))
- condition_momentum: float32 [1024, 768], P(('dp', 'copy'))
- encoder_master: float32 [1100, 768], P(None, ('dp', 'copy'))
- encoder_firsts: float32 [1100, 768], P(None, ('dp', 'copy'))
- encoder_seconds: float32 [1100, 768], P(None, ('dp', 'copy'))
- table_master: float32 [384, 1024], P(None, ('dp', 'copy'))
- table_firsts: float32 [384, 1024], P(None, ('dp', 'copy'))
- table_seconds: float32 [384, 1024], P(None, ('dp', 'copy'))
The draws below stay inside these ranges and needn't reach their ends.
Inputs may be any that keep to these rules, and one draw needn't show every extreme that they name: `image_ids`: numbered from 0 along each sequence, never falling; each image has 1 to 512 tokens, one exactly that many.
All inputs are finite; a program needn't handle non-finite values. No bound on the sum of `buffer_flags` or of `loss_mask` on one device may be relied on, other than what follows from the above.
Results may differ from the reference program's by a relative error of at most 0.0023.
The reference program's roundings to bfloat16 on the way count: a program that leaves them out, or rounds other values in their place, can miss the bound.
Values may be sent and summed in bfloat16 or wider, within the bound.
No kernel may reach another device: no remote copies, remote signals or barrier semaphores. Data moves between devices by JAX's collectives and lax.ppermute only.
A program may use at most 448 MiB of HBM per device.

```python
import math
import jax
import jax.numpy as jnp
import numpy as np
from jax import lax

D = 768
HEADS = 12
HD = 64
FF = 3072
HW = 1024
PATCH = 64
FREQ = 256
SEQ = 1024
IMAGES = 3
NS_STEPS = 2
STEP = 10
TSTEPS = 1000
SEQS = 16
COPIES = 2
P_ALL = 23520256


def draw_attend_weight(key, part):
    key = jax.random.fold_in(key, 1)
    base = jax.random.normal(key, (8, D, D), jnp.float32) * D ** (-0.5)
    return base * jnp.array([1.0, 1.0, 1.0, 4.0, 1.0, 1.0, 1.0, 4.0], jnp.float32)[:, None, None]


def draw_encoder_table(key, part):
    key = jax.random.fold_in(key, 2)
    base = jax.random.normal(key, (12 + PATCH + SEQ, D), jnp.float32)
    leading = jnp.array([0.2, 0.3, 0.2, 0.3, 0.2, 0.3, 0.2, 0.3, 0.2, 0.3, 1.0, 1.0], jnp.float32)
    row_factor = jnp.concatenate([leading, jnp.full((PATCH,), PATCH ** (-0.5), jnp.float32), jnp.full((SEQ,), 0.5, jnp.float32)])
    offsets = jnp.concatenate([jnp.array([1.0, 0.0, 1.0, 0.0, 1.0, 0.0, 1.0, 0.0, 1.0, 0.0, 0.0, 0.0], jnp.float32), jnp.zeros((PATCH + SEQ,), jnp.float32)])
    return base * row_factor[:, None] + offsets[:, None]


def draw_head_table(key, part):
    key = jax.random.fold_in(key, 3)
    base = jax.random.normal(key, (2 * PATCH + FREQ, HW), jnp.float32)
    row_factor = jnp.concatenate([jnp.full((PATCH,), PATCH ** (-0.5), jnp.float32), jnp.full((FREQ,), FREQ ** (-0.5), jnp.float32), jnp.full((PATCH,), HW ** (-0.5), jnp.float32)])
    return base * row_factor[:, None]


def touch_ends(result, rng, smallest, largest):
    place = [jax.random.randint(jax.random.fold_in(rng, axis), (), 0, length) for axis, length in enumerate(result.shape)]
    widest = result.shape.index(max(result.shape))
    neighbour = place[:widest] + [(place[widest] + 1) % result.shape[widest]] + place[widest + 1:]
    return result.at[tuple(place)].set(smallest).at[tuple(neighbour)].set(largest)


def level_of(stream_key, dims, cuts, smallest, top_value):
    level = 1.0
    for dim, shards_of in cuts:
        draws = jax.random.uniform(jax.random.fold_in(jax.random.fold_in(stream_key, 6), dim), (shards_of,), jnp.float32, smallest / len(cuts), top_value / len(cuts))
        level = level * jnp.repeat(jnp.exp(draws), dims[dim] // shards_of).reshape((-1,) + (1,) * (len(dims) - 1 - dim))
    return level


def split_up(amount, total, limit, lean):
    weights = [(1 << 20) // math.isqrt(rank ** lean) + 1 for rank in range(2, amount + 1)]
    rest, holding = total - limit - (amount - 1), [1] * (amount - 1)
    while rest > 0:
        candidates = [i for i in range(amount - 1) if holding[i] < limit]
        whole, left = sum([weights[i] for i in candidates]), rest
        for i in candidates:
            addition = min(limit - holding[i], max(1, left * weights[i] // whole), rest)
            holding[i] = holding[i] + addition
            rest = rest - addition
    return np.array([limit] + holding)


def ragged_sizes(key, count, total, reach, skew):
    if count == 2:
        one = jax.random.randint(key, (), max(1, total - reach), min(reach, total - 1) + 1)
        return jnp.stack([one, total - one])
    tallies = jnp.asarray(split_up(count, total, reach, skew), jnp.int32)
    couples = (count - 1) // 2
    donor, receiver = tallies[1:1 + 2 * couples:2], tallies[2:2 + 2 * couples:2]
    room = jnp.minimum(donor - 1, reach - receiver)
    passed = jax.random.randint(jax.random.fold_in(key, 1), (couples,), 0, 1 << 20) % (room + 1)
    tallies = tallies.at[1:1 + 2 * couples:2].set(donor - passed).at[2:2 + 2 * couples:2].set(receiver + passed)
    return tallies[jax.random.permutation(jax.random.fold_in(key, 2), count)]


def scatter_about(stream_key, dims, deviation, bound, cuts=(), held_as=jnp.bfloat16):
    values = jax.random.normal(stream_key, dims, jnp.float32) * deviation
    if len(cuts) > 0:
        values = level_of(stream_key, dims, cuts, -0.22, 0.18) * values
    return jnp.clip(values, min=-bound, max=bound).astype(held_as)


def setup_inputs(seed: int = 0) -> dict:
    key_of = jax.random.split(jax.random.key(seed), 23)
    patches = scatter_about(key_of[0], (SEQS, SEQ, PATCH), 1.0, 6.0, ((0, 16),))
    noise_copies = scatter_about(key_of[1], (COPIES, SEQS, SEQ, PATCH), 1.0, 6.0, ((0, 2), (1, 16)))
    image_ids = jax.vmap(lambda own: jnp.searchsorted(jnp.cumsum(ragged_sizes(own, IMAGES, SEQ, SEQ // 2, 0)), jnp.arange(SEQ), side="right"))(jax.random.split(key_of[2], SEQS)).reshape((SEQS, SEQ)).astype(jnp.int32)
    buffer_flags = touch_ends((jax.random.randint(key_of[3], (SEQS, SEQ), 0, 16) < 1).astype(jnp.int32), jax.random.fold_in(key_of[3], 1), 0, 1)
    loss_mask = touch_ends((jax.random.randint(key_of[4], (SEQS, SEQ), 0, 10) < 7).astype(jnp.int32), jax.random.fold_in(key_of[4], 1), 0, 1)
    timesteps = touch_ends(jax.random.randint(key_of[5], (COPIES, SEQS, SEQ), 0, TSTEPS), jax.random.fold_in(key_of[5], 1), 0, TSTEPS - 1).astype(jnp.int32)
    attend_weight = draw_attend_weight(jax.random.fold_in(key_of[22], 71), 0)
    attend_velocity = scatter_about(key_of[7], (8, D, D), (0.001 * P_ALL ** -0.5), 1.1920928955078125e-06, ((1, 32),), jnp.float32)
    expand_weight = scatter_about(key_of[8], (4, FF, D), D ** -0.5, 0.21875, ((1, 32),), jnp.float32)
    expand_velocity = scatter_about(key_of[9], (4, FF, D), (0.001 * P_ALL ** -0.5), 1.1920928955078125e-06, ((1, 32),), jnp.float32)
    dense_weight = scatter_about(key_of[10], (2, HW, HW), HW ** -0.5, 0.1875, ((1, 32),), jnp.float32)
    dense_velocity = scatter_about(key_of[11], (2, HW, HW), (0.001 * P_ALL ** -0.5), 1.1920928955078125e-06, ((1, 32),), jnp.float32)
    modulate_weight = scatter_about(key_of[12], (5 * HW, HW), HW ** -0.5, 0.1875, ((0, 32),), jnp.float32)
    modulate_velocity = scatter_about(key_of[13], (5 * HW, HW), (0.001 * P_ALL ** -0.5), 1.1920928955078125e-06, ((0, 32),), jnp.float32)
    condition_weight = scatter_about(key_of[14], (HW, D), D ** -0.5, 0.21875, ((0, 32),), jnp.float32)
    condition_velocity = scatter_about(key_of[15], (HW, D), (0.001 * P_ALL ** -0.5), 1.1920928955078125e-06, ((0, 32),), jnp.float32)
    encoder_table = draw_encoder_table(jax.random.fold_in(key_of[22], 71), 0)
    encoder_first = scatter_about(key_of[17], (12 + PATCH + SEQ, D), (1.1e-4 * P_ALL ** -0.5), 1.1920928955078125e-07, ((1, 32),), jnp.float32)
    encoder_second = jnp.clip(jnp.exp(math.log(1.7856948694239608e-14) - 2.7821581 * jax.random.uniform(key_of[18], (12 + PATCH + SEQ, D), jnp.float32) ** level_of(key_of[18], (12 + PATCH + SEQ, D), ((1, 32),), -0.2, 0.2)), 1.1054301945722365e-15, 1.7856948694239608e-14)
    head_table = draw_head_table(jax.random.fold_in(key_of[22], 71), 0)
    head_first = scatter_about(key_of[20], (2 * PATCH + FREQ, HW), (1.1e-4 * P_ALL ** -0.5), 1.1920928955078125e-07, ((1, 32),), jnp.float32)
    head_second = jnp.clip(jnp.exp(math.log(1.7856948694239608e-14) - 2.7821581 * jax.random.uniform(key_of[21], (2 * PATCH + FREQ, HW), jnp.float32) ** level_of(key_of[21], (2 * PATCH + FREQ, HW), ((1, 32),), -0.2, 0.2)), 1.1054301945722365e-15, 1.7856948694239608e-14)
    return dict(patches=patches, noise_copies=noise_copies, image_ids=image_ids, buffer_flags=buffer_flags, loss_mask=loss_mask, timesteps=timesteps, attend_weight=attend_weight, attend_velocity=attend_velocity, expand_weight=expand_weight, expand_velocity=expand_velocity, dense_weight=dense_weight, dense_velocity=dense_velocity, modulate_weight=modulate_weight, modulate_velocity=modulate_velocity, condition_weight=condition_weight, condition_velocity=condition_velocity, encoder_table=encoder_table, encoder_first=encoder_first, encoder_second=encoder_second, head_table=head_table, head_first=head_first, head_second=head_second)


@jax.custom_vjp
def low(v):
    return lax.optimization_barrier(v.astype(jnp.bfloat16)).astype(jnp.float32)

@jax.custom_vjp
def low_back(v):
    return v

def low_keep(v):
    return (low(v), None)

def low_pass(kept, grad):
    return (grad,)

def back_keep(v):
    return (v, None)

def back_low(kept, grad):
    return (low(grad),)
low.defvjp(low_keep, low_pass)
low_back.defvjp(back_keep, back_low)
precise_mode = lax.Precision.HIGHEST
norm_floor = 1e-06
score_factor = 0.125
newton_first = 3.4445
newton_second = -4.775
newton_third = 2.0315
muon_rate = 1.0
muon_decay = 0.01
muon_keep = 0.95
clip_bound = 0.001
adam_rate = 0.02
beta_first = 0.9
beta_second = 0.95
adam_floor = 1e-08
adam_decay = 0.1

def matmul(left_side, right_side):
    return jnp.dot(left_side, right_side, precision=precise_mode)

def layer_norm(values, gain_row, bias_row):
    centered = values - lax.optimization_barrier(jnp.mean(values, axis=-1, keepdims=True))
    spread = lax.optimization_barrier(jnp.mean(centered * centered, axis=-1, keepdims=True))
    return centered * lax.rsqrt(spread + norm_floor) * gain_row + bias_row

def plain_norm(values):
    centered = values - lax.optimization_barrier(jnp.mean(values, axis=-1, keepdims=True))
    spread = lax.optimization_barrier(jnp.mean(centered * centered, axis=-1, keepdims=True))
    return centered * lax.rsqrt(spread + norm_floor)

def alpha_bar(step_float):
    return jnp.cos(0.5 * math.pi * (step_float + 0.5) / TSTEPS) ** 2

def time_features(step_float):
    halfway = FREQ // 2
    frequency = jnp.exp(-math.log(10000.0) * jnp.arange(halfway).astype(step_float.dtype) / halfway)
    angles = step_float[:, None] * frequency[None, :]
    return jnp.concatenate([jnp.cos(angles), jnp.sin(angles)], axis=1)

def block(rows, attend, expand, gains, same_image):
    normed = low(layer_norm(rows, gains[0], gains[1]))
    query_rows = low(low_back(matmul(normed, attend[0]))).reshape(SEQ, HEADS, HD)
    key_rows = low(low_back(matmul(normed, attend[1]))).reshape(SEQ, HEADS, HD)
    values = low(low_back(matmul(normed, attend[2]))).reshape(SEQ, HEADS, HD)
    raw_scores = low_back(jnp.einsum('qhd,khd->hqk', query_rows, key_rows, precision=precise_mode))
    scores = jnp.where(same_image, raw_scores * score_factor, -1e+30)
    probabilities = low(jax.nn.softmax(scores, axis=-1))
    attended = low(low_back(jnp.einsum('hqk,khd->qhd', probabilities, values, precision=precise_mode))).reshape(SEQ, D)
    middle = rows + low_back(matmul(attended, attend[3]))
    normed = low(layer_norm(middle, gains[2], gains[3]))
    hidden = low(jax.nn.gelu(low_back(matmul(normed, expand[0].T))))
    return middle + low_back(matmul(hidden, expand[1]))

def sequence_loss(weights, patch_seq, noise_seq, image_rows, buffers, mask_rows, step_rows):
    attend, expand, dense_pair, modulate, condition, encoder_rows, head_rows = weights
    gain_rows = encoder_rows[:12]
    embedded = low_back(matmul(patch_seq, encoder_rows[12:12 + PATCH]))
    buffer_on = buffers[:, None] > 0
    masked_on = mask_rows[:, None] > 0
    entered = jnp.where(buffer_on, gain_rows[11], jnp.where(masked_on, gain_rows[10], embedded)) + encoder_rows[12 + PATCH:]
    same_image = (image_rows[:, None] == image_rows[None, :])[None]
    rows = entered
    for depth_index in range(2):
        rows = block(rows, attend[4 * depth_index:4 * depth_index + 4], expand[2 * depth_index:2 * depth_index + 2], gain_rows[4 * depth_index:4 * depth_index + 4], same_image)
    latent = low(layer_norm(rows, gain_rows[8], gain_rows[9]))
    condition_rows = low(low_back(matmul(latent, condition.T)))
    weight_row = (mask_rows * (1 - buffers)).astype(patch_seq.dtype)[:, None]
    loss_total = jnp.zeros((), patch_seq.dtype)
    for copy_index in range(COPIES):
        step_float = step_rows[copy_index].astype(patch_seq.dtype)
        alpha_row = alpha_bar(step_float)[:, None]
        target = noise_seq[copy_index]
        noisy = low(jnp.sqrt(alpha_row) * patch_seq + jnp.sqrt(1.0 - alpha_row) * target)
        lifted = low_back(matmul(noisy, head_rows[:PATCH]))
        time_rows = low_back(matmul(low(time_features(step_float)), head_rows[PATCH:PATCH + FREQ]))
        activated = low(jax.nn.silu(condition_rows + time_rows))
        modulation = low_back(matmul(activated, modulate.T))
        shift_one, scale_one, gate_one, shift_two, scale_two = jnp.split(modulation, 5, axis=1)
        inner_rows = low(plain_norm(lifted) * (1.0 + scale_one) + shift_one)
        inner_rows = low(jax.nn.gelu(low_back(matmul(inner_rows, dense_pair[0]))))
        lifted = lifted + gate_one * low_back(matmul(inner_rows, dense_pair[1]))
        outer_rows = low(plain_norm(lifted) * (1.0 + scale_two) + shift_two)
        predicted = low_back(matmul(outer_rows, head_rows[PATCH + FREQ:].T))
        loss_total = loss_total + jnp.sum(weight_row * (predicted - target) ** 2) / PATCH
    return loss_total

def orthogonalize(moment):
    current = moment / (jnp.sqrt(jnp.sum(moment * moment)) + 1e-07)
    for sweep_index in range(NS_STEPS):
        gram_matrix = matmul(current.T, current)
        polynomial = newton_second * gram_matrix + newton_third * matmul(gram_matrix, gram_matrix)
        current = newton_first * current + matmul(current, polynomial)
    return current

def muon_update(master, velocity, gradient):
    moment = muon_keep * velocity + gradient
    stacked = moment.reshape((-1,) + moment.shape[-2:])
    ortho_rows = lax.map(orthogonalize, stacked).reshape(moment.shape)
    ratio = max(1.0, moment.shape[-2] / moment.shape[-1]) ** 0.5
    return (master * (1.0 - muon_rate * muon_decay) - muon_rate * ratio * ortho_rows, moment)

def adam_update(master, first, second, gradient):
    first_new = beta_first * first + (1.0 - beta_first) * gradient
    second_new = beta_second * second + (1.0 - beta_second) * gradient * gradient
    corrected_first = first_new / (1.0 - beta_first ** STEP)
    corrected_second = second_new / (1.0 - beta_second ** STEP)
    master_new = master - adam_rate * (corrected_first / (jnp.sqrt(corrected_second) + adam_floor) + adam_decay * master)
    return (master_new, first_new, second_new)

def reference(patches, noise_copies, image_ids, buffer_flags, loss_mask, timesteps, attend_weight, attend_velocity, expand_weight, expand_velocity, dense_weight, dense_velocity, modulate_weight, modulate_velocity, condition_weight, condition_velocity, encoder_table, encoder_first, encoder_second, head_table, head_first, head_second):
    masters = (attend_weight, expand_weight, dense_weight, modulate_weight, condition_weight, encoder_table, head_table)
    patch_data = patches.astype(jnp.float32)
    token_count = COPIES * jnp.sum((loss_mask * (1 - buffer_flags)).astype(patch_data.dtype))
    noise_data = jnp.transpose(noise_copies.astype(jnp.float32), (1, 0, 2, 3))
    step_data = jnp.transpose(timesteps, (1, 0, 2))
    checked = jax.checkpoint(sequence_loss)

    def whole_loss(params):
        rounded = tuple((low(member) for member in params))

        def one_sequence(running, inputs):
            return (running + checked(rounded, *inputs), None)
        loss_total, unused = lax.scan(one_sequence, jnp.zeros((), patch_data.dtype), (patch_data, noise_data, image_ids, buffer_flags, loss_mask, step_data))
        return (loss_total / token_count, loss_total)
    unused_loss, pullback, loss_total = jax.vjp(whole_loss, masters, has_aux=True)
    gradients, = pullback(jnp.ones((), patch_data.dtype))
    squares = sum((jnp.sum(member * member) for member in gradients))
    clip_norm = jnp.sqrt(squares)
    factor = jnp.minimum(1.0, clip_bound / (clip_norm + 1e-06))
    clipped = tuple((member * factor for member in gradients))
    attend_master, attend_momentum = muon_update(attend_weight, attend_velocity, clipped[0])
    expand_master, expand_momentum = muon_update(expand_weight, expand_velocity, clipped[1])
    dense_master, dense_momentum = muon_update(dense_weight, dense_velocity, clipped[2])
    modulate_master, modulate_momentum = muon_update(modulate_weight, modulate_velocity, clipped[3])
    condition_master, condition_momentum = muon_update(condition_weight, condition_velocity, clipped[4])
    encoder_master, encoder_firsts, encoder_seconds = adam_update(encoder_table, encoder_first, encoder_second, clipped[5])
    table_master, table_firsts, table_seconds = adam_update(head_table, head_first, head_second, clipped[6])
    return (loss_total, token_count, clip_norm, attend_master, attend_momentum, expand_master, expand_momentum, dense_master, dense_momentum, modulate_master, modulate_momentum, condition_master, condition_momentum, encoder_master, encoder_firsts, encoder_seconds, table_master, table_firsts, table_seconds)
```

```python
import math

import jax
import jax.numpy as jnp
from jax import lax
from jax.sharding import PartitionSpec as P

D = 768
HEADS = 12
HD = 64
HW = 1024
PATCH = 64
FREQ = 256
SEQ = 1024
NS_STEPS = 2
STEP = 10
TSTEPS = 1000


precise_mode = lax.Precision.HIGHEST
norm_floor = 1e-06
score_factor = 0.125
newton_first = 3.4445
newton_second = -4.775
newton_third = 2.0315
muon_rate = 1.0
muon_decay = 0.01
muon_keep = 0.95
clip_bound = 0.001
adam_rate = 0.02
beta_first = 0.9
beta_second = 0.95
adam_floor = 1e-08
adam_decay = 0.1


def product(left_side, right_side):
    return jnp.dot(left_side, right_side, preferred_element_type=jnp.float32)


def product_left(left_side, right_side):
    return lax.dot_general(
        left_side, right_side, (((0,), (0,)), ((), ())), preferred_element_type=jnp.float32
    )


def product_right(left_side, right_side):
    return lax.dot_general(
        left_side, right_side, (((1,), (1,)), ((), ())), preferred_element_type=jnp.float32
    )


def to_low(values):
    return values.astype(jnp.bfloat16)


def layer_norm(values, gain_row, bias_row):
    centered = values - jnp.mean(values, axis=-1, keepdims=True)
    spread = jnp.mean(centered * centered, axis=-1, keepdims=True)
    return centered * lax.rsqrt(spread + norm_floor) * gain_row + bias_row


def plain_norm(values):
    centered = values - jnp.mean(values, axis=-1, keepdims=True)
    spread = jnp.mean(centered * centered, axis=-1, keepdims=True)
    return centered * lax.rsqrt(spread + norm_floor)


def alpha_bar(step_float):
    return jnp.cos(0.5 * math.pi * (step_float + 0.5) / TSTEPS) ** 2


def time_features(step_float):
    halfway = FREQ // 2
    frequency = jnp.exp(-math.log(10000.0) * jnp.arange(halfway).astype(jnp.float32) / halfway)
    angles = step_float[:, None] * frequency[None, :]
    return jnp.concatenate([jnp.cos(angles), jnp.sin(angles)], axis=1)


def first_modulate(lifted, modulation):
    return plain_norm(lifted) * (1.0 + modulation[:, HW : 2 * HW]) + modulation[:, :HW]


def last_modulate(lifted, modulation, branch):
    joined = lifted + modulation[:, 2 * HW : 3 * HW] * branch
    return plain_norm(joined) * (1.0 + modulation[:, 4 * HW :]) + modulation[:, 3 * HW : 4 * HW]


def grid_of(count):
    side = 1
    while 2 * side**3 < count:
        side *= 2
    if 2 * side**3 == count:
        return (2 * side, side, side)
    return (count, 1, 1)


def place_of(index, grid):
    return (index // (grid[1] * grid[2]), index // grid[2] % grid[1], index % grid[2])


def index_of(place, grid):
    return (place[0] * grid[1] + place[1]) * grid[2] + place[2]


def shift_pairs(grid, axis, shift):
    pairs = []
    for source in range(grid[0] * grid[1] * grid[2]):
        place = list(place_of(source, grid))
        place[axis] = (place[axis] + shift) % grid[axis]
        pairs.append((source, index_of(place, grid)))
    return pairs


def swap_core(values):
    return lax.ppermute(values, "copy", [(0, 1), (1, 0)])


def sum_all(values):
    values = values + swap_core(values)
    count = lax.axis_size("dp")
    if count & (count - 1):
        return lax.psum(values, "dp")
    step = 1
    while step < count:
        values = values + lax.ppermute(values, "dp", [(i, i ^ step) for i in range(count)])
        step *= 2
    return values


def scatter_axis(values, grid, axis, position, sent_type):
    size = grid[axis]
    mine = place_of(lax.axis_index("dp"), grid)[axis]
    total = lax.dynamic_index_in_dim(values, mine, position, keepdims=False)
    for shift in range(1, size):
        sent = lax.dynamic_index_in_dim(
            values, (mine + shift) % size, position, keepdims=False
        ).astype(sent_type)
        arrived = lax.ppermute(sent, "dp", shift_pairs(grid, axis, shift))
        total = total + arrived.astype(jnp.float32)
    return total


def scatter_rows(values, order):
    grid = grid_of(lax.axis_size("dp"))
    rows, columns = values.shape
    values = values.reshape(*grid, rows // lax.axis_size("dp"), columns)
    left = [0, 1, 2]
    for axis in order:
        sent_type = jnp.float32 if axis == order[-1] else jnp.bfloat16
        values = scatter_axis(values, grid, axis, left.index(axis), sent_type)
        left.remove(axis)
    return values


def share_columns(values):
    core = lax.axis_index("copy")
    rows = values.shape[0] // 2
    mine = lax.dynamic_slice_in_dim(values, core * rows, rows, 0)
    arrived = swap_core(lax.dynamic_slice_in_dim(values, (1 - core) * rows, rows, 0))
    first = jnp.where(core == 0, mine, arrived)
    last = jnp.where(core == 0, arrived, mine)
    return (first, last)


def columns_of(values, core):
    half = values.shape[1] // 2
    return lax.dynamic_slice_in_dim(values, core * half, half, 1)


def weight_grad(left_side, right_side):
    core = lax.axis_index("copy")
    arrived = swap_core(product_left(left_side, columns_of(right_side, 1 - core)))
    return product_left(left_side, columns_of(right_side, core)) + arrived


forward_order = (2, 1, 0)
crossed_order = (1, 2, 0)


def rows_whole(values, order):
    return jnp.concatenate(share_columns(scatter_rows(values, order)), axis=1)


def attention_scores(query_heads, key_heads, same_image):
    raw_scores = jnp.einsum(
        "qhd,khd->hqk", query_heads, key_heads, preferred_element_type=jnp.float32
    )
    return jnp.where(same_image[None], raw_scores * score_factor, -1e30)


def block_forward(entered, attend_low, expand_low, gain_rows, same_image):
    halfway = entered.shape[0]
    normed, first_back = jax.vjp(layer_norm, entered, gain_rows[0], gain_rows[1])
    normed_low = to_low(normed)
    key_low = to_low(product(normed_low, attend_low[1]))
    value_low = to_low(product(normed_low, attend_low[2]))
    key_all = jnp.concatenate([key_low, swap_core(key_low)], axis=0)
    value_all = jnp.concatenate([value_low, swap_core(value_low)], axis=0)
    query_low = to_low(product(normed_low, attend_low[0]))
    query_heads = query_low.reshape(halfway, HEADS, HD)
    key_heads = key_all.reshape(SEQ, HEADS, HD)
    value_heads = value_all.reshape(SEQ, HEADS, HD)
    scores = attention_scores(query_heads, key_heads, same_image)
    highest = jnp.max(scores, axis=-1, keepdims=True)
    exponent_rows = jnp.exp(scores - highest)
    row_total = jnp.sum(exponent_rows, axis=-1, keepdims=True)
    log_total = highest + jnp.log(row_total)
    attended = to_low(
        jnp.einsum(
            "hqk,khd->qhd",
            to_low(exponent_rows / row_total),
            value_heads,
            preferred_element_type=jnp.float32,
        ).reshape(halfway, D)
    )
    middle = entered + product(attended, attend_low[3])
    normed_two, second_back = jax.vjp(layer_norm, middle, gain_rows[2], gain_rows[3])
    normed_two_low = to_low(normed_two)
    hidden, gelu_back = jax.vjp(jax.nn.gelu, product_right(normed_two_low, expand_low[0]))
    hidden_low = to_low(hidden)
    output_rows = middle + product(hidden_low, expand_low[1])
    kept = (
        first_back,
        normed_low,
        query_heads,
        key_heads,
        value_heads,
        log_total,
        attended,
        second_back,
        normed_two_low,
        gelu_back,
        hidden_low,
    )
    return (output_rows, kept)


def block_backward(output_grad, kept, attend_low, expand_low, same_image):
    (
        first_back,
        normed_low,
        query_heads,
        key_heads,
        value_heads,
        log_total,
        attended,
        second_back,
        normed_two_low,
        gelu_back,
        hidden_low,
    ) = kept
    halfway = attended.shape[0]
    upper_low = to_low(output_grad)
    upper_delta = rows_whole(weight_grad(hidden_low, upper_low), forward_order)
    (hidden_grad,) = gelu_back(product_right(upper_low, expand_low[1]))
    hidden_grad_low = to_low(hidden_grad)
    lower_delta = rows_whole(weight_grad(hidden_grad_low, normed_two_low), crossed_order)
    middle_extra, gain_three, gain_four = second_back(product(hidden_grad_low, expand_low[0]))
    middle_grad = output_grad + middle_extra
    projected_low = to_low(middle_grad)
    output_delta = rows_whole(weight_grad(attended, projected_low), forward_order)
    attended_grad = to_low(product_right(projected_low, attend_low[3])).reshape(halfway, HEADS, HD)
    probability = jnp.exp(attention_scores(query_heads, key_heads, same_image) - log_total)
    soft_grad = jnp.einsum(
        "qhd,khd->hqk", attended_grad, value_heads, preferred_element_type=jnp.float32
    )
    value_part = jnp.einsum(
        "hqk,qhd->khd", to_low(probability), attended_grad, preferred_element_type=jnp.float32
    )
    score_low = to_low(
        probability
        * (soft_grad - jnp.sum(probability * soft_grad, axis=-1, keepdims=True))
        * score_factor
    )
    key_part = jnp.einsum(
        "hqk,qhd->khd", score_low, query_heads, preferred_element_type=jnp.float32
    )
    query_grad = to_low(
        jnp.einsum(
            "hqk,khd->qhd", score_low, key_heads, preferred_element_type=jnp.float32
        ).reshape(halfway, D)
    )
    key_part = key_part.reshape(SEQ, D)
    value_part = value_part.reshape(SEQ, D)
    value_grad = to_low(
        value_part[:halfway] + swap_core(to_low(value_part[halfway:])).astype(jnp.float32)
    )
    key_grad = to_low(
        key_part[:halfway] + swap_core(to_low(key_part[halfway:])).astype(jnp.float32)
    )
    normed_grad = (
        product_right(query_grad, attend_low[0])
        + product_right(key_grad, attend_low[1])
        + product_right(value_grad, attend_low[2])
    )
    entered_extra, gain_one, gain_two = first_back(normed_grad)
    attend_delta = jnp.stack(
        [
            rows_whole(weight_grad(normed_low, query_grad), forward_order),
            rows_whole(weight_grad(normed_low, key_grad), crossed_order),
            rows_whole(weight_grad(normed_low, value_grad), crossed_order),
            output_delta,
        ]
    )
    expand_delta = jnp.stack([lower_delta, upper_delta])
    gain_delta = jnp.stack([gain_one, gain_two, gain_three, gain_four])
    return (middle_grad + entered_extra, attend_delta, expand_delta, gain_delta)


def fine(left_side, right_side):
    return jnp.dot(
        left_side, right_side, precision=lax.Precision.HIGH, preferred_element_type=jnp.float32
    )


def newton_extra(gram_matrix):
    first_tail = newton_second * gram_matrix + newton_third * fine(gram_matrix, gram_matrix)
    once = newton_first * gram_matrix + fine(gram_matrix, first_tail)
    later = newton_first * once + fine(once, first_tail)
    last_tail = newton_second * later + newton_third * fine(later, later)
    return newton_first * (first_tail + last_tail) + fine(first_tail, last_tail)


def slots_of(devices):
    slots = [(14, 0, 2), (14, 1, 2)]
    for matrix in range(8, 12):
        slots += [(matrix, 0, 2), (matrix, 1, 2)]
    slots += [(matrix, 0, 1) for matrix in list(range(8)) + [12, 13, 15]]
    return slots + [None] * (devices - len(slots))


def padded(piece, rows, columns):
    return jnp.pad(piece, ((0, rows - piece.shape[0]), (0, columns - piece.shape[1])))


def muon_steps(moments):
    devices = lax.axis_size(("dp", "copy"))
    pieces = (
        [moments[0][i] for i in range(8)]
        + [moments[1][i] for i in range(4)]
        + [moments[2][i] for i in range(2)]
        + [moments[3], moments[4]]
    )
    slots = slots_of(devices)
    highest = max(pieces[slot[0]].shape[0] // slot[2] for slot in slots if slot)
    widest = max(piece.shape[1] for piece in pieces)
    sending = []
    for slot in slots:
        if slot is None:
            sending.append(jnp.zeros((highest, widest), jnp.bfloat16))
        else:
            rows = pieces[slot[0]].shape[0] // slot[2]
            piece = to_low(pieces[slot[0]][slot[1] * rows : (slot[1] + 1) * rows])
            sending.append(padded(piece, highest, widest))
    held = lax.all_to_all(jnp.stack(sending), ("dp", "copy"), 0, 0).reshape(
        devices * highest, widest
    )
    squares = sum_all(jnp.stack([jnp.sum(piece * piece) for piece in pieces]))
    inverse = 1.0 / (jnp.sqrt(squares) + 1e-07)
    me = lax.axis_index(("dp", "copy"))
    matrix_here = jnp.asarray([slot[0] if slot else 0 for slot in slots], jnp.int32)[me]
    shared_here = jnp.asarray([1.0 if slot and slot[2] == 2 else 0.0 for slot in slots])[me]
    scale_here = inverse[matrix_here]
    gram_matrix = product_left(held, held)
    gram_matrix = gram_matrix + shared_here * swap_core(gram_matrix)
    extra = newton_extra(gram_matrix * (scale_here * scale_here))
    result = to_low(product(held, to_low(extra)) * scale_here)
    back = lax.all_to_all(result.reshape(devices, highest, widest), ("dp", "copy"), 0, 0)
    found = []
    for matrix, piece in enumerate(pieces):
        parts = [
            back[device, : piece.shape[0] // slot[2], : piece.shape[1]]
            for device, slot in enumerate(slots)
            if slot and slot[0] == matrix
        ]
        whole = jnp.concatenate(parts, axis=0) if len(parts) > 1 else parts[0]
        found.append(
            newton_first * newton_first * inverse[matrix] * piece + whole.astype(jnp.float32)
        )
    return (
        jnp.stack(found[:8]),
        jnp.stack(found[8:12]),
        jnp.stack(found[12:14]),
        found[14],
        found[15],
    )


def adam_shard(master, first, second, gradient):
    first_new = beta_first * first + (1.0 - beta_first) * gradient
    second_new = beta_second * second + (1.0 - beta_second) * gradient * gradient
    corrected_first = first_new / (1.0 - beta_first**STEP)
    corrected_second = second_new / (1.0 - beta_second**STEP)
    master_new = master - adam_rate * (
        corrected_first / (jnp.sqrt(corrected_second) + adam_floor) + adam_decay * master
    )
    return (master_new, first_new, second_new)


def per_device(
    patches,
    noise_copies,
    image_ids,
    buffer_flags,
    loss_mask,
    timesteps,
    attend_weight,
    attend_velocity,
    expand_weight,
    expand_velocity,
    dense_weight,
    dense_velocity,
    modulate_weight,
    modulate_velocity,
    condition_weight,
    condition_velocity,
    encoder_table,
    encoder_first,
    encoder_second,
    head_table,
    head_first,
    head_second,
):
    everywhere = ("dp", "copy")
    core = lax.axis_index("copy")
    encoder_turned = lax.all_gather(to_low(encoder_table).T, everywhere, axis=0, tiled=True)
    attend_low, expand_low = (to_low(attend_weight), to_low(expand_weight))
    attend_all, expand_all = ([], [])
    for depth_index in range(2):
        attend_all.append(
            lax.all_gather(
                attend_low[4 * depth_index : 4 * depth_index + 4], everywhere, axis=1, tiled=True
            )
        )
        expand_all.append(
            lax.all_gather(
                expand_low[2 * depth_index : 2 * depth_index + 2], everywhere, axis=1, tiled=True
            )
        )
    condition_all = lax.all_gather(to_low(condition_weight), everywhere, axis=0, tiled=True)
    head_turned = lax.all_gather(to_low(head_table).T, everywhere, axis=0, tiled=True)
    modulate_all = lax.all_gather(to_low(modulate_weight), everywhere, axis=0, tiled=True)
    dense_all = lax.all_gather(to_low(dense_weight), everywhere, axis=1, tiled=True)
    encoder_all = encoder_turned.T
    head_all = head_turned.T
    halfway = SEQ // 2
    offset = core * halfway

    def own_first(values):
        return jnp.where(
            core == 0, values, jnp.concatenate([values[halfway:], values[:halfway]], axis=0)
        )

    patch_seq = own_first(patches[0])
    image_row = own_first(image_ids[0])
    buffer_row = own_first(buffer_flags[0])
    masked_row = own_first(loss_mask[0])
    weight_row = (masked_row * (1 - buffer_row)).astype(jnp.float32)
    token_count = sum_all(jnp.sum(weight_row))
    own_patch = patch_seq[:halfway]
    buffer_on = buffer_row[:halfway, None] > 0
    masked_on = masked_row[:halfway, None] > 0
    same_image = image_row[:halfway, None] == image_row[None, :]
    gain_rows = encoder_all[:12].astype(jnp.float32)
    position = lax.dynamic_slice_in_dim(encoder_all, 12 + PATCH + offset, halfway, 0).astype(
        jnp.float32
    )
    embedded = product(own_patch, encoder_all[12 : 12 + PATCH])

    def entry(embedded_rows, token_pair, position_rows):
        return (
            jnp.where(buffer_on, token_pair[1], jnp.where(masked_on, token_pair[0], embedded_rows))
            + position_rows
        )

    entered, entry_back = jax.vjp(entry, embedded, gain_rows[10:12], position)
    state_rows = entered
    kept_all = []
    for depth_index in range(2):
        state_rows, kept = block_forward(
            state_rows,
            attend_all[depth_index],
            expand_all[depth_index],
            gain_rows[4 * depth_index : 4 * depth_index + 4],
            same_image,
        )
        kept_all.append(kept)
    latent, third_back = jax.vjp(layer_norm, state_rows, gain_rows[8], gain_rows[9])
    latent_low = to_low(latent)
    condition_own = to_low(product_right(latent_low, condition_all))
    condition_rows = jnp.concatenate([condition_own, swap_core(condition_own)], axis=0)
    step_float = own_first(timesteps[0, 0]).astype(jnp.float32)
    alpha_row = alpha_bar(step_float)[:, None]
    target = own_first(noise_copies[0, 0]).astype(jnp.float32)
    noisy_low = to_low(
        jnp.sqrt(alpha_row) * patch_seq.astype(jnp.float32) + jnp.sqrt(1.0 - alpha_row) * target
    )
    lifted = product(noisy_low, head_all[:PATCH])
    feature_low = to_low(time_features(step_float))
    summed = condition_rows.astype(jnp.float32) + product(
        feature_low, head_all[PATCH : PATCH + FREQ]
    )
    activated, silu_back = jax.vjp(jax.nn.silu, summed)
    activated_low = to_low(activated)
    modulation = product_right(activated_low, modulate_all)
    inner_rows, inner_back = jax.vjp(first_modulate, lifted, modulation)
    inner_low = to_low(inner_rows)
    expanded, dense_back = jax.vjp(jax.nn.gelu, product(inner_low, dense_all[0]))
    expanded_low = to_low(expanded)
    branch = product(expanded_low, dense_all[1])
    outer_rows, outer_back = jax.vjp(last_modulate, lifted, modulation, branch)
    outer_low = to_low(outer_rows)
    predicted = product_right(outer_low, head_all[PATCH + FREQ :])
    residue = predicted - target
    loss_local = jnp.sum(weight_row[:, None] * residue * residue) / PATCH
    predicted_grad = to_low(2.0 * weight_row[:, None] * residue / (PATCH * token_count))
    final_turned = product_left(outer_low, predicted_grad)
    lifted_grad, modulation_grad, branch_grad = outer_back(
        product(predicted_grad, head_all[PATCH + FREQ :])
    )
    branch_low = to_low(branch_grad)
    second_delta = rows_whole(weight_grad(expanded_low, branch_low), forward_order)
    (expanded_grad,) = dense_back(product_right(branch_low, dense_all[1]))
    expanded_grad_low = to_low(expanded_grad)
    first_delta = rows_whole(weight_grad(inner_low, expanded_grad_low), crossed_order)
    lifted_extra, modulation_extra = inner_back(product_right(expanded_grad_low, dense_all[0]))
    modulation_low = to_low(modulation_grad + modulation_extra)
    modulate_half = weight_grad(modulation_low, activated_low)
    quarter = modulate_half.shape[1] // 2
    modulate_left = share_columns(scatter_rows(modulate_half[:, :quarter], forward_order))
    modulate_right = share_columns(scatter_rows(modulate_half[:, quarter:], crossed_order))
    modulate_delta = jnp.concatenate(
        [modulate_left[0], modulate_right[0], modulate_left[1], modulate_right[1]], axis=1
    )
    (summed_grad,) = silu_back(product(modulation_low, modulate_all))
    time_turned = product_left(to_low(summed_grad), feature_low)
    lift_turned = product_left(to_low(lifted_grad + lifted_extra), noisy_low)
    head_turned_grad = jnp.concatenate([lift_turned, time_turned, final_turned], axis=1)
    head_delta = rows_whole(
        columns_of(head_turned_grad, core) + swap_core(columns_of(head_turned_grad, 1 - core)),
        forward_order,
    ).T
    condition_grad = to_low(
        summed_grad[:halfway] + swap_core(to_low(summed_grad[halfway:])).astype(jnp.float32)
    )
    condition_delta = rows_whole(weight_grad(condition_grad, latent_low), crossed_order)
    state_grad, gain_nine, gain_ten = third_back(product(condition_grad, condition_all))
    attend_parts = [None, None]
    expand_parts = [None, None]
    gain_parts = [None, None]
    for depth_index in (1, 0):
        (
            state_grad,
            attend_parts[depth_index],
            expand_parts[depth_index],
            gain_parts[depth_index],
        ) = block_backward(
            state_grad,
            kept_all[depth_index],
            attend_all[depth_index],
            expand_all[depth_index],
            same_image,
        )
    embedded_grad, token_grad, position_grad = entry_back(state_grad)
    embed_delta = product_left(own_patch, to_low(embedded_grad))
    small_delta = jnp.concatenate(
        [
            gain_parts[0],
            gain_parts[1],
            jnp.stack([gain_nine, gain_ten]),
            token_grad,
            embed_delta,
        ],
        axis=0,
    )
    small_delta = small_delta + swap_core(small_delta)
    small_half = small_delta.shape[0] // 2
    encoder_half = jnp.concatenate(
        [position_grad, lax.dynamic_slice_in_dim(small_delta, core * small_half, small_half, 0)],
        axis=0,
    ).T
    encoder_first_half, encoder_last_half = share_columns(
        scatter_rows(encoder_half, crossed_order)
    )
    encoder_delta = jnp.concatenate(
        [
            encoder_first_half[:, halfway:],
            encoder_last_half[:, halfway:],
            encoder_first_half[:, :halfway],
            encoder_last_half[:, :halfway],
        ],
        axis=1,
    ).T
    reduced = (
        jnp.concatenate(attend_parts, axis=0),
        jnp.concatenate(expand_parts, axis=0),
        jnp.stack([first_delta, second_delta]),
        modulate_delta,
        condition_delta,
        encoder_delta,
        head_delta,
    )
    squares = sum((jnp.sum(member * member) for member in reduced))
    totals = sum_all(jnp.stack([squares, loss_local]))
    square_total, loss_sum = (totals[0], totals[1])
    clip_norm = jnp.sqrt(square_total)
    factor = jnp.minimum(1.0, clip_bound / (clip_norm + 1e-06))
    velocities = (
        attend_velocity,
        expand_velocity,
        dense_velocity,
        modulate_velocity,
        condition_velocity,
    )
    moments = tuple((muon_keep * velocities[i] + factor * reduced[i] for i in range(5)))
    current = muon_steps(moments)
    devices = lax.axis_size(everywhere)
    masters = (attend_weight, expand_weight, dense_weight, modulate_weight, condition_weight)
    updated = tuple(
        (
            masters[i] * (1.0 - muon_rate * muon_decay)
            - muon_rate
            * max(1.0, current[i].shape[-2] * devices / current[i].shape[-1]) ** 0.5
            * current[i]
            for i in range(5)
        )
    )
    encoder_master, encoder_firsts, encoder_seconds = adam_shard(
        encoder_table, encoder_first, encoder_second, factor * reduced[5]
    )
    table_master, table_firsts, table_seconds = adam_shard(
        head_table, head_first, head_second, factor * reduced[6]
    )
    return (
        loss_sum,
        token_count,
        clip_norm,
        updated[0],
        moments[0],
        updated[1],
        moments[1],
        updated[2],
        moments[2],
        updated[3],
        moments[3],
        updated[4],
        moments[4],
        encoder_master,
        encoder_firsts,
        encoder_seconds,
        table_master,
        table_firsts,
        table_seconds,
    )


def solution(mesh):
    placed = (
        P("dp", None, None),
        P("copy", "dp", None, None),
        P("dp", None),
        P("dp", None),
        P("dp", None),
        P("copy", "dp", None),
        P(None, ("dp", "copy"), None),
        P(None, ("dp", "copy"), None),
        P(None, ("dp", "copy"), None),
        P(None, ("dp", "copy"), None),
        P(None, ("dp", "copy"), None),
        P(None, ("dp", "copy"), None),
        P(("dp", "copy"), None),
        P(("dp", "copy"), None),
        P(("dp", "copy"), None),
        P(("dp", "copy"), None),
        P(None, ("dp", "copy")),
        P(None, ("dp", "copy")),
        P(None, ("dp", "copy")),
        P(None, ("dp", "copy")),
        P(None, ("dp", "copy")),
        P(None, ("dp", "copy")),
    )
    return jax.shard_map(
        per_device,
        mesh=mesh,
        in_specs=placed,
        out_specs=(
            P(),
            P(),
            P(),
            P(None, ("dp", "copy"), None),
            P(None, ("dp", "copy"), None),
            P(None, ("dp", "copy"), None),
            P(None, ("dp", "copy"), None),
            P(None, ("dp", "copy"), None),
            P(None, ("dp", "copy"), None),
            P(("dp", "copy"), None),
            P(("dp", "copy"), None),
            P(("dp", "copy"), None),
            P(("dp", "copy"), None),
            P(None, ("dp", "copy")),
            P(None, ("dp", "copy")),
            P(None, ("dp", "copy")),
            P(None, ("dp", "copy")),
            P(None, ("dp", "copy")),
            P(None, ("dp", "copy")),
        ),
        check_vma=False,
    )
```

```python
import math

import jax
import jax.numpy as jnp
from jax import lax
from jax.experimental import pallas as pl
from jax.experimental.pallas import tpu as pltpu
from jax.sharding import PartitionSpec as P

D = 768
HEADS = 12
HD = 64
HW = 1024
PATCH = 64
FREQ = 256
SEQ = 1024
NS_STEPS = 2
STEP = 10
TSTEPS = 1000


precise_mode = lax.Precision.HIGHEST
norm_floor = 1e-06
score_factor = 0.125
newton_first = 3.4445
newton_second = -4.775
newton_third = 2.0315
muon_rate = 1.0
muon_decay = 0.01
muon_keep = 0.95
clip_bound = 0.001
adam_rate = 0.02
beta_first = 0.9
beta_second = 0.95
adam_floor = 1e-08
adam_decay = 0.1


def product(left_side, right_side):
    return jnp.dot(left_side, right_side, preferred_element_type=jnp.float32)


def product_left(left_side, right_side):
    return lax.dot_general(
        left_side, right_side, (((0,), (0,)), ((), ())), preferred_element_type=jnp.float32
    )


def product_right(left_side, right_side):
    return lax.dot_general(
        left_side, right_side, (((1,), (1,)), ((), ())), preferred_element_type=jnp.float32
    )


def to_low(values):
    return values.astype(jnp.bfloat16)


def layer_norm(values, gain_row, bias_row):
    centered = values - jnp.mean(values, axis=-1, keepdims=True)
    spread = jnp.mean(centered * centered, axis=-1, keepdims=True)
    return centered * lax.rsqrt(spread + norm_floor) * gain_row + bias_row


def plain_norm(values):
    centered = values - jnp.mean(values, axis=-1, keepdims=True)
    spread = jnp.mean(centered * centered, axis=-1, keepdims=True)
    return centered * lax.rsqrt(spread + norm_floor)


def alpha_bar(step_float):
    return jnp.cos(0.5 * math.pi * (step_float + 0.5) / TSTEPS) ** 2


def time_features(step_float):
    halfway = FREQ // 2
    frequency = jnp.exp(-math.log(10000.0) * jnp.arange(halfway).astype(jnp.float32) / halfway)
    angles = step_float[:, None] * frequency[None, :]
    return jnp.concatenate([jnp.cos(angles), jnp.sin(angles)], axis=1)


def first_modulate(lifted, modulation):
    return plain_norm(lifted) * (1.0 + modulation[:, HW : 2 * HW]) + modulation[:, :HW]


def last_modulate(lifted, modulation, branch):
    joined = lifted + modulation[:, 2 * HW : 3 * HW] * branch
    return plain_norm(joined) * (1.0 + modulation[:, 4 * HW :]) + modulation[:, 3 * HW : 4 * HW]


def grid_of(count):
    side = 1
    while 2 * side**3 < count:
        side *= 2
    if 2 * side**3 == count:
        return (2 * side, side, side)
    return (count, 1, 1)


def place_of(index, grid):
    return (index // (grid[1] * grid[2]), index // grid[2] % grid[1], index % grid[2])


def index_of(place, grid):
    return (place[0] * grid[1] + place[1]) * grid[2] + place[2]


def shift_pairs(grid, axis, shift):
    pairs = []
    for source in range(grid[0] * grid[1] * grid[2]):
        place = list(place_of(source, grid))
        place[axis] = (place[axis] + shift) % grid[axis]
        pairs.append((source, index_of(place, grid)))
    return pairs


def swap_core(values):
    return lax.ppermute(values, "copy", [(0, 1), (1, 0)])


def sum_all(values):
    values = values + swap_core(values)
    count = lax.axis_size("dp")
    if count & (count - 1):
        return lax.psum(values, "dp")
    step = 1
    while step < count:
        values = values + lax.ppermute(values, "dp", [(i, i ^ step) for i in range(count)])
        step *= 2
    return values


def assemble(pieces, places, shape):
    indices = jnp.stack(
        [jnp.asarray(i, jnp.int32) for place in places for i in place if i is not None]
    )

    def kernel(index_ref, *refs):
        sources, target, semaphores = (refs[: len(pieces)], refs[-2], refs[-1])
        copies, number = ([], 0)
        for i, place in enumerate(places):
            view = []
            for wanted in place:
                if wanted is None:
                    view.append(slice(None))
                else:
                    view.append(index_ref[number])
                    number += 1
            copies.append(
                pltpu.make_async_copy(sources[i], target.at[tuple(view)], semaphores.at[i])
            )
            copies[-1].start()
        for copy in copies:
            copy.wait()

    size = 2 * math.prod(shape)
    return pl.pallas_call(
        kernel,
        out_shape=jax.ShapeDtypeStruct(shape, pieces[0].dtype),
        in_specs=[pl.BlockSpec(memory_space=pltpu.SMEM)]
        + [pl.BlockSpec(memory_space=pl.ANY)] * len(pieces),
        out_specs=pl.BlockSpec(memory_space=pl.ANY),
        scratch_shapes=[pltpu.SemaphoreType.DMA((len(pieces),))],
        cost_estimate=pl.CostEstimate(flops=0, bytes_accessed=2 * size, transcendentals=0),
    )(indices, *pieces)


class Flow:
    def __init__(self):
        self.live, self.results = ([], {})

    def begin(self, name, task):
        self.live.append([name, task, *next(task)])

    def tick(self, *carry):
        due = [entry for entry in self.live if entry[3] <= 1]
        for entry in self.live:
            entry[3] -= 1
        carry, arrived = lax.optimization_barrier((carry, [entry[2] for entry in due]))
        for entry, values in zip(due, arrived):
            try:
                entry[2], entry[3] = entry[1].send(values)
            except StopIteration as stop:
                self.results[entry[0]] = stop.value
                self.live.remove(entry)
        return carry if len(carry) > 1 else (carry[0] if carry else None)

    def take(self, *names):
        while any(name not in self.results for name in names):
            self.tick()
        return [self.results[name] for name in names]


forward_order = (2, 1, 0)
crossed_order = (1, 2, 0)


def gather_task(own, order):
    grid = grid_of(lax.axis_size("dp"))
    here = place_of(lax.axis_index("dp"), grid)
    core = lax.axis_index("copy")
    slots, rows, columns = own.shape
    values, found = (own, [])
    for axis in order[::-1][:-1]:
        size = grid[axis]
        arrived = yield (
            [lax.ppermute(values, "dp", shift_pairs(grid, axis, shift)) for shift in range(1, size)],
            1,
        )
        position = 1 + sum(1 for other in found if other < axis)
        shape = values.shape[:position] + (size,) + values.shape[position:]
        places = [
            (None,) * position + ((here[axis] - shift) % size,) for shift in range(size)
        ]
        values = assemble([values] + arrived, places, shape)
        found.append(axis)
    axis = order[0]
    size = grid[axis]
    arrived = yield (
        [swap_core(values)]
        + [lax.ppermute(values, "dp", shift_pairs(grid, axis, shift)) for shift in range(1, size)],
        1,
    )
    mine = [values] + arrived[1:]
    others = yield ([swap_core(piece) for piece in arrived[1:]], 1)
    others = [arrived[0]] + others
    position = 1 + sum(1 for other in found if other < axis)
    places = []
    for owner in (core, 1 - core):
        for shift in range(size):
            place = [None] * 4
            place[position] = (here[axis] - shift) % size
            places.append(tuple(place) + (owner,))
    whole = assemble(mine + others, places, (slots, *grid, 2, rows, columns))
    return whole.reshape(slots, 2 * math.prod(grid) * rows, columns)


def columns_of(values, core):
    half = values.shape[-1] // 2
    return lax.dynamic_slice_in_dim(values, core * half, half, values.ndim - 1)


def scatter_task(values, order):
    grid = grid_of(lax.axis_size("dp"))
    here = place_of(lax.axis_index("dp"), grid)
    core = lax.axis_index("copy")
    slots, rows, columns = values.shape
    values = values.reshape(slots, *grid, rows // math.prod(grid), columns)
    left = [0, 1, 2]
    for axis in order:
        position, size = (1 + left.index(axis), grid[axis])
        sent = [
            to_low(
                lax.dynamic_index_in_dim(
                    values, (here[axis] + shift) % size, position, keepdims=False
                )
            )
            for shift in range(1, size)
        ]
        arrived = yield (
            [
                lax.ppermute(sent[shift - 1], "dp", shift_pairs(grid, axis, shift))
                for shift in range(1, size)
            ],
            1,
        )
        total = lax.dynamic_index_in_dim(values, here[axis], position, keepdims=False)
        for part in arrived:
            total = total + part.astype(jnp.float32)
        values = total
        left.remove(axis)
    half = values.shape[1] // 2
    mine = lax.dynamic_slice_in_dim(values, core * half, half, 1)
    (arrived,) = yield (
        [swap_core(lax.dynamic_slice_in_dim(values, (1 - core) * half, half, 1))],
        1,
    )
    first = jnp.where(core == 0, mine, arrived)
    last = jnp.where(core == 0, arrived, mine)
    return (first, last)


def weight_task(left_side, right_side, order, slots=1):
    core = lax.axis_index("copy")
    (arrived,) = yield ([swap_core(product_left(left_side, columns_of(right_side, 1 - core)))], 1)
    total = product_left(left_side, columns_of(right_side, core)) + arrived
    total = total.reshape(slots, total.shape[0] // slots, total.shape[1])
    first, last = yield from scatter_task(total, order)
    return jnp.concatenate([first, last], axis=-1)


def split_weight_task(left_side, right_side, flow, names):
    core = lax.axis_index("copy")
    (arrived,) = yield ([swap_core(product_left(left_side, columns_of(right_side, 1 - core)))], 1)
    total = (product_left(left_side, columns_of(right_side, core)) + arrived)[None]
    quarter = total.shape[-1] // 2
    flow.begin(names[0], scatter_task(total[..., :quarter], forward_order))
    flow.begin(names[1], scatter_task(total[..., quarter:], crossed_order))
    return None


def shared_task(values, order):
    core = lax.axis_index("copy")
    (arrived,) = yield ([swap_core(columns_of(values, 1 - core))], 1)
    first, last = yield from scatter_task((columns_of(values, core) + arrived)[None], order)
    return jnp.concatenate([first, last], axis=-1)[0]


def attention_scores(query_heads, key_heads, same_image):
    raw_scores = jnp.einsum(
        "qhd,khd->hqk", query_heads, key_heads, preferred_element_type=jnp.float32
    )
    return jnp.where(same_image[None], raw_scores * score_factor, -1e30)


def block_forward(entered, attend_low, flow, depth, gain_rows, same_image):
    halfway = entered.shape[0]
    normed, first_back = jax.vjp(layer_norm, entered, gain_rows[0], gain_rows[1])
    normed_low = to_low(normed)
    key_low = to_low(product(normed_low, attend_low[1]))
    value_low = to_low(product(normed_low, attend_low[2]))
    key_all = jnp.concatenate([key_low, swap_core(key_low)], axis=0)
    value_all = jnp.concatenate([value_low, swap_core(value_low)], axis=0)
    query_low = to_low(product(normed_low, attend_low[0]))
    query_low, key_all, value_all = flow.tick(query_low, key_all, value_all)
    query_heads = query_low.reshape(halfway, HEADS, HD)
    key_heads = key_all.reshape(SEQ, HEADS, HD)
    value_heads = value_all.reshape(SEQ, HEADS, HD)
    scores = attention_scores(query_heads, key_heads, same_image)
    highest = jnp.max(scores, axis=-1, keepdims=True)
    exponent_rows = jnp.exp(scores - highest)
    row_total = jnp.sum(exponent_rows, axis=-1, keepdims=True)
    log_total = highest + jnp.log(row_total)
    attended = to_low(
        jnp.einsum(
            "hqk,khd->qhd",
            to_low(exponent_rows / row_total),
            value_heads,
            preferred_element_type=jnp.float32,
        ).reshape(halfway, D)
    )
    attended = flow.tick(attended)
    middle = entered + product(attended, attend_low[3])
    normed_two, second_back = jax.vjp(layer_norm, middle, gain_rows[2], gain_rows[3])
    normed_two_low = to_low(normed_two)
    first_expand, last_expand = flow.take("expand%d.0" % depth, "expand%d.1" % depth)
    expand_low = (first_expand.reshape(-1, D), last_expand.reshape(-1, D))
    hidden, gelu_back = jax.vjp(jax.nn.gelu, product_right(normed_two_low, expand_low[0]))
    hidden_low = flow.tick(to_low(hidden))
    output_rows = middle + product(hidden_low, expand_low[1])
    kept = (
        first_back,
        normed_low,
        query_heads,
        key_heads,
        value_heads,
        log_total,
        attended,
        second_back,
        normed_two_low,
        gelu_back,
        hidden_low,
        expand_low,
    )
    return (output_rows, kept)


def block_backward(output_grad, kept, attend_low, flow, depth, same_image):
    (
        first_back,
        normed_low,
        query_heads,
        key_heads,
        value_heads,
        log_total,
        attended,
        second_back,
        normed_two_low,
        gelu_back,
        hidden_low,
        expand_low,
    ) = kept
    halfway = attended.shape[0]
    copies = expand_low[0].shape[0] // D
    upper_low = to_low(output_grad)
    flow.begin("upper%d" % depth, weight_task(hidden_low, upper_low, forward_order, copies))
    (hidden_grad,) = gelu_back(product_right(upper_low, expand_low[1]))
    hidden_grad_low = flow.tick(to_low(hidden_grad))
    flow.begin("lower%d" % depth, weight_task(hidden_grad_low, normed_two_low, crossed_order, copies))
    middle_extra, gain_three, gain_four = second_back(product(hidden_grad_low, expand_low[0]))
    middle_grad = flow.tick(output_grad + middle_extra)
    projected_low = to_low(middle_grad)
    flow.begin("joined%d" % depth, weight_task(attended, projected_low, forward_order))
    attended_grad = to_low(product_right(projected_low, attend_low[3])).reshape(halfway, HEADS, HD)
    attended_grad = flow.tick(attended_grad)
    probability = jnp.exp(attention_scores(query_heads, key_heads, same_image) - log_total)
    soft_grad = jnp.einsum(
        "qhd,khd->hqk", attended_grad, value_heads, preferred_element_type=jnp.float32
    )
    value_part = jnp.einsum(
        "hqk,qhd->khd", to_low(probability), attended_grad, preferred_element_type=jnp.float32
    )
    score_low = to_low(
        probability
        * (soft_grad - jnp.sum(probability * soft_grad, axis=-1, keepdims=True))
        * score_factor
    )
    score_low, value_part = flow.tick(score_low, value_part)
    key_part = jnp.einsum(
        "hqk,qhd->khd", score_low, query_heads, preferred_element_type=jnp.float32
    )
    key_part = flow.tick(key_part)
    query_grad = to_low(
        jnp.einsum(
            "hqk,khd->qhd", score_low, key_heads, preferred_element_type=jnp.float32
        ).reshape(halfway, D)
    )
    key_part = key_part.reshape(SEQ, D)
    value_part = value_part.reshape(SEQ, D)
    value_grad = to_low(
        value_part[:halfway] + swap_core(to_low(value_part[halfway:])).astype(jnp.float32)
    )
    key_grad = to_low(
        key_part[:halfway] + swap_core(to_low(key_part[halfway:])).astype(jnp.float32)
    )
    query_grad, key_grad, value_grad = flow.tick(query_grad, key_grad, value_grad)
    flow.begin("value%d" % depth, weight_task(normed_low, value_grad, crossed_order))
    flow.begin("key%d" % depth, weight_task(normed_low, key_grad, crossed_order))
    flow.begin("query%d" % depth, weight_task(normed_low, query_grad, forward_order))
    normed_grad = (
        product_right(query_grad, attend_low[0])
        + product_right(key_grad, attend_low[1])
        + product_right(value_grad, attend_low[2])
    )
    entered_extra, gain_one, gain_two = first_back(normed_grad)
    gain_delta = jnp.stack([gain_one, gain_two, gain_three, gain_four])
    return (flow.tick(middle_grad + entered_extra), gain_delta)


def fine(left_side, right_side):
    return jnp.dot(
        left_side, right_side, precision=lax.Precision.HIGH, preferred_element_type=jnp.float32
    )


def newton_extra(gram_matrix):
    first_tail = newton_second * gram_matrix + newton_third * fine(gram_matrix, gram_matrix)
    once = newton_first * gram_matrix + fine(gram_matrix, first_tail)
    later = newton_first * once + fine(once, first_tail)
    last_tail = newton_second * later + newton_third * fine(later, later)
    return newton_first * (first_tail + last_tail) + fine(first_tail, last_tail)


def slots_of(devices):
    slots = [(14, 0, 2), (14, 1, 2)]
    for matrix in range(8, 12):
        slots += [(matrix, 0, 2), (matrix, 1, 2)]
    slots += [(matrix, 0, 1) for matrix in list(range(8)) + [12, 13, 15]]
    return slots + [None] * (devices - len(slots))


def padded(piece, rows, columns):
    return jnp.pad(piece, ((0, rows - piece.shape[0]), (0, columns - piece.shape[1])))


def muon_steps(moments):
    devices = lax.axis_size(("dp", "copy"))
    pieces = (
        [moments[0][i] for i in range(8)]
        + [moments[1][i] for i in range(4)]
        + [moments[2][i] for i in range(2)]
        + [moments[3], moments[4]]
    )
    slots = slots_of(devices)
    highest = max(pieces[slot[0]].shape[0] // slot[2] for slot in slots if slot)
    widest = max(piece.shape[1] for piece in pieces)
    sending = []
    for slot in slots:
        if slot is None:
            sending.append(jnp.zeros((highest, widest), jnp.bfloat16))
        else:
            rows = pieces[slot[0]].shape[0] // slot[2]
            piece = to_low(pieces[slot[0]][slot[1] * rows : (slot[1] + 1) * rows])
            sending.append(padded(piece, highest, widest))
    held = lax.all_to_all(jnp.stack(sending), ("dp", "copy"), 0, 0).reshape(
        devices * highest, widest
    )
    squares = sum_all(jnp.stack([jnp.sum(piece * piece) for piece in pieces]))
    inverse = 1.0 / (jnp.sqrt(squares) + 1e-07)
    me = lax.axis_index(("dp", "copy"))
    matrix_here = jnp.asarray([slot[0] if slot else 0 for slot in slots], jnp.int32)[me]
    shared_here = jnp.asarray([1.0 if slot and slot[2] == 2 else 0.0 for slot in slots])[me]
    scale_here = inverse[matrix_here]
    gram_matrix = product_left(held, held)
    gram_matrix = gram_matrix + shared_here * swap_core(gram_matrix)
    extra = newton_extra(gram_matrix * (scale_here * scale_here))
    result = to_low(product(held, to_low(extra)) * scale_here)
    back = lax.all_to_all(result.reshape(devices, highest, widest), ("dp", "copy"), 0, 0)
    found = []
    for matrix, piece in enumerate(pieces):
        parts = [
            back[device, : piece.shape[0] // slot[2], : piece.shape[1]]
            for device, slot in enumerate(slots)
            if slot and slot[0] == matrix
        ]
        whole = jnp.concatenate(parts, axis=0) if len(parts) > 1 else parts[0]
        found.append(
            newton_first * newton_first * inverse[matrix] * piece + whole.astype(jnp.float32)
        )
    return (
        jnp.stack(found[:8]),
        jnp.stack(found[8:12]),
        jnp.stack(found[12:14]),
        found[14],
        found[15],
    )


def adam_shard(master, first, second, gradient):
    first_new = beta_first * first + (1.0 - beta_first) * gradient
    second_new = beta_second * second + (1.0 - beta_second) * gradient * gradient
    corrected_first = first_new / (1.0 - beta_first**STEP)
    corrected_second = second_new / (1.0 - beta_second**STEP)
    master_new = master - adam_rate * (
        corrected_first / (jnp.sqrt(corrected_second) + adam_floor) + adam_decay * master
    )
    return (master_new, first_new, second_new)


def per_device(
    patches,
    noise_copies,
    image_ids,
    buffer_flags,
    loss_mask,
    timesteps,
    attend_weight,
    attend_velocity,
    expand_weight,
    expand_velocity,
    dense_weight,
    dense_velocity,
    modulate_weight,
    modulate_velocity,
    condition_weight,
    condition_velocity,
    encoder_table,
    encoder_first,
    encoder_second,
    head_table,
    head_first,
    head_second,
):
    everywhere = ("dp", "copy")
    core = lax.axis_index("copy")
    flow = Flow()
    attend_low, expand_low, dense_low = (
        to_low(attend_weight),
        to_low(expand_weight),
        to_low(dense_weight),
    )
    rows = attend_weight.shape[1]
    table_slots = -(-encoder_table.shape[0] // D)
    encoder_turned = padded(to_low(encoder_table).T, rows, table_slots * D)
    encoder_turned = encoder_turned.reshape(rows, table_slots, D).transpose(1, 0, 2)
    flow.begin(
        "table",
        gather_task(jnp.concatenate([encoder_turned, attend_low[0:1]], axis=0), forward_order),
    )
    flow.begin("attend0", gather_task(attend_low[1:4], crossed_order))
    flow.tick()
    flow.begin("expand0.0", gather_task(expand_low[0].reshape(-1, rows, D), forward_order))
    flow.begin("expand0.1", gather_task(expand_low[1].reshape(-1, rows, D), crossed_order))
    table_part, attend_part = flow.take("table", "attend0")
    attend_all = [[table_part[-1], attend_part[0], attend_part[1], attend_part[2]]]
    encoder_all = jnp.concatenate([table_part[i] for i in range(table_slots)], axis=1).T[
        : encoder_table.shape[0]
    ]
    halfway = SEQ // 2
    offset = core * halfway

    def own_first(values):
        return jnp.where(
            core == 0, values, jnp.concatenate([values[halfway:], values[:halfway]], axis=0)
        )

    patch_seq = own_first(patches[0])
    image_row = own_first(image_ids[0])
    buffer_row = own_first(buffer_flags[0])
    masked_row = own_first(loss_mask[0])
    weight_row = (masked_row * (1 - buffer_row)).astype(jnp.float32)
    flow.begin("attend1.0", gather_task(attend_low[4:6], forward_order))
    flow.begin("attend1.1", gather_task(attend_low[6:8], crossed_order))
    token_count = sum_all(jnp.sum(weight_row))
    own_patch = patch_seq[:halfway]
    buffer_on = buffer_row[:halfway, None] > 0
    masked_on = masked_row[:halfway, None] > 0
    same_image = image_row[:halfway, None] == image_row[None, :]
    gain_rows = encoder_all[:12].astype(jnp.float32)
    position = lax.dynamic_slice_in_dim(encoder_all, 12 + PATCH + offset, halfway, 0).astype(
        jnp.float32
    )
    embedded = product(own_patch, encoder_all[12 : 12 + PATCH])

    def entry(embedded_rows, token_pair, position_rows):
        return (
            jnp.where(buffer_on, token_pair[1], jnp.where(masked_on, token_pair[0], embedded_rows))
            + position_rows
        )

    entered, entry_back = jax.vjp(entry, embedded, gain_rows[10:12], position)
    state_rows = entered
    kept_all = []
    for depth_index in range(2):
        if depth_index == 1:
            attend_all.append([m for pair in flow.take("attend1.0", "attend1.1") for m in pair])
        state_rows, kept = block_forward(
            state_rows,
            attend_all[depth_index],
            flow,
            depth_index,
            gain_rows[4 * depth_index : 4 * depth_index + 4],
            same_image,
        )
        kept_all.append(kept)
        if depth_index == 0:
            flow.begin("expand1.0", gather_task(expand_low[2].reshape(-1, rows, D), forward_order))
            flow.begin("expand1.1", gather_task(expand_low[3].reshape(-1, rows, D), crossed_order))
            state_rows = flow.tick(state_rows)
            wide = dense_weight.shape[1]
            flow.begin(
                "head",
                gather_task(
                    jnp.stack(
                        [
                            padded(to_low(condition_weight), wide, HW),
                            padded(to_low(head_table).T, wide, HW),
                        ]
                    ),
                    forward_order,
                ),
            )
            flow.begin("dense", gather_task(dense_low, crossed_order))
    middle_rows = modulate_weight.shape[1] // 2
    modulate_low = to_low(modulate_weight)[None]
    flow.begin("modulate.0", gather_task(modulate_low[..., :middle_rows], forward_order))
    flow.begin("modulate.1", gather_task(modulate_low[..., middle_rows:], crossed_order))
    state_rows = flow.tick(state_rows)
    head_part, dense_all = flow.take("head", "dense")
    condition_all = head_part[0][:, :D]
    head_all = head_part[1][:, : head_table.shape[0]].T
    latent, third_back = jax.vjp(layer_norm, state_rows, gain_rows[8], gain_rows[9])
    latent_low = to_low(latent)
    condition_own = to_low(product_right(latent_low, condition_all))
    condition_rows = jnp.concatenate([condition_own, swap_core(condition_own)], axis=0)
    step_float = own_first(timesteps[0, 0]).astype(jnp.float32)
    alpha_row = alpha_bar(step_float)[:, None]
    target = own_first(noise_copies[0, 0]).astype(jnp.float32)
    noisy_low = to_low(
        jnp.sqrt(alpha_row) * patch_seq.astype(jnp.float32) + jnp.sqrt(1.0 - alpha_row) * target
    )
    lifted = product(noisy_low, head_all[:PATCH])
    feature_low = to_low(time_features(step_float))
    summed = condition_rows.astype(jnp.float32) + product(
        feature_low, head_all[PATCH : PATCH + FREQ]
    )
    activated, silu_back = jax.vjp(jax.nn.silu, summed)
    activated_low = flow.tick(to_low(activated))
    modulate_halves = [member[0] for member in flow.take("modulate.0", "modulate.1")]
    modulate_all = jnp.concatenate(modulate_halves, axis=1)
    modulation = product_right(activated_low, modulate_all)
    inner_rows, inner_back = jax.vjp(first_modulate, lifted, modulation)
    inner_low = to_low(inner_rows)
    expanded, dense_back = jax.vjp(jax.nn.gelu, product(inner_low, dense_all[0]))
    expanded_low = to_low(expanded)
    branch = product(expanded_low, dense_all[1])
    outer_rows, outer_back = jax.vjp(last_modulate, lifted, modulation, branch)
    outer_low = to_low(outer_rows)
    predicted = product_right(outer_low, head_all[PATCH + FREQ :])
    residue = predicted - target
    loss_local = jnp.sum(weight_row[:, None] * residue * residue) / PATCH
    predicted_grad = to_low(2.0 * weight_row[:, None] * residue / (PATCH * token_count))
    final_turned = product_left(outer_low, predicted_grad)
    lifted_grad, modulation_grad, branch_grad = outer_back(
        product(predicted_grad, head_all[PATCH + FREQ :])
    )
    branch_low = to_low(branch_grad)
    flow.begin("dense.1", weight_task(expanded_low, branch_low, forward_order))
    (expanded_grad,) = dense_back(product_right(branch_low, dense_all[1]))
    expanded_grad_low = flow.tick(to_low(expanded_grad))
    flow.begin("dense.0", weight_task(inner_low, expanded_grad_low, crossed_order))
    lifted_extra, modulation_extra = inner_back(product_right(expanded_grad_low, dense_all[0]))
    modulation_low = flow.tick(to_low(modulation_grad + modulation_extra))
    flow.begin(
        "spread",
        split_weight_task(modulation_low, activated_low, flow, ("modulate.2", "modulate.3")),
    )
    (summed_grad,) = silu_back(product(modulation_low, modulate_all))
    time_turned = product_left(to_low(summed_grad), feature_low)
    lift_turned = product_left(to_low(lifted_grad + lifted_extra), noisy_low)
    head_turned_grad = jnp.concatenate([lift_turned, time_turned, final_turned], axis=1)
    flow.begin("head_table", shared_task(head_turned_grad, forward_order))
    condition_grad = to_low(
        summed_grad[:halfway] + swap_core(to_low(summed_grad[halfway:])).astype(jnp.float32)
    )
    condition_grad = flow.tick(condition_grad)
    flow.begin("condition", weight_task(condition_grad, latent_low, crossed_order))
    state_grad, gain_nine, gain_ten = third_back(product(condition_grad, condition_all))
    gain_parts = [None, None]
    for depth_index in (1, 0):
        state_grad, gain_parts[depth_index] = block_backward(
            state_grad,
            kept_all[depth_index],
            attend_all[depth_index],
            flow,
            depth_index,
            same_image,
        )
    embedded_grad, token_grad, position_grad = entry_back(state_grad)
    embed_delta = product_left(own_patch, to_low(embedded_grad))
    small_delta = jnp.concatenate(
        [
            gain_parts[0],
            gain_parts[1],
            jnp.stack([gain_nine, gain_ten]),
            token_grad,
            embed_delta,
        ],
        axis=0,
    )
    small_delta = small_delta + swap_core(small_delta)
    small_half = small_delta.shape[0] // 2
    encoder_half = jnp.concatenate(
        [position_grad, lax.dynamic_slice_in_dim(small_delta, core * small_half, small_half, 0)],
        axis=0,
    ).T
    flow.begin("encoder", scatter_task(encoder_half[None], crossed_order))
    encoder_first_half, encoder_last_half = (m[0] for m in flow.take("encoder")[0])
    encoder_delta = jnp.concatenate(
        [
            encoder_first_half[:, halfway:],
            encoder_last_half[:, halfway:],
            encoder_first_half[:, :halfway],
            encoder_last_half[:, :halfway],
        ],
        axis=1,
    ).T
    flow.take("value0", "key0", "query0")
    results = flow.results
    attend_parts, expand_parts = ([], [])
    for depth_index in range(2):
        for name in ("query", "key", "value", "joined"):
            attend_parts.append(results[name + str(depth_index)][0])
        for name in ("lower", "upper"):
            expand_parts.append(results[name + str(depth_index)].reshape(-1, D))
    left_parts, right_parts = (results["modulate.2"], results["modulate.3"])
    reduced = (
        jnp.stack(attend_parts),
        jnp.stack(expand_parts),
        jnp.stack([results["dense.0"][0], results["dense.1"][0]]),
        jnp.concatenate([left_parts[0], right_parts[0], left_parts[1], right_parts[1]], axis=-1)[0],
        results["condition"][0],
        encoder_delta,
        results["head_table"].T,
    )
    squares = sum((jnp.sum(member * member) for member in reduced))
    totals = sum_all(jnp.stack([squares, loss_local]))
    square_total, loss_sum = (totals[0], totals[1])
    clip_norm = jnp.sqrt(square_total)
    factor = jnp.minimum(1.0, clip_bound / (clip_norm + 1e-06))
    velocities = (
        attend_velocity,
        expand_velocity,
        dense_velocity,
        modulate_velocity,
        condition_velocity,
    )
    moments = tuple((muon_keep * velocities[i] + factor * reduced[i] for i in range(5)))
    current = muon_steps(moments)
    devices = lax.axis_size(everywhere)
    masters = (attend_weight, expand_weight, dense_weight, modulate_weight, condition_weight)
    updated = tuple(
        (
            masters[i] * (1.0 - muon_rate * muon_decay)
            - muon_rate
            * max(1.0, current[i].shape[-2] * devices / current[i].shape[-1]) ** 0.5
            * current[i]
            for i in range(5)
        )
    )
    encoder_master, encoder_firsts, encoder_seconds = adam_shard(
        encoder_table, encoder_first, encoder_second, factor * reduced[5]
    )
    table_master, table_firsts, table_seconds = adam_shard(
        head_table, head_first, head_second, factor * reduced[6]
    )
    return (
        loss_sum,
        token_count,
        clip_norm,
        updated[0],
        moments[0],
        updated[1],
        moments[1],
        updated[2],
        moments[2],
        updated[3],
        moments[3],
        updated[4],
        moments[4],
        encoder_master,
        encoder_firsts,
        encoder_seconds,
        table_master,
        table_firsts,
        table_seconds,
    )


def solution(mesh):
    placed = (
        P("dp", None, None),
        P("copy", "dp", None, None),
        P("dp", None),
        P("dp", None),
        P("dp", None),
        P("copy", "dp", None),
        P(None, ("dp", "copy"), None),
        P(None, ("dp", "copy"), None),
        P(None, ("dp", "copy"), None),
        P(None, ("dp", "copy"), None),
        P(None, ("dp", "copy"), None),
        P(None, ("dp", "copy"), None),
        P(("dp", "copy"), None),
        P(("dp", "copy"), None),
        P(("dp", "copy"), None),
        P(("dp", "copy"), None),
        P(None, ("dp", "copy")),
        P(None, ("dp", "copy")),
        P(None, ("dp", "copy")),
        P(None, ("dp", "copy")),
        P(None, ("dp", "copy")),
        P(None, ("dp", "copy")),
    )
    return jax.shard_map(
        per_device,
        mesh=mesh,
        in_specs=placed,
        out_specs=(
            P(),
            P(),
            P(),
            P(None, ("dp", "copy"), None),
            P(None, ("dp", "copy"), None),
            P(None, ("dp", "copy"), None),
            P(None, ("dp", "copy"), None),
            P(None, ("dp", "copy"), None),
            P(None, ("dp", "copy"), None),
            P(("dp", "copy"), None),
            P(("dp", "copy"), None),
            P(("dp", "copy"), None),
            P(("dp", "copy"), None),
            P(None, ("dp", "copy")),
            P(None, ("dp", "copy")),
            P(None, ("dp", "copy")),
            P(None, ("dp", "copy")),
            P(None, ("dp", "copy")),
            P(None, ("dp", "copy")),
        ),
        check_vma=False,
    )
```

```python
import math

import jax
import jax.numpy as jnp
from jax import lax
from jax.sharding import PartitionSpec as P

D = 768
HEADS = 12
HD = 64
HW = 1024
PATCH = 64
FREQ = 256
SEQ = 1024
NS_STEPS = 2
STEP = 10
TSTEPS = 1000


precise_mode = lax.Precision.HIGHEST
norm_floor = 1e-06
score_factor = 0.125
newton_first = 3.4445
newton_second = -4.775
newton_third = 2.0315
muon_rate = 1.0
muon_decay = 0.01
muon_keep = 0.95
clip_bound = 0.001
adam_rate = 0.02
beta_first = 0.9
beta_second = 0.95
adam_floor = 1e-08
adam_decay = 0.1


def product(left_side, right_side):
    return jnp.dot(left_side, right_side, preferred_element_type=jnp.float32)


def product_left(left_side, right_side):
    return lax.dot_general(
        left_side, right_side, (((0,), (0,)), ((), ())), preferred_element_type=jnp.float32
    )


def product_right(left_side, right_side):
    return lax.dot_general(
        left_side, right_side, (((1,), (1,)), ((), ())), preferred_element_type=jnp.float32
    )


def to_low(values):
    return values.astype(jnp.bfloat16)


def layer_norm(values, gain_row, bias_row):
    centered = values - jnp.mean(values, axis=-1, keepdims=True)
    spread = jnp.mean(centered * centered, axis=-1, keepdims=True)
    return centered * lax.rsqrt(spread + norm_floor) * gain_row + bias_row


def plain_norm(values):
    centered = values - jnp.mean(values, axis=-1, keepdims=True)
    spread = jnp.mean(centered * centered, axis=-1, keepdims=True)
    return centered * lax.rsqrt(spread + norm_floor)


def alpha_bar(step_float):
    return jnp.cos(0.5 * math.pi * (step_float + 0.5) / TSTEPS) ** 2


def time_features(step_float):
    halfway = FREQ // 2
    frequency = jnp.exp(-math.log(10000.0) * jnp.arange(halfway).astype(jnp.float32) / halfway)
    angles = step_float[:, None] * frequency[None, :]
    return jnp.concatenate([jnp.cos(angles), jnp.sin(angles)], axis=1)


def first_modulate(lifted, modulation):
    return plain_norm(lifted) * (1.0 + modulation[:, HW : 2 * HW]) + modulation[:, :HW]


def last_modulate(lifted, modulation, branch):
    joined = lifted + modulation[:, 2 * HW : 3 * HW] * branch
    return plain_norm(joined) * (1.0 + modulation[:, 4 * HW :]) + modulation[:, 3 * HW : 4 * HW]


def grid_of(count):
    side = 1
    while 2 * side**3 < count:
        side *= 2
    if 2 * side**3 == count:
        return (2 * side, side, side)
    return (count, 1, 1)


def swap_core(values):
    return lax.ppermute(values, "copy", [(0, 1), (1, 0)])


def sum_all(values):
    values = values + swap_core(values)
    count = lax.axis_size("dp")
    if count & (count - 1):
        return lax.psum(values, "dp")
    step = 1
    while step < count:
        values = values + lax.ppermute(values, "dp", [(i, i ^ step) for i in range(count)])
        step *= 2
    return values


class Flow:
    def __init__(self):
        self.live, self.results = ([], {})

    def begin(self, name, task):
        self.live.append([name, task, *next(task)])

    def tick(self, *carry):
        due = [entry for entry in self.live if entry[3] <= 1]
        for entry in self.live:
            entry[3] -= 1
        carry, arrived = lax.optimization_barrier((carry, [entry[2] for entry in due]))
        for entry, values in zip(due, arrived):
            try:
                entry[2], entry[3] = entry[1].send(values)
            except StopIteration as stop:
                self.results[entry[0]] = stop.value
                self.live.remove(entry)
        return carry if len(carry) > 1 else (carry[0] if carry else None)

    def take(self, *names):
        while any(name not in self.results for name in names):
            self.tick()
        return [self.results[name] for name in names]


def columns_of(values, core):
    half = values.shape[-1] // 2
    return lax.dynamic_slice_in_dim(values, core * half, half, values.ndim - 1)


def joined(parts, axis):
    return parts[0] if len(parts) == 1 else jnp.concatenate(parts, axis=axis)


def bits_in_order(crossed):
    grid = grid_of(lax.axis_size("dp"))
    counts = [size.bit_length() - 1 for size in grid]
    z_bits = list(range(counts[2] + counts[1], sum(counts)))
    y_bits = list(range(counts[2], counts[2] + counts[1]))
    x_bits = list(range(counts[2]))
    return (y_bits + x_bits if crossed else x_bits + y_bits) + z_bits


def scatter_task(parts, crossed, axis, exact, lag=2):
    core = lax.axis_index("copy")
    here = lax.axis_index("dp")
    chips = lax.axis_size("dp")
    sizes = [part.shape[axis] for part in parts]
    order = bits_in_order(crossed)
    parts = [
        part.reshape(
            part.shape[0], *[2] * len(order), part.shape[1] // chips, part.shape[2]
        )
        for part in parts
    ]
    left = sorted(order, reverse=True)
    for bit in order:
        position, mine = (1 + left.index(bit), here // 2**bit % 2)
        sent = []
        for part, keep in zip(parts, exact):
            half = lax.dynamic_index_in_dim(part, 1 - mine, position, keepdims=False)
            if keep:
                near = lax.reduce_precision(half, 8, 7)
                sent += [to_low(near), to_low(half - near)]
            else:
                sent.append(to_low(half))
        pairs = [(i, i ^ 2**bit) for i in range(chips)]
        (arrived,) = yield ([lax.ppermute(joined(sent, axis), "dp", pairs)], lag)
        start, totals = (0, [])
        for part, keep, size in zip(parts, exact, sizes):
            total = lax.dynamic_index_in_dim(part, mine, position, keepdims=False)
            for number in range(2 if keep else 1):
                piece = lax.slice_in_dim(
                    arrived, start, start + size, axis=axis % arrived.ndim
                )
                total = total + piece.astype(jnp.float32)
                start += size
            totals.append(total)
        parts = totals
        left.remove(bit)
    values = joined(parts, axis)
    half = values.shape[1] // 2
    mine = lax.dynamic_slice_in_dim(values, core * half, half, 1)
    (arrived,) = yield (
        [swap_core(lax.dynamic_slice_in_dim(values, (1 - core) * half, half, 1))],
        1,
    )
    first = jnp.where(core == 0, mine, arrived)
    last = jnp.where(core == 0, arrived, mine)
    starts = [sum(sizes[:i]) for i in range(len(sizes))]
    return [
        tuple(lax.slice_in_dim(m, start, start + size, axis=axis % m.ndim) for m in (first, last))
        for start, size in zip(starts, sizes)
    ]


def weight_task(products, crossed, axis, tables=(), lag=2):
    core = lax.axis_index("copy")

    def some(right_sides, which):
        return joined([columns_of(right, which) for right in right_sides], 1)

    sent = [product_left(left, some(rights, 1 - core)) for slots, left, rights in products]
    sent += [columns_of(table, 1 - core) for table in tables]
    arrived = yield ([swap_core(part) for part in sent], 1)
    totals = [
        product_left(left, some(rights, core)) + part
        for (slots, left, rights), part in zip(products, arrived)
    ]
    totals = [
        total.reshape(member[0], total.shape[0] // member[0], total.shape[1])
        for total, member in zip(totals, products)
    ]
    for table, part in zip(tables, arrived[len(products) :]):
        totals.append((columns_of(table, core) + part)[None])
    exact = [False] * len(products) + [True] * len(tables)
    halves = yield from scatter_task(totals, crossed, axis, exact, lag)
    found = []
    counts = [len(member[2]) for member in products] + [1] * len(tables)
    for (first, last), count in zip(halves, counts):
        width = first.shape[-1] // count
        for i in range(count):
            pair = [m[..., i * width : (i + 1) * width] for m in (first, last)]
            found.append(jnp.concatenate(pair, axis=-1))
    return found


def split_weight_task(left_side, right_side, flow, names):
    core = lax.axis_index("copy")
    (arrived,) = yield ([swap_core(product_left(left_side, columns_of(right_side, 1 - core)))], 1)
    total = (product_left(left_side, columns_of(right_side, core)) + arrived)[None]
    quarter = total.shape[-1] // 2
    flow.begin(names[0], scatter_task([total[..., :quarter]], False, 0, [False]))
    flow.begin(names[1], scatter_task([total[..., quarter:]], True, 0, [False]))
    return None


def attention_scores(query_heads, key_heads, same_image):
    raw_scores = jnp.einsum(
        "qhd,khd->hqk", query_heads, key_heads, preferred_element_type=jnp.float32
    )
    return jnp.where(same_image[None], raw_scores * score_factor, -1e30)


def block_forward(entered, attend_low, expand_low, flow, gain_rows, same_image):
    halfway = entered.shape[0]
    normed, first_back = jax.vjp(layer_norm, entered, gain_rows[0], gain_rows[1])
    normed_low = to_low(normed)
    key_low = to_low(product(normed_low, attend_low[1]))
    value_low = to_low(product(normed_low, attend_low[2]))
    key_all = jnp.concatenate([key_low, swap_core(key_low)], axis=0)
    value_all = jnp.concatenate([value_low, swap_core(value_low)], axis=0)
    query_low = to_low(product(normed_low, attend_low[0]))
    query_heads = query_low.reshape(halfway, HEADS, HD)
    key_heads = key_all.reshape(SEQ, HEADS, HD)
    value_heads = value_all.reshape(SEQ, HEADS, HD)
    scores = attention_scores(query_heads, key_heads, same_image)
    highest = jnp.max(scores, axis=-1, keepdims=True)
    exponent_rows = jnp.exp(scores - highest)
    row_total = jnp.sum(exponent_rows, axis=-1, keepdims=True)
    log_total = highest + jnp.log(row_total)
    attended = to_low(
        jnp.einsum(
            "hqk,khd->qhd",
            to_low(exponent_rows / row_total),
            value_heads,
            preferred_element_type=jnp.float32,
        ).reshape(halfway, D)
    )
    middle = entered + product(attended, attend_low[3])
    normed_two, second_back = jax.vjp(layer_norm, middle, gain_rows[2], gain_rows[3])
    normed_two_low = to_low(normed_two)
    hidden, gelu_back = jax.vjp(jax.nn.gelu, product_right(normed_two_low, expand_low[0]))
    hidden_low = to_low(hidden)
    output_rows = middle + product(hidden_low, expand_low[1])
    kept = (
        first_back,
        normed_low,
        query_heads,
        key_heads,
        value_heads,
        log_total,
        attended,
        second_back,
        normed_two_low,
        gelu_back,
        hidden_low,
        expand_low,
    )
    return (output_rows, kept)


def block_backward(output_grad, kept, attend_low, flow, depth, same_image):
    (
        first_back,
        normed_low,
        query_heads,
        key_heads,
        value_heads,
        log_total,
        attended,
        second_back,
        normed_two_low,
        gelu_back,
        hidden_low,
        expand_low,
    ) = kept
    halfway = attended.shape[0]
    copies = expand_low[0].shape[0] // D
    upper_low = to_low(output_grad)
    flow.begin(
        "upper%d" % depth,
        weight_task([(copies, hidden_low, [upper_low])], False, 0),
    )
    (hidden_grad,) = gelu_back(product_right(upper_low, expand_low[1]))
    hidden_grad_low = flow.tick(to_low(hidden_grad))
    middle_extra, gain_three, gain_four = second_back(product(hidden_grad_low, expand_low[0]))
    middle_grad = flow.tick(output_grad + middle_extra)
    projected_low = to_low(middle_grad)
    flow.begin(
        "lower%d" % depth,
        weight_task(
            [(copies, hidden_grad_low, [normed_two_low]), (1, attended, [projected_low])],
            True,
            0,
        ),
    )
    attended_grad = to_low(product_right(projected_low, attend_low[3])).reshape(halfway, HEADS, HD)
    attended_grad = flow.tick(attended_grad)
    probability = jnp.exp(attention_scores(query_heads, key_heads, same_image) - log_total)
    soft_grad = jnp.einsum(
        "qhd,khd->hqk", attended_grad, value_heads, preferred_element_type=jnp.float32
    )
    value_part = jnp.einsum(
        "hqk,qhd->khd", to_low(probability), attended_grad, preferred_element_type=jnp.float32
    )
    score_low = to_low(
        probability
        * (soft_grad - jnp.sum(probability * soft_grad, axis=-1, keepdims=True))
        * score_factor
    )
    score_low, value_part = flow.tick(score_low, value_part)
    key_part = jnp.einsum(
        "hqk,qhd->khd", score_low, query_heads, preferred_element_type=jnp.float32
    )
    key_part = flow.tick(key_part)
    query_grad = to_low(
        jnp.einsum(
            "hqk,khd->qhd", score_low, key_heads, preferred_element_type=jnp.float32
        ).reshape(halfway, D)
    )
    key_part = key_part.reshape(SEQ, D)
    value_part = value_part.reshape(SEQ, D)
    value_grad = to_low(
        value_part[:halfway] + swap_core(to_low(value_part[halfway:])).astype(jnp.float32)
    )
    key_grad = to_low(
        key_part[:halfway] + swap_core(to_low(key_part[halfway:])).astype(jnp.float32)
    )
    query_grad, key_grad, value_grad = flow.tick(query_grad, key_grad, value_grad)
    flow.begin(
        "attend%d" % depth,
        weight_task([(1, normed_low, [query_grad, key_grad, value_grad])], False, 0, (), 1 + depth),
    )
    normed_grad = (
        product_right(query_grad, attend_low[0])
        + product_right(key_grad, attend_low[1])
        + product_right(value_grad, attend_low[2])
    )
    entered_extra, gain_one, gain_two = first_back(normed_grad)
    gain_delta = jnp.stack([gain_one, gain_two, gain_three, gain_four])
    return (flow.tick(middle_grad + entered_extra), gain_delta)


def fine(left_side, right_side):
    return jnp.dot(
        left_side, right_side, precision=lax.Precision.HIGH, preferred_element_type=jnp.float32
    )


def newton_extra(gram_matrix):
    first_tail = newton_second * gram_matrix + newton_third * fine(gram_matrix, gram_matrix)
    once = newton_first * gram_matrix + fine(gram_matrix, first_tail)
    later = newton_first * once + fine(once, first_tail)
    last_tail = newton_second * later + newton_third * fine(later, later)
    return newton_first * (first_tail + last_tail) + fine(first_tail, last_tail)


def slots_of(devices):
    slots = [(14, 0, 2), (14, 1, 2)]
    for matrix in range(8, 12):
        slots += [(matrix, 0, 2), (matrix, 1, 2)]
    slots += [(matrix, 0, 1) for matrix in list(range(8)) + [12, 13, 15]]
    return slots + [None] * (devices - len(slots))


def padded(piece, rows, columns):
    return jnp.pad(piece, ((0, rows - piece.shape[0]), (0, columns - piece.shape[1])))


def muon_steps(moments):
    devices = lax.axis_size(("dp", "copy"))
    pieces = (
        [moments[0][i] for i in range(8)]
        + [moments[1][i] for i in range(4)]
        + [moments[2][i] for i in range(2)]
        + [moments[3], moments[4]]
    )
    slots = slots_of(devices)
    highest = max(pieces[slot[0]].shape[0] // slot[2] for slot in slots if slot)
    widest = max(piece.shape[1] for piece in pieces)
    sending = []
    for slot in slots:
        if slot is None:
            sending.append(jnp.zeros((highest, widest), jnp.bfloat16))
        else:
            rows = pieces[slot[0]].shape[0] // slot[2]
            piece = to_low(pieces[slot[0]][slot[1] * rows : (slot[1] + 1) * rows])
            sending.append(padded(piece, highest, widest))
    held = lax.all_to_all(jnp.stack(sending), ("dp", "copy"), 0, 0).reshape(
        devices * highest, widest
    )
    squares = sum_all(jnp.stack([jnp.sum(piece * piece) for piece in pieces]))
    inverse = 1.0 / (jnp.sqrt(squares) + 1e-07)
    me = lax.axis_index(("dp", "copy"))
    matrix_here = jnp.asarray([slot[0] if slot else 0 for slot in slots], jnp.int32)[me]
    shared_here = jnp.asarray([1.0 if slot and slot[2] == 2 else 0.0 for slot in slots])[me]
    scale_here = inverse[matrix_here]
    gram_matrix = product_left(held, held)
    gram_matrix = gram_matrix + shared_here * swap_core(gram_matrix)
    extra = newton_extra(gram_matrix * (scale_here * scale_here))
    result = to_low(product(held, to_low(extra)) * scale_here)
    back = lax.all_to_all(result.reshape(devices, highest, widest), ("dp", "copy"), 0, 0)
    found = []
    for matrix, piece in enumerate(pieces):
        parts = [
            back[device, : piece.shape[0] // slot[2], : piece.shape[1]]
            for device, slot in enumerate(slots)
            if slot and slot[0] == matrix
        ]
        whole = jnp.concatenate(parts, axis=0) if len(parts) > 1 else parts[0]
        found.append(
            newton_first * newton_first * inverse[matrix] * piece + whole.astype(jnp.float32)
        )
    return (
        jnp.stack(found[:8]),
        jnp.stack(found[8:12]),
        jnp.stack(found[12:14]),
        found[14],
        found[15],
    )


def adam_shard(master, first, second, gradient):
    first_new = beta_first * first + (1.0 - beta_first) * gradient
    second_new = beta_second * second + (1.0 - beta_second) * gradient * gradient
    corrected_first = first_new / (1.0 - beta_first**STEP)
    corrected_second = second_new / (1.0 - beta_second**STEP)
    master_new = master - adam_rate * (
        corrected_first / (jnp.sqrt(corrected_second) + adam_floor) + adam_decay * master
    )
    return (master_new, first_new, second_new)


def per_device(
    patches,
    noise_copies,
    image_ids,
    buffer_flags,
    loss_mask,
    timesteps,
    attend_weight,
    attend_velocity,
    expand_weight,
    expand_velocity,
    dense_weight,
    dense_velocity,
    modulate_weight,
    modulate_velocity,
    condition_weight,
    condition_velocity,
    encoder_table,
    encoder_first,
    encoder_second,
    head_table,
    head_first,
    head_second,
):
    everywhere = ("dp", "copy")
    core = lax.axis_index("copy")
    flow = Flow()
    attend_low, expand_low, dense_low = (
        to_low(attend_weight),
        to_low(expand_weight),
        to_low(dense_weight),
    )
    rows, wide = (attend_weight.shape[1], dense_weight.shape[1])
    table_slots = -(-encoder_table.shape[0] // D)
    encoder_turned = padded(to_low(encoder_table).T, rows, table_slots * D)
    encoder_turned = encoder_turned.reshape(rows, table_slots, D).transpose(1, 0, 2)
    expand_slots = expand_low.reshape(expand_low.shape[0], -1, rows, D)
    copies = expand_slots.shape[1]

    def gathered(members):
        return lax.all_gather(jnp.concatenate(members, axis=0), everywhere, axis=1, tiled=True)

    entry_part = gathered([attend_low[:4], encoder_turned])
    expand_part = gathered([expand_slots[0], expand_slots[1]])
    later_part = gathered([attend_low[4:], expand_slots[2], expand_slots[3]])
    modulate_slots = to_low(modulate_weight).reshape(-1, wide, HW)
    head_part = gathered(
        [
            padded(to_low(head_table).T, wide, HW)[None],
            padded(to_low(condition_weight), wide, HW)[None],
            dense_low,
            modulate_slots,
        ]
    )
    attend_all = [entry_part[:4], later_part[:4]]
    expand_all = [
        (
            member[: copies].reshape(copies * D, D),
            member[copies:].reshape(copies * D, D),
        )
        for member in (expand_part, later_part[4:])
    ]
    encoder_all = jnp.concatenate([entry_part[4 + i] for i in range(table_slots)], axis=1).T[
        : encoder_table.shape[0]
    ]
    head_all = head_part[0][:, : head_table.shape[0]].T
    condition_all = head_part[1][:, :D]
    dense_all = head_part[2:4]
    modulate_all = (
        head_part[4:]
        .reshape(modulate_slots.shape[0], -1, wide, HW)
        .transpose(1, 0, 2, 3)
        .reshape(modulate_slots.shape[0] * HW, HW)
    )
    halfway = SEQ // 2
    offset = core * halfway

    def own_first(values):
        return jnp.where(
            core == 0, values, jnp.concatenate([values[halfway:], values[:halfway]], axis=0)
        )

    patch_seq = own_first(patches[0])
    image_row = own_first(image_ids[0])
    buffer_row = own_first(buffer_flags[0])
    masked_row = own_first(loss_mask[0])
    weight_row = (masked_row * (1 - buffer_row)).astype(jnp.float32)
    token_count = sum_all(jnp.sum(weight_row))
    own_patch = patch_seq[:halfway]
    buffer_on = buffer_row[:halfway, None] > 0
    masked_on = masked_row[:halfway, None] > 0
    same_image = image_row[:halfway, None] == image_row[None, :]
    gain_rows = encoder_all[:12].astype(jnp.float32)
    position = lax.dynamic_slice_in_dim(encoder_all, 12 + PATCH + offset, halfway, 0).astype(
        jnp.float32
    )
    embedded = product(own_patch, encoder_all[12 : 12 + PATCH])

    def entry(embedded_rows, token_pair, position_rows):
        return (
            jnp.where(buffer_on, token_pair[1], jnp.where(masked_on, token_pair[0], embedded_rows))
            + position_rows
        )

    entered, entry_back = jax.vjp(entry, embedded, gain_rows[10:12], position)
    state_rows = entered
    kept_all = []
    for depth_index in range(2):
        state_rows, kept = block_forward(
            state_rows,
            attend_all[depth_index],
            expand_all[depth_index],
            flow,
            gain_rows[4 * depth_index : 4 * depth_index + 4],
            same_image,
        )
        kept_all.append(kept)
    latent, third_back = jax.vjp(layer_norm, state_rows, gain_rows[8], gain_rows[9])
    latent_low = to_low(latent)
    condition_own = to_low(product_right(latent_low, condition_all))
    condition_rows = jnp.concatenate([condition_own, swap_core(condition_own)], axis=0)
    step_float = own_first(timesteps[0, 0]).astype(jnp.float32)
    alpha_row = alpha_bar(step_float)[:, None]
    target = own_first(noise_copies[0, 0]).astype(jnp.float32)
    noisy_low = to_low(
        jnp.sqrt(alpha_row) * patch_seq.astype(jnp.float32) + jnp.sqrt(1.0 - alpha_row) * target
    )
    lifted = product(noisy_low, head_all[:PATCH])
    feature_low = to_low(time_features(step_float))
    summed = condition_rows.astype(jnp.float32) + product(
        feature_low, head_all[PATCH : PATCH + FREQ]
    )
    activated, silu_back = jax.vjp(jax.nn.silu, summed)
    activated_low = to_low(activated)
    modulation = product_right(activated_low, modulate_all)
    inner_rows, inner_back = jax.vjp(first_modulate, lifted, modulation)
    inner_low = to_low(inner_rows)
    expanded, dense_back = jax.vjp(jax.nn.gelu, product(inner_low, dense_all[0]))
    expanded_low = to_low(expanded)
    branch = product(expanded_low, dense_all[1])
    outer_rows, outer_back = jax.vjp(last_modulate, lifted, modulation, branch)
    outer_low = to_low(outer_rows)
    predicted = product_right(outer_low, head_all[PATCH + FREQ :])
    residue = predicted - target
    loss_local = jnp.sum(weight_row[:, None] * residue * residue) / PATCH
    predicted_grad = to_low(2.0 * weight_row[:, None] * residue / (PATCH * token_count))
    final_turned = product_left(outer_low, predicted_grad)
    lifted_grad, modulation_grad, branch_grad = outer_back(
        product(predicted_grad, head_all[PATCH + FREQ :])
    )
    branch_low = to_low(branch_grad)
    (expanded_grad,) = dense_back(product_right(branch_low, dense_all[1]))
    expanded_grad_low = to_low(expanded_grad)
    lifted_extra, modulation_extra = inner_back(product_right(expanded_grad_low, dense_all[0]))
    modulation_low = flow.tick(to_low(modulation_grad + modulation_extra))
    flow.begin(
        "spread",
        split_weight_task(modulation_low, activated_low, flow, ("modulate.2", "modulate.3")),
    )
    (summed_grad,) = silu_back(product(modulation_low, modulate_all))
    time_turned = product_left(to_low(summed_grad), feature_low)
    lift_turned = product_left(to_low(lifted_grad + lifted_extra), noisy_low)
    head_turned_grad = jnp.concatenate([lift_turned, time_turned, final_turned], axis=1)
    condition_grad = to_low(
        summed_grad[:halfway] + swap_core(to_low(summed_grad[halfway:])).astype(jnp.float32)
    )
    condition_grad = flow.tick(condition_grad)
    flow.begin(
        "head",
        weight_task(
            [
                (1, inner_low, [expanded_grad_low]),
                (1, expanded_low, [branch_low]),
                (1, condition_grad, [latent_low]),
            ],
            True,
            -1,
            [head_turned_grad],
        ),
    )
    state_grad, gain_nine, gain_ten = third_back(product(condition_grad, condition_all))
    gain_parts = [None, None]
    for depth_index in (1, 0):
        state_grad, gain_parts[depth_index] = block_backward(
            state_grad,
            kept_all[depth_index],
            attend_all[depth_index],
            flow,
            depth_index,
            same_image,
        )
    embedded_grad, token_grad, position_grad = entry_back(state_grad)
    embed_delta = product_left(own_patch, to_low(embedded_grad))
    small_delta = jnp.concatenate(
        [
            gain_parts[0],
            gain_parts[1],
            jnp.stack([gain_nine, gain_ten]),
            token_grad,
            embed_delta,
        ],
        axis=0,
    )
    small_delta = small_delta + swap_core(small_delta)
    small_half = small_delta.shape[0] // 2
    encoder_half = jnp.concatenate(
        [position_grad, lax.dynamic_slice_in_dim(small_delta, core * small_half, small_half, 0)],
        axis=0,
    ).T
    flow.begin("encoder", scatter_task([encoder_half[None]], True, 0, [True], 1))
    encoder_first_half, encoder_last_half = (m[0] for m in flow.take("encoder")[0][0])
    encoder_delta = jnp.concatenate(
        [
            encoder_first_half[:, halfway:],
            encoder_last_half[:, halfway:],
            encoder_first_half[:, :halfway],
            encoder_last_half[:, :halfway],
        ],
        axis=1,
    ).T
    blocks = [name + str(i) for i in range(2) for name in ("upper", "lower", "attend")]
    flow.take("head", "modulate.2", "modulate.3", *blocks)
    results = flow.results
    attend_parts, expand_parts = ([], [])
    for depth_index in range(2):
        lower_delta, output_delta = results["lower%d" % depth_index]
        (upper_delta,) = results["upper%d" % depth_index]
        attend_parts += [member[0] for member in results["attend%d" % depth_index]]
        attend_parts.append(output_delta[0])
        expand_parts += [lower_delta.reshape(-1, D), upper_delta.reshape(-1, D)]
    first_delta, second_delta, condition_delta, head_delta = results["head"]
    (left_parts,), (right_parts,) = (results["modulate.2"], results["modulate.3"])
    reduced = (
        jnp.stack(attend_parts),
        jnp.stack(expand_parts),
        jnp.stack([first_delta[0], second_delta[0]]),
        jnp.concatenate([left_parts[0], right_parts[0], left_parts[1], right_parts[1]], axis=-1)[0],
        condition_delta[0],
        encoder_delta,
        head_delta[0].T,
    )
    squares = sum((jnp.sum(member * member) for member in reduced))
    totals = sum_all(jnp.stack([squares, loss_local]))
    square_total, loss_sum = (totals[0], totals[1])
    clip_norm = jnp.sqrt(square_total)
    factor = jnp.minimum(1.0, clip_bound / (clip_norm + 1e-06))
    velocities = (
        attend_velocity,
        expand_velocity,
        dense_velocity,
        modulate_velocity,
        condition_velocity,
    )
    moments = tuple((muon_keep * velocities[i] + factor * reduced[i] for i in range(5)))
    current = muon_steps(moments)
    devices = lax.axis_size(everywhere)
    masters = (attend_weight, expand_weight, dense_weight, modulate_weight, condition_weight)
    updated = tuple(
        (
            masters[i] * (1.0 - muon_rate * muon_decay)
            - muon_rate
            * max(1.0, current[i].shape[-2] * devices / current[i].shape[-1]) ** 0.5
            * current[i]
            for i in range(5)
        )
    )
    encoder_master, encoder_firsts, encoder_seconds = adam_shard(
        encoder_table, encoder_first, encoder_second, factor * reduced[5]
    )
    table_master, table_firsts, table_seconds = adam_shard(
        head_table, head_first, head_second, factor * reduced[6]
    )
    return (
        loss_sum,
        token_count,
        clip_norm,
        updated[0],
        moments[0],
        updated[1],
        moments[1],
        updated[2],
        moments[2],
        updated[3],
        moments[3],
        updated[4],
        moments[4],
        encoder_master,
        encoder_firsts,
        encoder_seconds,
        table_master,
        table_firsts,
        table_seconds,
    )


def solution(mesh):
    placed = (
        P("dp", None, None),
        P("copy", "dp", None, None),
        P("dp", None),
        P("dp", None),
        P("dp", None),
        P("copy", "dp", None),
        P(None, ("dp", "copy"), None),
        P(None, ("dp", "copy"), None),
        P(None, ("dp", "copy"), None),
        P(None, ("dp", "copy"), None),
        P(None, ("dp", "copy"), None),
        P(None, ("dp", "copy"), None),
        P(("dp", "copy"), None),
        P(("dp", "copy"), None),
        P(("dp", "copy"), None),
        P(("dp", "copy"), None),
        P(None, ("dp", "copy")),
        P(None, ("dp", "copy")),
        P(None, ("dp", "copy")),
        P(None, ("dp", "copy")),
        P(None, ("dp", "copy")),
        P(None, ("dp", "copy")),
    )
    return jax.shard_map(
        per_device,
        mesh=mesh,
        in_specs=placed,
        out_specs=(
            P(),
            P(),
            P(),
            P(None, ("dp", "copy"), None),
            P(None, ("dp", "copy"), None),
            P(None, ("dp", "copy"), None),
            P(None, ("dp", "copy"), None),
            P(None, ("dp", "copy"), None),
            P(None, ("dp", "copy"), None),
            P(("dp", "copy"), None),
            P(("dp", "copy"), None),
            P(("dp", "copy"), None),
            P(("dp", "copy"), None),
            P(None, ("dp", "copy")),
            P(None, ("dp", "copy")),
            P(None, ("dp", "copy")),
            P(None, ("dp", "copy")),
            P(None, ("dp", "copy")),
            P(None, ("dp", "copy")),
        ),
        check_vma=False,
    )
```

```python
import math

import jax
import jax.numpy as jnp
from jax import lax
from jax.sharding import PartitionSpec as P

D = 768
HEADS = 12
HD = 64
HW = 1024
PATCH = 64
FREQ = 256
SEQ = 1024
NS_STEPS = 2
STEP = 10
TSTEPS = 1000


precise_mode = lax.Precision.HIGHEST
norm_floor = 1e-06
score_factor = 0.125
newton_first = 3.4445
newton_second = -4.775
newton_third = 2.0315
muon_rate = 1.0
muon_decay = 0.01
muon_keep = 0.95
clip_bound = 0.001
adam_rate = 0.02
beta_first = 0.9
beta_second = 0.95
adam_floor = 1e-08
adam_decay = 0.1


def product(left_side, right_side):
    return jnp.dot(left_side, right_side, preferred_element_type=jnp.float32)


def product_left(left_side, right_side):
    return lax.dot_general(
        left_side, right_side, (((0,), (0,)), ((), ())), preferred_element_type=jnp.float32
    )


def product_right(left_side, right_side):
    return lax.dot_general(
        left_side, right_side, (((1,), (1,)), ((), ())), preferred_element_type=jnp.float32
    )


def to_low(values):
    return values.astype(jnp.bfloat16)


def layer_norm(values, gain_row, bias_row):
    centered = values - jnp.mean(values, axis=-1, keepdims=True)
    spread = jnp.mean(centered * centered, axis=-1, keepdims=True)
    return centered * lax.rsqrt(spread + norm_floor) * gain_row + bias_row


def plain_norm(values):
    centered = values - jnp.mean(values, axis=-1, keepdims=True)
    spread = jnp.mean(centered * centered, axis=-1, keepdims=True)
    return centered * lax.rsqrt(spread + norm_floor)


def alpha_bar(step_float):
    return jnp.cos(0.5 * math.pi * (step_float + 0.5) / TSTEPS) ** 2


def time_features(step_float):
    halfway = FREQ // 2
    frequency = jnp.exp(-math.log(10000.0) * jnp.arange(halfway).astype(jnp.float32) / halfway)
    angles = step_float[:, None] * frequency[None, :]
    return jnp.concatenate([jnp.cos(angles), jnp.sin(angles)], axis=1)


def first_modulate(lifted, modulation):
    return plain_norm(lifted) * (1.0 + modulation[:, HW : 2 * HW]) + modulation[:, :HW]


def last_modulate(lifted, modulation, branch):
    joined = lifted + modulation[:, 2 * HW : 3 * HW] * branch
    return plain_norm(joined) * (1.0 + modulation[:, 4 * HW :]) + modulation[:, 3 * HW : 4 * HW]


def grid_of(count):
    side = 1
    while 2 * side**3 < count:
        side *= 2
    if 2 * side**3 == count:
        return (2 * side, side, side)
    return (count, 1, 1)


def swap_core(values):
    return lax.ppermute(values, "copy", [(0, 1), (1, 0)])


def sum_all(values):
    values = values + swap_core(values)
    count = lax.axis_size("dp")
    if count & (count - 1):
        return lax.psum(values, "dp")
    step = 1
    while step < count:
        values = values + lax.ppermute(values, "dp", [(i, i ^ step) for i in range(count)])
        step *= 2
    return values


class Flow:
    def __init__(self):
        self.live, self.results, self.waiting = ([], {}, [])

    def begin(self, name, task):
        self.live.append([name, task, *next(task)])

    def when(self, names, name, make):
        self.waiting.append((names, name, make))

    def tick(self, *carry):
        due = [entry for entry in self.live if entry[3] <= 1]
        for entry in self.live:
            entry[3] -= 1
        carry, arrived = lax.optimization_barrier((carry, [entry[2] for entry in due]))
        for entry, values in zip(due, arrived):
            try:
                entry[2], entry[3] = entry[1].send(values)
            except StopIteration as stop:
                self.results[entry[0]] = stop.value
                self.live.remove(entry)
        for entry in list(self.waiting):
            if all(name in self.results for name in entry[0]):
                self.waiting.remove(entry)
                self.begin(entry[1], entry[2]())
        return carry if len(carry) > 1 else (carry[0] if carry else None)

    def take(self, *names):
        while any(name not in self.results for name in names):
            self.tick()
        return [self.results[name] for name in names]


def columns_of(values, core):
    half = values.shape[-1] // 2
    return lax.dynamic_slice_in_dim(values, core * half, half, values.ndim - 1)


def joined(parts, axis):
    return parts[0] if len(parts) == 1 else jnp.concatenate(parts, axis=axis)


def bits_in_order(crossed):
    grid = grid_of(lax.axis_size("dp"))
    counts = [size.bit_length() - 1 for size in grid]
    z_bits = list(range(counts[2] + counts[1], sum(counts)))
    y_bits = list(range(counts[2], counts[2] + counts[1]))
    x_bits = list(range(counts[2]))
    return (y_bits + x_bits if crossed else x_bits + y_bits) + z_bits


def scatter_task(parts, crossed, axis, exact, lag=2):
    core = lax.axis_index("copy")
    here = lax.axis_index("dp")
    chips = lax.axis_size("dp")
    sizes = [part.shape[axis] for part in parts]
    order = bits_in_order(crossed)
    parts = [
        part.reshape(
            part.shape[0], *[2] * len(order), part.shape[1] // chips, part.shape[2]
        )
        for part in parts
    ]
    left = sorted(order, reverse=True)
    for bit in order:
        position, mine = (1 + left.index(bit), here // 2**bit % 2)
        sent = []
        for part, keep in zip(parts, exact):
            half = lax.dynamic_index_in_dim(part, 1 - mine, position, keepdims=False)
            if keep:
                near = lax.reduce_precision(half, 8, 7)
                sent += [to_low(near), to_low(half - near)]
            else:
                sent.append(to_low(half))
        pairs = [(i, i ^ 2**bit) for i in range(chips)]
        (arrived,) = yield ([lax.ppermute(joined(sent, axis), "dp", pairs)], lag)
        start, totals = (0, [])
        for part, keep, size in zip(parts, exact, sizes):
            total = lax.dynamic_index_in_dim(part, mine, position, keepdims=False)
            for number in range(2 if keep else 1):
                piece = lax.slice_in_dim(
                    arrived, start, start + size, axis=axis % arrived.ndim
                )
                total = total + piece.astype(jnp.float32)
                start += size
            totals.append(total)
        parts = totals
        left.remove(bit)
    values = joined(parts, axis)
    half = values.shape[1] // 2
    mine = lax.dynamic_slice_in_dim(values, core * half, half, 1)
    (arrived,) = yield (
        [swap_core(lax.dynamic_slice_in_dim(values, (1 - core) * half, half, 1))],
        1,
    )
    first = jnp.where(core == 0, mine, arrived)
    last = jnp.where(core == 0, arrived, mine)
    starts = [sum(sizes[:i]) for i in range(len(sizes))]
    return [
        tuple(lax.slice_in_dim(m, start, start + size, axis=axis % m.ndim) for m in (first, last))
        for start, size in zip(starts, sizes)
    ]


def weight_task(products, crossed, axis, tables=(), lag=2):
    core = lax.axis_index("copy")

    def some(right_sides, which):
        return joined([columns_of(right, which) for right in right_sides], 1)

    sent = [product_left(left, some(rights, 1 - core)) for slots, left, rights in products]
    sent += [columns_of(table, 1 - core) for table in tables]
    arrived = yield ([swap_core(part) for part in sent], 1)
    totals = [
        product_left(left, some(rights, core)) + part
        for (slots, left, rights), part in zip(products, arrived)
    ]
    totals = [
        total.reshape(member[0], total.shape[0] // member[0], total.shape[1])
        for total, member in zip(totals, products)
    ]
    for table, part in zip(tables, arrived[len(products) :]):
        totals.append((columns_of(table, core) + part)[None])
    exact = [False] * len(products) + [True] * len(tables)
    halves = yield from scatter_task(totals, crossed, axis, exact, lag)
    found = []
    counts = [len(member[2]) for member in products] + [1] * len(tables)
    for (first, last), count in zip(halves, counts):
        width = first.shape[-1] // count
        for i in range(count):
            pair = [m[..., i * width : (i + 1) * width] for m in (first, last)]
            found.append(jnp.concatenate(pair, axis=-1))
    return found


def split_weight_task(left_side, right_side, flow, names):
    core = lax.axis_index("copy")
    (arrived,) = yield ([swap_core(product_left(left_side, columns_of(right_side, 1 - core)))], 1)
    total = (product_left(left_side, columns_of(right_side, core)) + arrived)[None]
    quarter = total.shape[-1] // 2
    flow.begin(names[0], scatter_task([total[..., :quarter]], False, 0, [False]))
    flow.begin(names[1], scatter_task([total[..., quarter:]], True, 0, [False]))
    return None


def attention_scores(query_heads, key_heads, same_image):
    raw_scores = jnp.einsum(
        "qhd,khd->hqk", query_heads, key_heads, preferred_element_type=jnp.float32
    )
    return jnp.where(same_image[None], raw_scores * score_factor, -1e30)


def block_forward(entered, attend_low, expand_low, flow, gain_rows, same_image):
    halfway = entered.shape[0]
    normed, first_back = jax.vjp(layer_norm, entered, gain_rows[0], gain_rows[1])
    normed_low = to_low(normed)
    key_low = to_low(product(normed_low, attend_low[1]))
    value_low = to_low(product(normed_low, attend_low[2]))
    key_all = jnp.concatenate([key_low, swap_core(key_low)], axis=0)
    value_all = jnp.concatenate([value_low, swap_core(value_low)], axis=0)
    query_low = to_low(product(normed_low, attend_low[0]))
    query_heads = query_low.reshape(halfway, HEADS, HD)
    key_heads = key_all.reshape(SEQ, HEADS, HD)
    value_heads = value_all.reshape(SEQ, HEADS, HD)
    scores = attention_scores(query_heads, key_heads, same_image)
    highest = jnp.max(scores, axis=-1, keepdims=True)
    exponent_rows = jnp.exp(scores - highest)
    row_total = jnp.sum(exponent_rows, axis=-1, keepdims=True)
    log_total = highest + jnp.log(row_total)
    attended = to_low(
        jnp.einsum(
            "hqk,khd->qhd",
            to_low(exponent_rows / row_total),
            value_heads,
            preferred_element_type=jnp.float32,
        ).reshape(halfway, D)
    )
    middle = entered + product(attended, attend_low[3])
    normed_two, second_back = jax.vjp(layer_norm, middle, gain_rows[2], gain_rows[3])
    normed_two_low = to_low(normed_two)
    hidden, gelu_back = jax.vjp(jax.nn.gelu, product_right(normed_two_low, expand_low[0]))
    hidden_low = to_low(hidden)
    output_rows = middle + product(hidden_low, expand_low[1])
    kept = (
        first_back,
        normed_low,
        query_heads,
        key_heads,
        value_heads,
        log_total,
        attended,
        second_back,
        normed_two_low,
        gelu_back,
        hidden_low,
        expand_low,
    )
    return (output_rows, kept)


def block_backward(output_grad, kept, attend_low, flow, depth, same_image):
    (
        first_back,
        normed_low,
        query_heads,
        key_heads,
        value_heads,
        log_total,
        attended,
        second_back,
        normed_two_low,
        gelu_back,
        hidden_low,
        expand_low,
    ) = kept
    halfway = attended.shape[0]
    copies = expand_low[0].shape[0] // D
    upper_low = to_low(output_grad)
    flow.begin(
        "upper%d" % depth,
        weight_task([(copies, hidden_low, [upper_low])], False, 0),
    )
    (hidden_grad,) = gelu_back(product_right(upper_low, expand_low[1]))
    hidden_grad_low = flow.tick(to_low(hidden_grad))
    middle_extra, gain_three, gain_four = second_back(product(hidden_grad_low, expand_low[0]))
    middle_grad = flow.tick(output_grad + middle_extra)
    projected_low = to_low(middle_grad)
    flow.begin(
        "lower%d" % depth,
        weight_task(
            [(copies, hidden_grad_low, [normed_two_low]), (1, attended, [projected_low])],
            True,
            0,
        ),
    )
    attended_grad = to_low(product_right(projected_low, attend_low[3])).reshape(halfway, HEADS, HD)
    attended_grad = flow.tick(attended_grad)
    probability = jnp.exp(attention_scores(query_heads, key_heads, same_image) - log_total)
    soft_grad = jnp.einsum(
        "qhd,khd->hqk", attended_grad, value_heads, preferred_element_type=jnp.float32
    )
    value_part = jnp.einsum(
        "hqk,qhd->khd", to_low(probability), attended_grad, preferred_element_type=jnp.float32
    )
    score_low = to_low(
        probability
        * (soft_grad - jnp.sum(probability * soft_grad, axis=-1, keepdims=True))
        * score_factor
    )
    score_low, value_part = flow.tick(score_low, value_part)
    key_part = jnp.einsum(
        "hqk,qhd->khd", score_low, query_heads, preferred_element_type=jnp.float32
    )
    key_part = flow.tick(key_part)
    query_grad = to_low(
        jnp.einsum(
            "hqk,khd->qhd", score_low, key_heads, preferred_element_type=jnp.float32
        ).reshape(halfway, D)
    )
    key_part = key_part.reshape(SEQ, D)
    value_part = value_part.reshape(SEQ, D)
    value_grad = to_low(
        value_part[:halfway] + swap_core(to_low(value_part[halfway:])).astype(jnp.float32)
    )
    key_grad = to_low(
        key_part[:halfway] + swap_core(to_low(key_part[halfway:])).astype(jnp.float32)
    )
    query_grad, key_grad, value_grad = flow.tick(query_grad, key_grad, value_grad)
    flow.begin(
        "attend%d" % depth,
        weight_task([(1, normed_low, [query_grad, key_grad, value_grad])], False, 0, (), 1 + depth),
    )
    normed_grad = (
        product_right(query_grad, attend_low[0])
        + product_right(key_grad, attend_low[1])
        + product_right(value_grad, attend_low[2])
    )
    entered_extra, gain_one, gain_two = first_back(normed_grad)
    gain_delta = jnp.stack([gain_one, gain_two, gain_three, gain_four])
    return (flow.tick(middle_grad + entered_extra), gain_delta)


def newton_extra(gram_matrix):
    gram_low = to_low(gram_matrix)
    first_tail = newton_second * gram_matrix + newton_third * product(gram_low, gram_low)
    tail_low = to_low(first_tail)
    once = newton_first * gram_matrix + product(gram_low, tail_low)
    later = newton_first * once + product(to_low(once), tail_low)
    later_low = to_low(later)
    last_tail = newton_second * later + newton_third * product(later_low, later_low)
    return newton_first * (first_tail + last_tail) + product(tail_low, to_low(last_tail))


def padded(piece, rows, columns):
    lead = [(0, 0)] * (piece.ndim - 2)
    return jnp.pad(
        piece, (*lead, (0, rows - piece.shape[-2]), (0, columns - piece.shape[-1]))
    )


muon_counts = (2, 8, 8, 2, 1)


def first_owner():
    return lax.axis_size(("dp", "copy")) // 4


def owner_tables():
    matrices = [14, 14] + [8 + i // 2 for i in range(8)] + list(range(8)) + [12, 13, 15]
    shared = [1.0] * 10 + [0.0] * 11
    devices, start = (lax.axis_size(("dp", "copy")), first_owner())
    rest = devices - start - len(matrices)
    return (
        jnp.asarray([0] * start + matrices + [0] * rest, jnp.int32),
        jnp.asarray([0.0] * start + shared + [0.0] * rest, jnp.float32),
    )


def owner_buffer(modulate, expand, attend, dense, condition, rows, columns):
    devices, start = (lax.axis_size(("dp", "copy")), first_owner())
    groups = [jnp.zeros((start, rows, columns), jnp.bfloat16)]
    for given, count in zip((modulate, expand, attend, dense, condition), muon_counts):
        held = 0
        for member in given:
            if isinstance(member, int):
                groups.append(jnp.zeros((member, rows, columns), jnp.bfloat16))
                held += member
            else:
                groups.append(padded(to_low(member), rows, columns))
                held += member.shape[0]
        assert held == count
    groups.append(
        jnp.zeros((devices - start - sum(muon_counts), rows, columns), jnp.bfloat16)
    )
    return jnp.concatenate(groups, axis=0)


def two_parts(values):
    return values.reshape(-1, values.shape[-2] // 2, values.shape[-1])


def exchange_task(buffer, lag):
    (arrived,) = yield ([lax.all_to_all(buffer, ("dp", "copy"), 0, 0)], lag)
    return arrived


def muon_steps(moments, held, inverse):
    devices, highest, widest = held.shape
    held = held.reshape(devices * highest, widest)
    me = lax.axis_index(("dp", "copy"))
    matrix_here, shared_here = owner_tables()
    scale_here = inverse[matrix_here[me]]
    gram_matrix = product_left(held, held)
    gram_matrix = gram_matrix + shared_here[me] * swap_core(gram_matrix)
    extra = newton_extra(gram_matrix * (scale_here * scale_here))
    result = to_low(product(held, to_low(extra)) * scale_here)
    back = lax.all_to_all(result.reshape(devices, highest, widest), ("dp", "copy"), 0, 0)
    scaled = newton_first * newton_first * inverse
    found, start = ([], first_owner())
    shapes = [moments[i].shape for i in (3, 1, 0, 2, 4)]
    for shape, count in zip(shapes, muon_counts):
        part = back[start : start + count]
        rows = math.prod(shape[:-1]) // count
        found.append(part[:, :rows, : shape[-1]].reshape(shape).astype(jnp.float32))
        start += count
    modulate, expand, attend, dense, condition = found
    return (
        scaled[:8, None, None] * moments[0] + attend,
        scaled[8:12, None, None] * moments[1] + expand,
        scaled[12:14, None, None] * moments[2] + dense,
        scaled[14] * moments[3] + modulate,
        scaled[15] * moments[4] + condition,
    )


def adam_shard(master, first, second, gradient):
    first_new = beta_first * first + (1.0 - beta_first) * gradient
    second_new = beta_second * second + (1.0 - beta_second) * gradient * gradient
    corrected_first = first_new / (1.0 - beta_first**STEP)
    corrected_second = second_new / (1.0 - beta_second**STEP)
    master_new = master - adam_rate * (
        corrected_first / (jnp.sqrt(corrected_second) + adam_floor) + adam_decay * master
    )
    return (master_new, first_new, second_new)


def per_device(
    patches,
    noise_copies,
    image_ids,
    buffer_flags,
    loss_mask,
    timesteps,
    attend_weight,
    attend_velocity,
    expand_weight,
    expand_velocity,
    dense_weight,
    dense_velocity,
    modulate_weight,
    modulate_velocity,
    condition_weight,
    condition_velocity,
    encoder_table,
    encoder_first,
    encoder_second,
    head_table,
    head_first,
    head_second,
):
    everywhere = ("dp", "copy")
    core = lax.axis_index("copy")
    flow = Flow()
    attend_low, expand_low, dense_low = (
        to_low(attend_weight),
        to_low(expand_weight),
        to_low(dense_weight),
    )
    rows, wide = (attend_weight.shape[1], dense_weight.shape[1])
    table_slots = -(-encoder_table.shape[0] // D)
    encoder_turned = padded(to_low(encoder_table).T, rows, table_slots * D)
    encoder_turned = encoder_turned.reshape(rows, table_slots, D).transpose(1, 0, 2)
    expand_slots = expand_low.reshape(expand_low.shape[0], -1, rows, D)
    copies = expand_slots.shape[1]

    def gathered(members):
        return lax.all_gather(jnp.concatenate(members, axis=0), everywhere, axis=1, tiled=True)

    entry_part = gathered([attend_low[:4], encoder_turned])
    expand_part = gathered([expand_slots[0], expand_slots[1]])
    later_part = gathered([attend_low[4:], expand_slots[2], expand_slots[3]])
    modulate_rows = modulate_weight.shape[0]
    head_part = lax.all_gather(
        jnp.concatenate(
            [
                to_low(modulate_weight),
                dense_low[0],
                dense_low[1],
                padded(to_low(condition_weight), wide, HW),
                padded(to_low(head_table).T, wide, HW),
            ],
            axis=0,
        )[None],
        everywhere,
        axis=0,
        tiled=True,
    )

    def rows_of(start, count):
        return head_part[:, start : start + count].reshape(-1, HW)

    attend_all = [entry_part[:4], later_part[:4]]
    expand_all = [
        (
            member[: copies].reshape(copies * D, D),
            member[copies:].reshape(copies * D, D),
        )
        for member in (expand_part, later_part[4:])
    ]
    encoder_all = jnp.concatenate([entry_part[4 + i] for i in range(table_slots)], axis=1).T[
        : encoder_table.shape[0]
    ]
    modulate_all = rows_of(0, modulate_rows)
    dense_all = [rows_of(modulate_rows, wide), rows_of(modulate_rows + wide, wide)]
    condition_all = rows_of(modulate_rows + 2 * wide, wide)[:, :D]
    head_all = rows_of(modulate_rows + 3 * wide, wide)[:, : head_table.shape[0]].T
    halfway = SEQ // 2
    offset = core * halfway

    def own_first(values):
        return jnp.where(
            core == 0, values, jnp.concatenate([values[halfway:], values[:halfway]], axis=0)
        )

    patch_seq = own_first(patches[0])
    image_row = own_first(image_ids[0])
    buffer_row = own_first(buffer_flags[0])
    masked_row = own_first(loss_mask[0])
    weight_row = (masked_row * (1 - buffer_row)).astype(jnp.float32)
    token_count = sum_all(jnp.sum(weight_row))
    own_patch = patch_seq[:halfway]
    buffer_on = buffer_row[:halfway, None] > 0
    masked_on = masked_row[:halfway, None] > 0
    same_image = image_row[:halfway, None] == image_row[None, :]
    gain_rows = encoder_all[:12].astype(jnp.float32)
    position = lax.dynamic_slice_in_dim(encoder_all, 12 + PATCH + offset, halfway, 0).astype(
        jnp.float32
    )
    embedded = product(own_patch, encoder_all[12 : 12 + PATCH])

    def entry(embedded_rows, token_pair, position_rows):
        return (
            jnp.where(buffer_on, token_pair[1], jnp.where(masked_on, token_pair[0], embedded_rows))
            + position_rows
        )

    entered, entry_back = jax.vjp(entry, embedded, gain_rows[10:12], position)
    state_rows = entered
    kept_all = []
    for depth_index in range(2):
        state_rows, kept = block_forward(
            state_rows,
            attend_all[depth_index],
            expand_all[depth_index],
            flow,
            gain_rows[4 * depth_index : 4 * depth_index + 4],
            same_image,
        )
        kept_all.append(kept)
    latent, third_back = jax.vjp(layer_norm, state_rows, gain_rows[8], gain_rows[9])
    latent_low = to_low(latent)
    condition_own = to_low(product_right(latent_low, condition_all))
    condition_rows = jnp.concatenate([condition_own, swap_core(condition_own)], axis=0)
    highest = max(
        modulate_weight.shape[0] // 2,
        expand_weight.shape[1] // 2,
        attend_weight.shape[1],
        dense_weight.shape[1],
        condition_weight.shape[0],
    )
    condition_rows, velocity_buffer = lax.optimization_barrier(
        (
            condition_rows,
            owner_buffer(
                [two_parts(modulate_velocity)],
                [two_parts(expand_velocity)],
                [attend_velocity],
                [dense_velocity],
                [condition_velocity[None]],
                highest,
                HW,
            ),
        )
    )
    flow.begin("velocity", exchange_task(velocity_buffer, 2))
    step_float = own_first(timesteps[0, 0]).astype(jnp.float32)
    alpha_row = alpha_bar(step_float)[:, None]
    target = own_first(noise_copies[0, 0]).astype(jnp.float32)
    noisy_low = to_low(
        jnp.sqrt(alpha_row) * patch_seq.astype(jnp.float32) + jnp.sqrt(1.0 - alpha_row) * target
    )
    lifted = product(noisy_low, head_all[:PATCH])
    feature_low = to_low(time_features(step_float))
    summed = condition_rows.astype(jnp.float32) + product(
        feature_low, head_all[PATCH : PATCH + FREQ]
    )
    activated, silu_back = jax.vjp(jax.nn.silu, summed)
    activated_low = to_low(activated)
    modulation = product_right(activated_low, modulate_all)
    inner_rows, inner_back = jax.vjp(first_modulate, lifted, modulation)
    inner_low = to_low(inner_rows)
    expanded, dense_back = jax.vjp(jax.nn.gelu, product(inner_low, dense_all[0]))
    expanded_low = to_low(expanded)
    branch = product(expanded_low, dense_all[1])
    outer_rows, outer_back = jax.vjp(last_modulate, lifted, modulation, branch)
    outer_low = to_low(outer_rows)
    predicted = product_right(outer_low, head_all[PATCH + FREQ :])
    residue = predicted - target
    loss_local = jnp.sum(weight_row[:, None] * residue * residue) / PATCH
    predicted_grad = to_low(2.0 * weight_row[:, None] * residue / (PATCH * token_count))
    final_turned = product_left(outer_low, predicted_grad)
    lifted_grad, modulation_grad, branch_grad = outer_back(
        product(predicted_grad, head_all[PATCH + FREQ :])
    )
    branch_low = to_low(branch_grad)
    (expanded_grad,) = dense_back(product_right(branch_low, dense_all[1]))
    expanded_grad_low = to_low(expanded_grad)
    lifted_extra, modulation_extra = inner_back(product_right(expanded_grad_low, dense_all[0]))
    modulation_low = flow.tick(to_low(modulation_grad + modulation_extra))
    flow.begin(
        "spread",
        split_weight_task(modulation_low, activated_low, flow, ("modulate.2", "modulate.3")),
    )
    (summed_grad,) = silu_back(product(modulation_low, modulate_all))
    time_turned = product_left(to_low(summed_grad), feature_low)
    lift_turned = product_left(to_low(lifted_grad + lifted_extra), noisy_low)
    head_turned_grad = jnp.concatenate([lift_turned, time_turned, final_turned], axis=1)
    condition_grad = to_low(
        summed_grad[:halfway] + swap_core(to_low(summed_grad[halfway:])).astype(jnp.float32)
    )
    condition_grad = flow.tick(condition_grad)
    flow.begin(
        "head",
        weight_task(
            [
                (1, inner_low, [expanded_grad_low]),
                (1, expanded_low, [branch_low]),
                (1, condition_grad, [latent_low]),
            ],
            True,
            -1,
            [head_turned_grad],
        ),
    )
    state_grad, gain_nine, gain_ten = third_back(product(condition_grad, condition_all))

    def modulate_whole():
        (left_parts,), (right_parts,) = (flow.results["modulate.2"], flow.results["modulate.3"])
        quarters = [left_parts[0], right_parts[0], left_parts[1], right_parts[1]]
        return jnp.concatenate(quarters, axis=-1)[0]

    def attend_whole(depth):
        lower = flow.results["lower%d" % depth]
        return jnp.concatenate([*flow.results["attend%d" % depth], lower[1]], axis=0)

    def expand_whole(depth):
        lower, upper = (flow.results["lower%d" % depth], flow.results["upper%d" % depth])
        return jnp.stack([lower[0].reshape(-1, D), upper[0].reshape(-1, D)])

    def dense_whole():
        return jnp.concatenate(flow.results["head"][:2], axis=0)

    flow.when(
        ["head", "modulate.2", "modulate.3", "upper1", "lower1", "attend1"],
        "early",
        lambda: exchange_task(
            owner_buffer(
                [two_parts(modulate_whole())],
                [4, two_parts(expand_whole(1))],
                [4, attend_whole(1)],
                [dense_whole()],
                [flow.results["head"][2]],
                highest,
                HW,
            ),
            4,
        ),
    )
    gain_parts = [None, None]
    for depth_index in (1, 0):
        state_grad, gain_parts[depth_index] = block_backward(
            state_grad,
            kept_all[depth_index],
            attend_all[depth_index],
            flow,
            depth_index,
            same_image,
        )
    embedded_grad, token_grad, position_grad = entry_back(state_grad)
    embed_delta = product_left(own_patch, to_low(embedded_grad))
    small_delta = jnp.concatenate(
        [
            gain_parts[0],
            gain_parts[1],
            jnp.stack([gain_nine, gain_ten]),
            token_grad,
            embed_delta,
        ],
        axis=0,
    )
    small_delta = small_delta + swap_core(small_delta)
    small_half = small_delta.shape[0] // 2
    encoder_half = jnp.concatenate(
        [position_grad, lax.dynamic_slice_in_dim(small_delta, core * small_half, small_half, 0)],
        axis=0,
    ).T
    flow.begin("encoder", scatter_task([encoder_half[None]], True, 0, [True], 1))
    encoder_first_half, encoder_last_half = (m[0] for m in flow.take("encoder")[0][0])
    encoder_delta = jnp.concatenate(
        [
            encoder_first_half[:, halfway:],
            encoder_last_half[:, halfway:],
            encoder_first_half[:, :halfway],
            encoder_last_half[:, :halfway],
        ],
        axis=1,
    ).T
    flow.take("upper0", "lower0", "attend0")
    late_rows = max(expand_weight.shape[1] // 2, attend_weight.shape[1])
    late = lax.all_to_all(
        owner_buffer(
            [2], [two_parts(expand_whole(0)), 4], [attend_whole(0), 4], [2], [1], late_rows, D
        ),
        everywhere,
        0,
        0,
    )
    reduced = (
        jnp.concatenate([attend_whole(0), attend_whole(1)], axis=0),
        jnp.concatenate([expand_whole(0), expand_whole(1)], axis=0),
        dense_whole(),
        modulate_whole(),
        flow.results["head"][2][0],
        encoder_delta,
        flow.results["head"][3][0].T,
    )
    velocities = (
        attend_velocity,
        expand_velocity,
        dense_velocity,
        modulate_velocity,
        condition_velocity,
    )

    def pairs_of(left, right):
        return jnp.concatenate(
            [
                jnp.sum((left[i] * right[i]).reshape(-1, *left[i].shape[-2:]), axis=(1, 2))
                for i in range(5)
            ]
        )

    table_squares = sum(jnp.sum(member * member) for member in reduced[5:])
    totals = sum_all(
        jnp.concatenate(
            [
                pairs_of(reduced, reduced),
                pairs_of(velocities, reduced),
                pairs_of(velocities, velocities),
                jnp.stack([table_squares, loss_local]),
            ]
        )
    )
    loss_sum = totals[49]
    clip_norm = jnp.sqrt(jnp.sum(totals[:16]) + totals[48])
    factor = jnp.minimum(1.0, clip_bound / (clip_norm + 1e-06))
    moment_squares = (
        factor * factor * totals[:16]
        + 2.0 * muon_keep * factor * totals[16:32]
        + muon_keep * muon_keep * totals[32:48]
    )
    inverse = 1.0 / (jnp.sqrt(jnp.maximum(moment_squares, 0.0)) + 1e-07)
    moments = tuple((muon_keep * velocities[i] + factor * reduced[i] for i in range(5)))
    early, velocity_held = flow.take("early", "velocity")
    held = to_low(
        muon_keep * velocity_held.astype(jnp.float32)
        + factor
        * (early.astype(jnp.float32) + padded(late, highest, HW).astype(jnp.float32))
    )
    current = muon_steps(moments, held, inverse)
    devices = lax.axis_size(everywhere)
    masters = (attend_weight, expand_weight, dense_weight, modulate_weight, condition_weight)
    updated = tuple(
        (
            masters[i] * (1.0 - muon_rate * muon_decay)
            - muon_rate
            * max(1.0, current[i].shape[-2] * devices / current[i].shape[-1]) ** 0.5
            * current[i]
            for i in range(5)
        )
    )
    encoder_master, encoder_firsts, encoder_seconds = adam_shard(
        encoder_table, encoder_first, encoder_second, factor * reduced[5]
    )
    table_master, table_firsts, table_seconds = adam_shard(
        head_table, head_first, head_second, factor * reduced[6]
    )
    return (
        loss_sum,
        token_count,
        clip_norm,
        updated[0],
        moments[0],
        updated[1],
        moments[1],
        updated[2],
        moments[2],
        updated[3],
        moments[3],
        updated[4],
        moments[4],
        encoder_master,
        encoder_firsts,
        encoder_seconds,
        table_master,
        table_firsts,
        table_seconds,
    )


def solution(mesh):
    placed = (
        P("dp", None, None),
        P("copy", "dp", None, None),
        P("dp", None),
        P("dp", None),
        P("dp", None),
        P("copy", "dp", None),
        P(None, ("dp", "copy"), None),
        P(None, ("dp", "copy"), None),
        P(None, ("dp", "copy"), None),
        P(None, ("dp", "copy"), None),
        P(None, ("dp", "copy"), None),
        P(None, ("dp", "copy"), None),
        P(("dp", "copy"), None),
        P(("dp", "copy"), None),
        P(("dp", "copy"), None),
        P(("dp", "copy"), None),
        P(None, ("dp", "copy")),
        P(None, ("dp", "copy")),
        P(None, ("dp", "copy")),
        P(None, ("dp", "copy")),
        P(None, ("dp", "copy")),
        P(None, ("dp", "copy")),
    )
    return jax.shard_map(
        per_device,
        mesh=mesh,
        in_specs=placed,
        out_specs=(
            P(),
            P(),
            P(),
            P(None, ("dp", "copy"), None),
            P(None, ("dp", "copy"), None),
            P(None, ("dp", "copy"), None),
            P(None, ("dp", "copy"), None),
            P(None, ("dp", "copy"), None),
            P(None, ("dp", "copy"), None),
            P(("dp", "copy"), None),
            P(("dp", "copy"), None),
            P(("dp", "copy"), None),
            P(("dp", "copy"), None),
            P(None, ("dp", "copy")),
            P(None, ("dp", "copy")),
            P(None, ("dp", "copy")),
            P(None, ("dp", "copy")),
            P(None, ("dp", "copy")),
            P(None, ("dp", "copy")),
        ),
        check_vma=False,
    )
```

```python
import math

import jax
import jax.numpy as jnp
from jax import lax
from jax.sharding import PartitionSpec as P

D = 768
HEADS = 12
HD = 64
HW = 1024
PATCH = 64
FREQ = 256
SEQ = 1024
NS_STEPS = 2
STEP = 10
TSTEPS = 1000


precise_mode = lax.Precision.HIGHEST
norm_floor = 1e-06
score_factor = 0.125
newton_first = 3.4445
newton_second = -4.775
newton_third = 2.0315
muon_rate = 1.0
muon_decay = 0.01
muon_keep = 0.95
clip_bound = 0.001
adam_rate = 0.02
beta_first = 0.9
beta_second = 0.95
adam_floor = 1e-08
adam_decay = 0.1


def product(left_side, right_side):
    return jnp.dot(left_side, right_side, preferred_element_type=jnp.float32)


def product_left(left_side, right_side):
    return lax.dot_general(
        left_side, right_side, (((0,), (0,)), ((), ())), preferred_element_type=jnp.float32
    )


def product_right(left_side, right_side):
    return lax.dot_general(
        left_side, right_side, (((1,), (1,)), ((), ())), preferred_element_type=jnp.float32
    )


def to_low(values):
    return values.astype(jnp.bfloat16)


def layer_norm(values, gain_row, bias_row):
    centered = values - jnp.mean(values, axis=-1, keepdims=True)
    spread = jnp.mean(centered * centered, axis=-1, keepdims=True)
    return centered * lax.rsqrt(spread + norm_floor) * gain_row + bias_row


def plain_norm(values):
    centered = values - jnp.mean(values, axis=-1, keepdims=True)
    spread = jnp.mean(centered * centered, axis=-1, keepdims=True)
    return centered * lax.rsqrt(spread + norm_floor)


def alpha_bar(step_float):
    return jnp.cos(0.5 * math.pi * (step_float + 0.5) / TSTEPS) ** 2


def time_features(step_float):
    halfway = FREQ // 2
    frequency = jnp.exp(-math.log(10000.0) * jnp.arange(halfway).astype(jnp.float32) / halfway)
    angles = step_float[:, None] * frequency[None, :]
    return jnp.concatenate([jnp.cos(angles), jnp.sin(angles)], axis=1)


def first_modulate(lifted, modulation):
    return plain_norm(lifted) * (1.0 + modulation[:, HW : 2 * HW]) + modulation[:, :HW]


def last_modulate(lifted, modulation, branch):
    joined = lifted + modulation[:, 2 * HW : 3 * HW] * branch
    return plain_norm(joined) * (1.0 + modulation[:, 4 * HW :]) + modulation[:, 3 * HW : 4 * HW]


def grid_of(count):
    side = 1
    while 2 * side**3 < count:
        side *= 2
    if 2 * side**3 == count:
        return (2 * side, side, side)
    return (count, 1, 1)


def swap_core(values):
    return lax.ppermute(values, "copy", [(0, 1), (1, 0)])


def sum_all(values):
    values = values + swap_core(values)
    count = lax.axis_size("dp")
    if count & (count - 1):
        return lax.psum(values, "dp")
    step = 1
    while step < count:
        values = values + lax.ppermute(values, "dp", [(i, i ^ step) for i in range(count)])
        step *= 2
    return values


class Flow:
    def __init__(self):
        self.live, self.results = ([], {})

    def begin(self, name, task):
        self.live.append([name, task, *next(task)])

    def tick(self, *carry):
        due = [entry for entry in self.live if entry[3] <= 1]
        for entry in self.live:
            entry[3] -= 1
        carry, arrived = lax.optimization_barrier((carry, [entry[2] for entry in due]))
        for entry, values in zip(due, arrived):
            try:
                entry[2], entry[3] = entry[1].send(values)
            except StopIteration as stop:
                self.results[entry[0]] = stop.value
                self.live.remove(entry)
        return carry if len(carry) > 1 else (carry[0] if carry else None)

    def take(self, *names):
        while any(name not in self.results for name in names):
            self.tick()
        return [self.results[name] for name in names]


def columns_of(values, core):
    half = values.shape[-1] // 2
    return lax.dynamic_slice_in_dim(values, core * half, half, values.ndim - 1)


def joined(parts, axis):
    return parts[0] if len(parts) == 1 else jnp.concatenate(parts, axis=axis)


def bits_in_order(crossed):
    grid = grid_of(lax.axis_size("dp"))
    counts = [size.bit_length() - 1 for size in grid]
    z_bits = list(range(counts[2] + counts[1], sum(counts)))
    y_bits = list(range(counts[2], counts[2] + counts[1]))
    x_bits = list(range(counts[2]))
    return (y_bits + x_bits if crossed else x_bits + y_bits) + z_bits


def scatter_task(parts, crossed, axis, exact, lag=2):
    core = lax.axis_index("copy")
    here = lax.axis_index("dp")
    chips = lax.axis_size("dp")
    sizes = [part.shape[axis] for part in parts]
    order = bits_in_order(crossed)
    parts = [
        part.reshape(
            part.shape[0], *[2] * len(order), part.shape[1] // chips, part.shape[2]
        )
        for part in parts
    ]
    left = sorted(order, reverse=True)
    for bit in order:
        position, mine = (1 + left.index(bit), here // 2**bit % 2)
        sent = []
        for part, keep in zip(parts, exact):
            half = lax.dynamic_index_in_dim(part, 1 - mine, position, keepdims=False)
            if keep:
                near = lax.reduce_precision(half, 8, 7)
                sent += [to_low(near), to_low(half - near)]
            else:
                sent.append(to_low(half))
        pairs = [(i, i ^ 2**bit) for i in range(chips)]
        (arrived,) = yield ([lax.ppermute(joined(sent, axis), "dp", pairs)], lag)
        start, totals = (0, [])
        for part, keep, size in zip(parts, exact, sizes):
            total = lax.dynamic_index_in_dim(part, mine, position, keepdims=False)
            for number in range(2 if keep else 1):
                piece = lax.slice_in_dim(
                    arrived, start, start + size, axis=axis % arrived.ndim
                )
                total = total + piece.astype(jnp.float32)
                start += size
            totals.append(total)
        parts = totals
        left.remove(bit)
    values = joined(parts, axis)
    half = values.shape[1] // 2
    mine = lax.dynamic_slice_in_dim(values, core * half, half, 1)
    (arrived,) = yield (
        [swap_core(lax.dynamic_slice_in_dim(values, (1 - core) * half, half, 1))],
        1,
    )
    first = jnp.where(core == 0, mine, arrived)
    last = jnp.where(core == 0, arrived, mine)
    starts = [sum(sizes[:i]) for i in range(len(sizes))]
    return [
        tuple(lax.slice_in_dim(m, start, start + size, axis=axis % m.ndim) for m in (first, last))
        for start, size in zip(starts, sizes)
    ]


def weight_task(products, crossed, axis, tables=(), lag=2):
    core = lax.axis_index("copy")

    def some(right_sides, which):
        return joined([columns_of(right, which) for right in right_sides], 1)

    sent = [product_left(left, some(rights, 1 - core)) for slots, left, rights in products]
    sent += [columns_of(table, 1 - core) for table in tables]
    arrived = yield ([swap_core(part) for part in sent], 1)
    totals = [
        product_left(left, some(rights, core)) + part
        for (slots, left, rights), part in zip(products, arrived)
    ]
    totals = [
        total.reshape(member[0], total.shape[0] // member[0], total.shape[1])
        for total, member in zip(totals, products)
    ]
    for table, part in zip(tables, arrived[len(products) :]):
        totals.append((columns_of(table, core) + part)[None])
    exact = [False] * len(products) + [True] * len(tables)
    halves = yield from scatter_task(totals, crossed, axis, exact, lag)
    found = []
    counts = [len(member[2]) for member in products] + [1] * len(tables)
    for (first, last), count in zip(halves, counts):
        width = first.shape[-1] // count
        for i in range(count):
            pair = [m[..., i * width : (i + 1) * width] for m in (first, last)]
            found.append(jnp.concatenate(pair, axis=-1))
    return found


def split_weight_task(left_side, right_side, flow, names):
    core = lax.axis_index("copy")
    (arrived,) = yield ([swap_core(product_left(left_side, columns_of(right_side, 1 - core)))], 1)
    total = (product_left(left_side, columns_of(right_side, core)) + arrived)[None]
    quarter = total.shape[-1] // 2
    flow.begin(names[0], scatter_task([total[..., :quarter]], False, 0, [False]))
    flow.begin(names[1], scatter_task([total[..., quarter:]], True, 0, [False]))
    return None


def attention_scores(query_heads, key_heads, same_image):
    raw_scores = jnp.einsum(
        "qhd,khd->hqk", query_heads, key_heads, preferred_element_type=jnp.float32
    )
    return jnp.where(same_image[None], raw_scores * score_factor, -1e30)


def block_forward(entered, attend_low, expand_low, flow, gain_rows, same_image):
    halfway = entered.shape[0]
    normed, first_back = jax.vjp(layer_norm, entered, gain_rows[0], gain_rows[1])
    normed_low = to_low(normed)
    key_low = to_low(product(normed_low, attend_low[1]))
    value_low = to_low(product(normed_low, attend_low[2]))
    key_all = jnp.concatenate([key_low, swap_core(key_low)], axis=0)
    value_all = jnp.concatenate([value_low, swap_core(value_low)], axis=0)
    query_low = to_low(product(normed_low, attend_low[0]))
    query_heads = query_low.reshape(halfway, HEADS, HD)
    key_heads = key_all.reshape(SEQ, HEADS, HD)
    value_heads = value_all.reshape(SEQ, HEADS, HD)
    scores = attention_scores(query_heads, key_heads, same_image)
    highest = jnp.max(scores, axis=-1, keepdims=True)
    exponent_rows = jnp.exp(scores - highest)
    row_total = jnp.sum(exponent_rows, axis=-1, keepdims=True)
    log_total = highest + jnp.log(row_total)
    attended = to_low(
        jnp.einsum(
            "hqk,khd->qhd",
            to_low(exponent_rows / row_total),
            value_heads,
            preferred_element_type=jnp.float32,
        ).reshape(halfway, D)
    )
    middle = entered + product(attended, attend_low[3])
    normed_two, second_back = jax.vjp(layer_norm, middle, gain_rows[2], gain_rows[3])
    normed_two_low = to_low(normed_two)
    hidden, gelu_back = jax.vjp(jax.nn.gelu, product_right(normed_two_low, expand_low[0]))
    hidden_low = to_low(hidden)
    output_rows = middle + product(hidden_low, expand_low[1])
    kept = (
        first_back,
        normed_low,
        query_heads,
        key_heads,
        value_heads,
        log_total,
        attended,
        second_back,
        normed_two_low,
        gelu_back,
        hidden_low,
        expand_low,
    )
    return (output_rows, kept)


def block_backward(output_grad, kept, attend_low, flow, depth, same_image):
    (
        first_back,
        normed_low,
        query_heads,
        key_heads,
        value_heads,
        log_total,
        attended,
        second_back,
        normed_two_low,
        gelu_back,
        hidden_low,
        expand_low,
    ) = kept
    halfway = attended.shape[0]
    copies = expand_low[0].shape[0] // D
    upper_low = to_low(output_grad)
    flow.begin(
        "upper%d" % depth,
        weight_task([(copies, hidden_low, [upper_low])], False, 0),
    )
    (hidden_grad,) = gelu_back(product_right(upper_low, expand_low[1]))
    hidden_grad_low = flow.tick(to_low(hidden_grad))
    middle_extra, gain_three, gain_four = second_back(product(hidden_grad_low, expand_low[0]))
    middle_grad = flow.tick(output_grad + middle_extra)
    projected_low = to_low(middle_grad)
    flow.begin(
        "lower%d" % depth,
        weight_task(
            [(copies, hidden_grad_low, [normed_two_low]), (1, attended, [projected_low])],
            True,
            0,
        ),
    )
    attended_grad = to_low(product_right(projected_low, attend_low[3])).reshape(halfway, HEADS, HD)
    attended_grad = flow.tick(attended_grad)
    probability = jnp.exp(attention_scores(query_heads, key_heads, same_image) - log_total)
    soft_grad = jnp.einsum(
        "qhd,khd->hqk", attended_grad, value_heads, preferred_element_type=jnp.float32
    )
    value_part = jnp.einsum(
        "hqk,qhd->khd", to_low(probability), attended_grad, preferred_element_type=jnp.float32
    )
    score_low = to_low(
        probability
        * (soft_grad - jnp.sum(probability * soft_grad, axis=-1, keepdims=True))
        * score_factor
    )
    score_low, value_part = flow.tick(score_low, value_part)
    key_part = jnp.einsum(
        "hqk,qhd->khd", score_low, query_heads, preferred_element_type=jnp.float32
    )
    key_part = flow.tick(key_part)
    query_grad = to_low(
        jnp.einsum(
            "hqk,khd->qhd", score_low, key_heads, preferred_element_type=jnp.float32
        ).reshape(halfway, D)
    )
    key_part = key_part.reshape(SEQ, D)
    value_part = value_part.reshape(SEQ, D)
    value_grad = to_low(
        value_part[:halfway] + swap_core(to_low(value_part[halfway:])).astype(jnp.float32)
    )
    key_grad = to_low(
        key_part[:halfway] + swap_core(to_low(key_part[halfway:])).astype(jnp.float32)
    )
    query_grad, key_grad, value_grad = flow.tick(query_grad, key_grad, value_grad)
    flow.begin(
        "attend%d" % depth,
        weight_task([(1, normed_low, [query_grad, key_grad, value_grad])], False, 0, (), 1 + depth),
    )
    normed_grad = (
        product_right(query_grad, attend_low[0])
        + product_right(key_grad, attend_low[1])
        + product_right(value_grad, attend_low[2])
    )
    entered_extra, gain_one, gain_two = first_back(normed_grad)
    gain_delta = jnp.stack([gain_one, gain_two, gain_three, gain_four])
    return (flow.tick(middle_grad + entered_extra), gain_delta)


def newton_extra(gram_matrix):
    gram_low = to_low(gram_matrix)
    first_tail = newton_second * gram_matrix + newton_third * product(gram_low, gram_low)
    tail_low = to_low(first_tail)
    once = newton_first * gram_matrix + product(gram_low, tail_low)
    later = newton_first * once + product(to_low(once), tail_low)
    later_low = to_low(later)
    last_tail = newton_second * later + newton_third * product(later_low, later_low)
    return newton_first * (first_tail + last_tail) + product(tail_low, to_low(last_tail))


def padded(piece, rows, columns):
    lead = [(0, 0)] * (piece.ndim - 2)
    return jnp.pad(
        piece, (*lead, (0, rows - piece.shape[-2]), (0, columns - piece.shape[-1]))
    )


muon_counts = (4, 8, 8, 2, 1)


def first_owner():
    return lax.axis_size(("dp", "copy")) // 4


def owner_tables():
    devices, start = (lax.axis_size(("dp", "copy")), first_owner())

    def table(values, kind):
        return jnp.asarray([0] * start + values + [0] * (devices - start - len(values)), kind)

    return (
        table([1] * 12 + [0] * 11, jnp.float32),
        table([1] * 4 + [0] * 19, jnp.float32),
    )


def owner_buffer(modulate, expand, attend, dense, condition, rows, columns):
    devices, start = (lax.axis_size(("dp", "copy")), first_owner())
    groups = [jnp.zeros((start, rows, columns), jnp.bfloat16)]
    for given, count in zip((modulate, expand, attend, dense, condition), muon_counts):
        held = 0
        for member in given:
            if isinstance(member, int):
                groups.append(jnp.zeros((member, rows, columns), jnp.bfloat16))
                held += member
            else:
                groups.append(padded(to_low(member), rows, columns))
                held += member.shape[0]
        assert held == count
    groups.append(
        jnp.zeros((devices - start - sum(muon_counts), rows, columns), jnp.bfloat16)
    )
    return jnp.concatenate(groups, axis=0)


def in_parts(values, count):
    return values.reshape(-1, values.shape[-2] // count, values.shape[-1])


def muon_steps(moments):
    attend, expand, dense, modulate, condition = moments
    highest = max(
        modulate.shape[0] // 4,
        expand.shape[1] // 2,
        attend.shape[1],
        dense.shape[1],
        condition.shape[0],
    )
    held = lax.all_to_all(
        owner_buffer(
            [in_parts(modulate, 4)],
            [in_parts(expand, 2)],
            [attend],
            [dense],
            [condition[None]],
            highest,
            HW,
        ),
        ("dp", "copy"),
        0,
        0,
    )
    devices = held.shape[0]
    held = held.reshape(devices * highest, HW)
    core, me = (lax.axis_index("copy"), lax.axis_index(("dp", "copy")))
    shared_here, crossed_here = owner_tables()
    gram_matrix = product_left(held, held)
    gram_matrix = gram_matrix + shared_here[me] * swap_core(gram_matrix)
    chips = [(i, i ^ 1) for i in range(lax.axis_size("dp"))]
    near = lax.ppermute(to_low(columns_of(gram_matrix, core)), "dp", chips)
    far = swap_core(near)
    crossed = jnp.concatenate(
        [jnp.where(core == 0, near, far), jnp.where(core == 0, far, near)], axis=1
    )
    gram_matrix = gram_matrix + crossed_here[me] * crossed.astype(jnp.float32)
    rows = lax.broadcasted_iota(jnp.int32, gram_matrix.shape, 0)
    columns = lax.broadcasted_iota(jnp.int32, gram_matrix.shape, 1)
    trace = jnp.sum(jnp.where(rows == columns, gram_matrix, 0.0))
    scale_here = 1.0 / (jnp.sqrt(trace) + 1e-07)
    extra = newton_extra(gram_matrix * (scale_here * scale_here))
    result = to_low(product(held, to_low(extra)) * scale_here)
    back = lax.all_to_all(result.reshape(devices, highest, HW), ("dp", "copy"), 0, 0)
    squares = [
        jnp.sum((member * member).reshape(-1, *member.shape[-2:]), axis=(1, 2))
        for member in moments
    ]
    inverse = 1.0 / (jnp.sqrt(sum_all(jnp.concatenate(squares))) + 1e-07)
    scaled = newton_first * newton_first * inverse
    found, start = ([], first_owner())
    shapes = [moments[i].shape for i in (3, 1, 0, 2, 4)]
    for shape, count in zip(shapes, muon_counts):
        part = back[start : start + count]
        rows = math.prod(shape[:-1]) // count
        found.append(part[:, :rows, : shape[-1]].reshape(shape).astype(jnp.float32))
        start += count
    modulate, expand, attend, dense, condition = found
    return (
        scaled[:8, None, None] * moments[0] + attend,
        scaled[8:12, None, None] * moments[1] + expand,
        scaled[12:14, None, None] * moments[2] + dense,
        scaled[14] * moments[3] + modulate,
        scaled[15] * moments[4] + condition,
    )


def adam_shard(master, first, second, gradient):
    first_new = beta_first * first + (1.0 - beta_first) * gradient
    second_new = beta_second * second + (1.0 - beta_second) * gradient * gradient
    corrected_first = first_new / (1.0 - beta_first**STEP)
    corrected_second = second_new / (1.0 - beta_second**STEP)
    master_new = master - adam_rate * (
        corrected_first / (jnp.sqrt(corrected_second) + adam_floor) + adam_decay * master
    )
    return (master_new, first_new, second_new)


def per_device(
    patches,
    noise_copies,
    image_ids,
    buffer_flags,
    loss_mask,
    timesteps,
    attend_weight,
    attend_velocity,
    expand_weight,
    expand_velocity,
    dense_weight,
    dense_velocity,
    modulate_weight,
    modulate_velocity,
    condition_weight,
    condition_velocity,
    encoder_table,
    encoder_first,
    encoder_second,
    head_table,
    head_first,
    head_second,
):
    everywhere = ("dp", "copy")
    core = lax.axis_index("copy")
    flow = Flow()
    attend_low, expand_low, dense_low = (
        to_low(attend_weight),
        to_low(expand_weight),
        to_low(dense_weight),
    )
    rows, wide = (attend_weight.shape[1], dense_weight.shape[1])
    table_slots = -(-encoder_table.shape[0] // D)
    encoder_turned = padded(to_low(encoder_table).T, rows, table_slots * D)
    encoder_turned = encoder_turned.reshape(rows, table_slots, D).transpose(1, 0, 2)
    expand_slots = expand_low.reshape(expand_low.shape[0], -1, rows, D)
    copies = expand_slots.shape[1]

    def gathered(members):
        return lax.all_gather(jnp.concatenate(members, axis=0), everywhere, axis=1, tiled=True)

    entry_part = gathered([attend_low[:4], encoder_turned])
    expand_part = gathered([expand_slots[0], expand_slots[1]])
    later_part = gathered([attend_low[4:], expand_slots[2], expand_slots[3]])
    modulate_rows = modulate_weight.shape[0]
    head_part = lax.all_gather(
        jnp.concatenate(
            [
                to_low(modulate_weight),
                dense_low[0],
                dense_low[1],
                padded(to_low(condition_weight), wide, HW),
                padded(to_low(head_table).T, wide, HW),
            ],
            axis=0,
        )[None],
        everywhere,
        axis=0,
        tiled=True,
    )

    def rows_of(start, count):
        return head_part[:, start : start + count].reshape(-1, HW)

    attend_all = [entry_part[:4], later_part[:4]]
    expand_all = [
        (
            member[: copies].reshape(copies * D, D),
            member[copies:].reshape(copies * D, D),
        )
        for member in (expand_part, later_part[4:])
    ]
    encoder_all = jnp.concatenate([entry_part[4 + i] for i in range(table_slots)], axis=1).T[
        : encoder_table.shape[0]
    ]
    modulate_all = rows_of(0, modulate_rows)
    dense_all = [rows_of(modulate_rows, wide), rows_of(modulate_rows + wide, wide)]
    condition_all = rows_of(modulate_rows + 2 * wide, wide)[:, :D]
    head_all = rows_of(modulate_rows + 3 * wide, wide)[:, : head_table.shape[0]].T
    halfway = SEQ // 2
    offset = core * halfway

    def own_first(values):
        return jnp.where(
            core == 0, values, jnp.concatenate([values[halfway:], values[:halfway]], axis=0)
        )

    patch_seq = own_first(patches[0])
    image_row = own_first(image_ids[0])
    buffer_row = own_first(buffer_flags[0])
    masked_row = own_first(loss_mask[0])
    weight_row = (masked_row * (1 - buffer_row)).astype(jnp.float32)
    token_count = sum_all(jnp.sum(weight_row))
    own_patch = patch_seq[:halfway]
    buffer_on = buffer_row[:halfway, None] > 0
    masked_on = masked_row[:halfway, None] > 0
    same_image = image_row[:halfway, None] == image_row[None, :]
    gain_rows = encoder_all[:12].astype(jnp.float32)
    position = lax.dynamic_slice_in_dim(encoder_all, 12 + PATCH + offset, halfway, 0).astype(
        jnp.float32
    )
    embedded = product(own_patch, encoder_all[12 : 12 + PATCH])

    def entry(embedded_rows, token_pair, position_rows):
        return (
            jnp.where(buffer_on, token_pair[1], jnp.where(masked_on, token_pair[0], embedded_rows))
            + position_rows
        )

    entered, entry_back = jax.vjp(entry, embedded, gain_rows[10:12], position)
    state_rows = entered
    kept_all = []
    for depth_index in range(2):
        state_rows, kept = block_forward(
            state_rows,
            attend_all[depth_index],
            expand_all[depth_index],
            flow,
            gain_rows[4 * depth_index : 4 * depth_index + 4],
            same_image,
        )
        kept_all.append(kept)
    latent, third_back = jax.vjp(layer_norm, state_rows, gain_rows[8], gain_rows[9])
    latent_low = to_low(latent)
    condition_own = to_low(product_right(latent_low, condition_all))
    condition_rows = jnp.concatenate([condition_own, swap_core(condition_own)], axis=0)
    step_float = own_first(timesteps[0, 0]).astype(jnp.float32)
    alpha_row = alpha_bar(step_float)[:, None]
    target = own_first(noise_copies[0, 0]).astype(jnp.float32)
    noisy_low = to_low(
        jnp.sqrt(alpha_row) * patch_seq.astype(jnp.float32) + jnp.sqrt(1.0 - alpha_row) * target
    )
    lifted = product(noisy_low, head_all[:PATCH])
    feature_low = to_low(time_features(step_float))
    summed = condition_rows.astype(jnp.float32) + product(
        feature_low, head_all[PATCH : PATCH + FREQ]
    )
    activated, silu_back = jax.vjp(jax.nn.silu, summed)
    activated_low = to_low(activated)
    modulation = product_right(activated_low, modulate_all)
    inner_rows, inner_back = jax.vjp(first_modulate, lifted, modulation)
    inner_low = to_low(inner_rows)
    expanded, dense_back = jax.vjp(jax.nn.gelu, product(inner_low, dense_all[0]))
    expanded_low = to_low(expanded)
    branch = product(expanded_low, dense_all[1])
    outer_rows, outer_back = jax.vjp(last_modulate, lifted, modulation, branch)
    outer_low = to_low(outer_rows)
    predicted = product_right(outer_low, head_all[PATCH + FREQ :])
    residue = predicted - target
    loss_local = jnp.sum(weight_row[:, None] * residue * residue) / PATCH
    predicted_grad = to_low(2.0 * weight_row[:, None] * residue / (PATCH * token_count))
    final_turned = product_left(outer_low, predicted_grad)
    lifted_grad, modulation_grad, branch_grad = outer_back(
        product(predicted_grad, head_all[PATCH + FREQ :])
    )
    branch_low = to_low(branch_grad)
    (expanded_grad,) = dense_back(product_right(branch_low, dense_all[1]))
    expanded_grad_low = to_low(expanded_grad)
    lifted_extra, modulation_extra = inner_back(product_right(expanded_grad_low, dense_all[0]))
    modulation_low = flow.tick(to_low(modulation_grad + modulation_extra))
    flow.begin(
        "spread",
        split_weight_task(modulation_low, activated_low, flow, ("modulate.2", "modulate.3")),
    )
    (summed_grad,) = silu_back(product(modulation_low, modulate_all))
    time_turned = product_left(to_low(summed_grad), feature_low)
    lift_turned = product_left(to_low(lifted_grad + lifted_extra), noisy_low)
    head_turned_grad = jnp.concatenate([lift_turned, time_turned, final_turned], axis=1)
    condition_grad = to_low(
        summed_grad[:halfway] + swap_core(to_low(summed_grad[halfway:])).astype(jnp.float32)
    )
    condition_grad = flow.tick(condition_grad)
    flow.begin(
        "head",
        weight_task(
            [
                (1, inner_low, [expanded_grad_low]),
                (1, expanded_low, [branch_low]),
                (1, condition_grad, [latent_low]),
            ],
            True,
            -1,
            [head_turned_grad],
        ),
    )
    state_grad, gain_nine, gain_ten = third_back(product(condition_grad, condition_all))

    def modulate_whole():
        (left_parts,), (right_parts,) = (flow.results["modulate.2"], flow.results["modulate.3"])
        quarters = [left_parts[0], right_parts[0], left_parts[1], right_parts[1]]
        return jnp.concatenate(quarters, axis=-1)[0]

    def attend_whole(depth):
        lower = flow.results["lower%d" % depth]
        return jnp.concatenate([*flow.results["attend%d" % depth], lower[1]], axis=0)

    def expand_whole(depth):
        lower, upper = (flow.results["lower%d" % depth], flow.results["upper%d" % depth])
        return jnp.stack([lower[0].reshape(-1, D), upper[0].reshape(-1, D)])

    def dense_whole():
        return jnp.concatenate(flow.results["head"][:2], axis=0)

    gain_parts = [None, None]
    for depth_index in (1, 0):
        state_grad, gain_parts[depth_index] = block_backward(
            state_grad,
            kept_all[depth_index],
            attend_all[depth_index],
            flow,
            depth_index,
            same_image,
        )
    embedded_grad, token_grad, position_grad = entry_back(state_grad)
    embed_delta = product_left(own_patch, to_low(embedded_grad))
    small_delta = jnp.concatenate(
        [
            gain_parts[0],
            gain_parts[1],
            jnp.stack([gain_nine, gain_ten]),
            token_grad,
            embed_delta,
        ],
        axis=0,
    )
    small_delta = small_delta + swap_core(small_delta)
    small_half = small_delta.shape[0] // 2
    encoder_half = jnp.concatenate(
        [position_grad, lax.dynamic_slice_in_dim(small_delta, core * small_half, small_half, 0)],
        axis=0,
    ).T
    flow.begin("encoder", scatter_task([encoder_half[None]], True, 0, [True], 1))
    encoder_first_half, encoder_last_half = (m[0] for m in flow.take("encoder")[0][0])
    encoder_delta = jnp.concatenate(
        [
            encoder_first_half[:, halfway:],
            encoder_last_half[:, halfway:],
            encoder_first_half[:, :halfway],
            encoder_last_half[:, :halfway],
        ],
        axis=1,
    ).T
    blocks = [name + str(i) for i in range(2) for name in ("upper", "lower", "attend")]
    flow.take("head", "modulate.2", "modulate.3", *blocks)
    reduced = (
        jnp.concatenate([attend_whole(0), attend_whole(1)], axis=0),
        jnp.concatenate([expand_whole(0), expand_whole(1)], axis=0),
        dense_whole(),
        modulate_whole(),
        flow.results["head"][2][0],
        encoder_delta,
        flow.results["head"][3][0].T,
    )
    velocities = (
        attend_velocity,
        expand_velocity,
        dense_velocity,
        modulate_velocity,
        condition_velocity,
    )

    squares = sum((jnp.sum(member * member) for member in reduced))
    totals = sum_all(jnp.stack([squares, loss_local]))
    square_total, loss_sum = (totals[0], totals[1])
    clip_norm = jnp.sqrt(square_total)
    factor = jnp.minimum(1.0, clip_bound / (clip_norm + 1e-06))
    moments = tuple((muon_keep * velocities[i] + factor * reduced[i] for i in range(5)))
    current = muon_steps(moments)
    devices = lax.axis_size(everywhere)
    masters = (attend_weight, expand_weight, dense_weight, modulate_weight, condition_weight)
    updated = tuple(
        (
            masters[i] * (1.0 - muon_rate * muon_decay)
            - muon_rate
            * max(1.0, current[i].shape[-2] * devices / current[i].shape[-1]) ** 0.5
            * current[i]
            for i in range(5)
        )
    )
    encoder_master, encoder_firsts, encoder_seconds = adam_shard(
        encoder_table, encoder_first, encoder_second, factor * reduced[5]
    )
    table_master, table_firsts, table_seconds = adam_shard(
        head_table, head_first, head_second, factor * reduced[6]
    )
    return (
        loss_sum,
        token_count,
        clip_norm,
        updated[0],
        moments[0],
        updated[1],
        moments[1],
        updated[2],
        moments[2],
        updated[3],
        moments[3],
        updated[4],
        moments[4],
        encoder_master,
        encoder_firsts,
        encoder_seconds,
        table_master,
        table_firsts,
        table_seconds,
    )


def solution(mesh):
    placed = (
        P("dp", None, None),
        P("copy", "dp", None, None),
        P("dp", None),
        P("dp", None),
        P("dp", None),
        P("copy", "dp", None),
        P(None, ("dp", "copy"), None),
        P(None, ("dp", "copy"), None),
        P(None, ("dp", "copy"), None),
        P(None, ("dp", "copy"), None),
        P(None, ("dp", "copy"), None),
        P(None, ("dp", "copy"), None),
        P(("dp", "copy"), None),
        P(("dp", "copy"), None),
        P(("dp", "copy"), None),
        P(("dp", "copy"), None),
        P(None, ("dp", "copy")),
        P(None, ("dp", "copy")),
        P(None, ("dp", "copy")),
        P(None, ("dp", "copy")),
        P(None, ("dp", "copy")),
        P(None, ("dp", "copy")),
    )
    return jax.shard_map(
        per_device,
        mesh=mesh,
        in_specs=placed,
        out_specs=(
            P(),
            P(),
            P(),
            P(None, ("dp", "copy"), None),
            P(None, ("dp", "copy"), None),
            P(None, ("dp", "copy"), None),
            P(None, ("dp", "copy"), None),
            P(None, ("dp", "copy"), None),
            P(None, ("dp", "copy"), None),
            P(("dp", "copy"), None),
            P(("dp", "copy"), None),
            P(("dp", "copy"), None),
            P(("dp", "copy"), None),
            P(None, ("dp", "copy")),
            P(None, ("dp", "copy")),
            P(None, ("dp", "copy")),
            P(None, ("dp", "copy")),
            P(None, ("dp", "copy")),
            P(None, ("dp", "copy")),
        ),
        check_vma=False,
    )
```

```python
import math

import jax
import jax.numpy as jnp
from jax import lax
from jax.experimental import pallas as pl
from jax.experimental.pallas import tpu as pltpu
from jax.sharding import PartitionSpec as P

D = 768
HEADS = 12
HD = 64
HW = 1024
PATCH = 64
FREQ = 256
SEQ = 1024
NS_STEPS = 2
STEP = 10
TSTEPS = 1000


precise_mode = lax.Precision.HIGHEST
norm_floor = 1e-06
score_factor = 0.125
newton_first = 3.4445
newton_second = -4.775
newton_third = 2.0315
muon_rate = 1.0
muon_decay = 0.01
muon_keep = 0.95
clip_bound = 0.001
adam_rate = 0.02
beta_first = 0.9
beta_second = 0.95
adam_floor = 1e-08
adam_decay = 0.1


def product(left_side, right_side):
    return jnp.dot(left_side, right_side, preferred_element_type=jnp.float32)


def product_left(left_side, right_side):
    return lax.dot_general(
        left_side, right_side, (((0,), (0,)), ((), ())), preferred_element_type=jnp.float32
    )


def product_right(left_side, right_side):
    return lax.dot_general(
        left_side, right_side, (((1,), (1,)), ((), ())), preferred_element_type=jnp.float32
    )


def to_low(values):
    return values.astype(jnp.bfloat16)


def layer_norm(values, gain_row, bias_row):
    centered = values - jnp.mean(values, axis=-1, keepdims=True)
    spread = jnp.mean(centered * centered, axis=-1, keepdims=True)
    return centered * lax.rsqrt(spread + norm_floor) * gain_row + bias_row


def plain_norm(values):
    centered = values - jnp.mean(values, axis=-1, keepdims=True)
    spread = jnp.mean(centered * centered, axis=-1, keepdims=True)
    return centered * lax.rsqrt(spread + norm_floor)


def alpha_bar(step_float):
    return jnp.cos(0.5 * math.pi * (step_float + 0.5) / TSTEPS) ** 2


def time_features(step_float):
    halfway = FREQ // 2
    frequency = jnp.exp(-math.log(10000.0) * jnp.arange(halfway).astype(jnp.float32) / halfway)
    angles = step_float[:, None] * frequency[None, :]
    return jnp.concatenate([jnp.cos(angles), jnp.sin(angles)], axis=1)


def first_modulate(lifted, modulation):
    return plain_norm(lifted) * (1.0 + modulation[:, HW : 2 * HW]) + modulation[:, :HW]


def last_modulate(lifted, modulation, branch):
    joined = lifted + modulation[:, 2 * HW : 3 * HW] * branch
    return plain_norm(joined) * (1.0 + modulation[:, 4 * HW :]) + modulation[:, 3 * HW : 4 * HW]


def grid_of(count):
    side = 1
    while 2 * side**3 < count:
        side *= 2
    if 2 * side**3 == count:
        return (2 * side, side, side)
    return (count, 1, 1)


def swap_core(values):
    return lax.ppermute(values, "copy", [(0, 1), (1, 0)])


def sum_all(values):
    values = values + swap_core(values)
    count = lax.axis_size("dp")
    if count & (count - 1):
        return lax.psum(values, "dp")
    step = 1
    while step < count:
        values = values + lax.ppermute(values, "dp", [(i, i ^ step) for i in range(count)])
        step *= 2
    return values


class Flow:
    def __init__(self):
        self.live, self.results = ([], {})

    def begin(self, name, task):
        self.live.append([name, task, *next(task)])

    def tick(self, *carry):
        due = [entry for entry in self.live if entry[3] <= 1]
        for entry in self.live:
            entry[3] -= 1
        carry, arrived = lax.optimization_barrier((carry, [entry[2] for entry in due]))
        for entry, values in zip(due, arrived):
            try:
                entry[2], entry[3] = entry[1].send(values)
            except StopIteration as stop:
                self.results[entry[0]] = stop.value
                self.live.remove(entry)
        return carry if len(carry) > 1 else (carry[0] if carry else None)

    def take(self, *names):
        while any(name not in self.results for name in names):
            self.tick()
        return [self.results[name] for name in names]


def columns_of(values, core):
    half = values.shape[-1] // 2
    return lax.dynamic_slice_in_dim(values, core * half, half, values.ndim - 1)


def joined(parts, axis):
    return parts[0] if len(parts) == 1 else jnp.concatenate(parts, axis=axis)


def bits_in_order(crossed):
    grid = grid_of(lax.axis_size("dp"))
    counts = [size.bit_length() - 1 for size in grid]
    z_bits = list(range(counts[2] + counts[1], sum(counts)))
    y_bits = list(range(counts[2], counts[2] + counts[1]))
    x_bits = list(range(counts[2]))
    return (y_bits + x_bits if crossed else x_bits + y_bits) + z_bits


def scatter_task(parts, crossed, axis, exact, lag=2):
    core = lax.axis_index("copy")
    here = lax.axis_index("dp")
    chips = lax.axis_size("dp")
    sizes = [part.shape[axis] for part in parts]
    order = bits_in_order(crossed)
    parts = [
        part.reshape(
            part.shape[0], *[2] * len(order), part.shape[1] // chips, part.shape[2]
        )
        for part in parts
    ]
    left = sorted(order, reverse=True)
    for bit in order:
        position, mine = (1 + left.index(bit), here // 2**bit % 2)
        sent = []
        for part, keep in zip(parts, exact):
            half = lax.dynamic_index_in_dim(part, 1 - mine, position, keepdims=False)
            if keep:
                near = lax.reduce_precision(half, 8, 7)
                sent += [to_low(near), to_low(half - near)]
            else:
                sent.append(to_low(half))
        pairs = [(i, i ^ 2**bit) for i in range(chips)]
        (arrived,) = yield ([lax.ppermute(joined(sent, axis), "dp", pairs)], lag)
        start, totals = (0, [])
        for part, keep, size in zip(parts, exact, sizes):
            total = lax.dynamic_index_in_dim(part, mine, position, keepdims=False)
            for number in range(2 if keep else 1):
                piece = lax.slice_in_dim(
                    arrived, start, start + size, axis=axis % arrived.ndim
                )
                total = total + piece.astype(jnp.float32)
                start += size
            totals.append(total)
        parts = totals
        left.remove(bit)
    values = joined(parts, axis)
    half = values.shape[1] // 2
    mine = lax.dynamic_slice_in_dim(values, core * half, half, 1)
    (arrived,) = yield (
        [swap_core(lax.dynamic_slice_in_dim(values, (1 - core) * half, half, 1))],
        1,
    )
    first = jnp.where(core == 0, mine, arrived)
    last = jnp.where(core == 0, arrived, mine)
    starts = [sum(sizes[:i]) for i in range(len(sizes))]
    return [
        tuple(lax.slice_in_dim(m, start, start + size, axis=axis % m.ndim) for m in (first, last))
        for start, size in zip(starts, sizes)
    ]


def weight_task(products, crossed, axis, tables=(), lag=2):
    core = lax.axis_index("copy")

    def some(right_sides, which):
        return joined([columns_of(right, which) for right in right_sides], 1)

    sent = [product_left(left, some(rights, 1 - core)) for slots, left, rights in products]
    sent += [columns_of(table, 1 - core) for table in tables]
    arrived = yield ([swap_core(part) for part in sent], 1)
    totals = [
        product_left(left, some(rights, core)) + part
        for (slots, left, rights), part in zip(products, arrived)
    ]
    totals = [
        total.reshape(member[0], total.shape[0] // member[0], total.shape[1])
        for total, member in zip(totals, products)
    ]
    for table, part in zip(tables, arrived[len(products) :]):
        totals.append((columns_of(table, core) + part)[None])
    exact = [False] * len(products) + [True] * len(tables)
    halves = yield from scatter_task(totals, crossed, axis, exact, lag)
    found = []
    counts = [len(member[2]) for member in products] + [1] * len(tables)
    for (first, last), count in zip(halves, counts):
        width = first.shape[-1] // count
        for i in range(count):
            pair = [m[..., i * width : (i + 1) * width] for m in (first, last)]
            found.append(jnp.concatenate(pair, axis=-1))
    return found


def split_weight_task(left_side, right_side, flow, names):
    core = lax.axis_index("copy")
    (arrived,) = yield ([swap_core(product_left(left_side, columns_of(right_side, 1 - core)))], 1)
    total = (product_left(left_side, columns_of(right_side, core)) + arrived)[None]
    quarter = total.shape[-1] // 2
    flow.begin(names[0], scatter_task([total[..., :quarter]], False, 0, [False]))
    flow.begin(names[1], scatter_task([total[..., quarter:]], True, 0, [False]))
    return None


def attention_back_kernel(
    query_ref, key_ref, value_ref, grad_ref, log_ref, query_id, key_id, dq_ref, dk_ref, dv_ref
):
    same = key_id[...] == query_id[...]
    query, key, value, grad = (query_ref[...], key_ref[...], value_ref[...], grad_ref[...])
    width = query.shape[1]
    lane = lax.broadcasted_iota(jnp.int32, (1, width), 1)
    query_grad, key_grad, value_grad = (None, None, None)
    for head in range(width // HD):
        inside = jnp.where((lane >= head * HD) & (lane < (head + 1) * HD), 1.0, 0.0)
        query_here = to_low(query.astype(jnp.float32) * inside)
        grad_here = to_low(grad.astype(jnp.float32) * inside)
        key_here = to_low(key.astype(jnp.float32) * inside)
        scores = product_right(key, query_here) * score_factor
        chance = jnp.where(same, jnp.exp(scores - log_ref[head]), 0.0)
        soft_grad = product_right(value, grad_here)
        total = jnp.sum(chance * soft_grad, axis=0, keepdims=True)
        score_low = to_low(chance * (soft_grad - total) * score_factor)
        parts = (
            product_left(key_here, score_low),
            product(score_low, query_here),
            product(to_low(chance), grad_here),
        )
        if head == 0:
            query_grad, key_grad, value_grad = parts
        else:
            query_grad, key_grad, value_grad = (
                query_grad + parts[0],
                key_grad + parts[1],
                value_grad + parts[2],
            )
    dq_ref[...] = to_low(query_grad.T)
    first = pl.program_id(1) == 0

    @pl.when(first)
    def _():
        dk_ref[...] = key_grad
        dv_ref[...] = value_grad

    @pl.when(jnp.logical_not(first))
    def _():
        dk_ref[...] += key_grad
        dv_ref[...] += value_grad


def attention_back(query, key, value, grad, log_total, query_ids, key_ids):
    queries, keys = (query.shape[0], key.shape[0])
    width, chunk = (2 * HD, 256)
    own = pl.BlockSpec((chunk, width), lambda pair, part: (part, pair))
    whole = pl.BlockSpec((keys, width), lambda pair, part: (0, pair))
    return pl.pallas_call(
        attention_back_kernel,
        grid=(D // width, queries // chunk),
        in_specs=[
            own,
            whole,
            whole,
            own,
            pl.BlockSpec((2, 1, chunk), lambda pair, part: (pair, 0, part)),
            pl.BlockSpec((1, chunk), lambda pair, part: (0, part)),
            pl.BlockSpec((keys, 1), lambda pair, part: (0, 0)),
        ],
        out_specs=[own, whole, whole],
        out_shape=[
            jax.ShapeDtypeStruct((queries, D), jnp.bfloat16),
            jax.ShapeDtypeStruct((keys, D), jnp.float32),
            jax.ShapeDtypeStruct((keys, D), jnp.float32),
        ],
        compiler_params=pltpu.CompilerParams(vmem_limit_bytes=48 * 2**20),
        cost_estimate=pl.CostEstimate(
            flops=10 * queries * keys * D * 2,
            bytes_accessed=12 * keys * D,
            transcendentals=queries * keys * HEADS,
        ),
    )(query, key, value, grad, log_total, query_ids[None, :], key_ids[:, None])


def attention_scores(query_heads, key_heads, same_image):
    raw_scores = jnp.einsum(
        "qhd,khd->hqk", query_heads, key_heads, preferred_element_type=jnp.float32
    )
    return jnp.where(same_image[None], raw_scores * score_factor, -1e30)


def block_forward(entered, attend_low, expand_low, flow, gain_rows, same_image):
    halfway = entered.shape[0]
    normed, first_back = jax.vjp(layer_norm, entered, gain_rows[0], gain_rows[1])
    normed_low = to_low(normed)
    key_low = to_low(product(normed_low, attend_low[1]))
    value_low = to_low(product(normed_low, attend_low[2]))
    key_all = jnp.concatenate([key_low, swap_core(key_low)], axis=0)
    value_all = jnp.concatenate([value_low, swap_core(value_low)], axis=0)
    query_low = to_low(product(normed_low, attend_low[0]))
    query_heads = query_low.reshape(halfway, HEADS, HD)
    key_heads = key_all.reshape(SEQ, HEADS, HD)
    value_heads = value_all.reshape(SEQ, HEADS, HD)
    scores = attention_scores(query_heads, key_heads, same_image)
    highest = jnp.max(scores, axis=-1, keepdims=True)
    exponent_rows = jnp.exp(scores - highest)
    row_total = jnp.sum(exponent_rows, axis=-1, keepdims=True)
    log_total = highest + jnp.log(row_total)
    attended = to_low(
        jnp.einsum(
            "hqk,khd->qhd",
            to_low(exponent_rows / row_total),
            value_heads,
            preferred_element_type=jnp.float32,
        ).reshape(halfway, D)
    )
    middle = entered + product(attended, attend_low[3])
    normed_two, second_back = jax.vjp(layer_norm, middle, gain_rows[2], gain_rows[3])
    normed_two_low = to_low(normed_two)
    hidden, gelu_back = jax.vjp(jax.nn.gelu, product_right(normed_two_low, expand_low[0]))
    hidden_low = to_low(hidden)
    output_rows = middle + product(hidden_low, expand_low[1])
    kept = (
        first_back,
        normed_low,
        query_low,
        key_all,
        value_all,
        log_total,
        attended,
        second_back,
        normed_two_low,
        gelu_back,
        hidden_low,
        expand_low,
    )
    return (output_rows, kept)


def block_backward(output_grad, kept, attend_low, flow, depth, image_row):
    (
        first_back,
        normed_low,
        query_low,
        key_all,
        value_all,
        log_total,
        attended,
        second_back,
        normed_two_low,
        gelu_back,
        hidden_low,
        expand_low,
    ) = kept
    halfway = attended.shape[0]
    copies = expand_low[0].shape[0] // D
    upper_low = to_low(output_grad)
    flow.begin(
        "upper%d" % depth,
        weight_task([(copies, hidden_low, [upper_low])], False, 0),
    )
    (hidden_grad,) = gelu_back(product_right(upper_low, expand_low[1]))
    hidden_grad_low = flow.tick(to_low(hidden_grad))
    middle_extra, gain_three, gain_four = second_back(product(hidden_grad_low, expand_low[0]))
    middle_grad = flow.tick(output_grad + middle_extra)
    projected_low = to_low(middle_grad)
    flow.begin(
        "lower%d" % depth,
        weight_task(
            [(copies, hidden_grad_low, [normed_two_low]), (1, attended, [projected_low])],
            True,
            0,
        ),
    )
    attended_grad = flow.tick(to_low(product_right(projected_low, attend_low[3])))
    query_grad, key_part, value_part = attention_back(
        query_low,
        key_all,
        value_all,
        attended_grad,
        log_total.reshape(HEADS, 1, halfway),
        image_row[:halfway],
        image_row,
    )
    key_part, value_part = flow.tick(key_part, value_part)
    value_grad = to_low(
        value_part[:halfway] + swap_core(to_low(value_part[halfway:])).astype(jnp.float32)
    )
    key_grad = to_low(
        key_part[:halfway] + swap_core(to_low(key_part[halfway:])).astype(jnp.float32)
    )
    query_grad, key_grad, value_grad = flow.tick(query_grad, key_grad, value_grad)
    flow.begin(
        "attend%d" % depth,
        weight_task([(1, normed_low, [query_grad, key_grad, value_grad])], False, 0, (), 1 + depth),
    )
    normed_grad = (
        product_right(query_grad, attend_low[0])
        + product_right(key_grad, attend_low[1])
        + product_right(value_grad, attend_low[2])
    )
    entered_extra, gain_one, gain_two = first_back(normed_grad)
    gain_delta = jnp.stack([gain_one, gain_two, gain_three, gain_four])
    return (flow.tick(middle_grad + entered_extra), gain_delta)


def newton_extra(gram_matrix):
    gram_low = to_low(gram_matrix)
    first_tail = newton_second * gram_matrix + newton_third * product(gram_low, gram_low)
    tail_low = to_low(first_tail)
    once = newton_first * gram_matrix + product(gram_low, tail_low)
    later = newton_first * once + product(to_low(once), tail_low)
    later_low = to_low(later)
    last_tail = newton_second * later + newton_third * product(later_low, later_low)
    return newton_first * (first_tail + last_tail) + product(tail_low, to_low(last_tail))


def padded(piece, rows, columns):
    lead = [(0, 0)] * (piece.ndim - 2)
    return jnp.pad(
        piece, (*lead, (0, rows - piece.shape[-2]), (0, columns - piece.shape[-1]))
    )


muon_counts = (4, 8, 8, 2, 1)


def first_owner():
    return lax.axis_size(("dp", "copy")) // 4


def owner_tables():
    devices, start = (lax.axis_size(("dp", "copy")), first_owner())

    def table(values, kind):
        return jnp.asarray([0] * start + values + [0] * (devices - start - len(values)), kind)

    return (
        table([1] * 12 + [0] * 11, jnp.float32),
        table([1] * 4 + [0] * 19, jnp.float32),
    )


def owner_buffer(modulate, expand, attend, dense, condition, rows, columns):
    devices, start = (lax.axis_size(("dp", "copy")), first_owner())
    groups = [jnp.zeros((start, rows, columns), jnp.bfloat16)]
    for given, count in zip((modulate, expand, attend, dense, condition), muon_counts):
        held = 0
        for member in given:
            if isinstance(member, int):
                groups.append(jnp.zeros((member, rows, columns), jnp.bfloat16))
                held += member
            else:
                groups.append(padded(to_low(member), rows, columns))
                held += member.shape[0]
        assert held == count
    groups.append(
        jnp.zeros((devices - start - sum(muon_counts), rows, columns), jnp.bfloat16)
    )
    return jnp.concatenate(groups, axis=0)


def in_parts(values, count):
    return values.reshape(-1, values.shape[-2] // count, values.shape[-1])


def muon_steps(moments):
    attend, expand, dense, modulate, condition = moments
    highest = max(
        modulate.shape[0] // 4,
        expand.shape[1] // 2,
        attend.shape[1],
        dense.shape[1],
        condition.shape[0],
    )
    held = lax.all_to_all(
        owner_buffer(
            [in_parts(modulate, 4)],
            [in_parts(expand, 2)],
            [attend],
            [dense],
            [condition[None]],
            highest,
            HW,
        ),
        ("dp", "copy"),
        0,
        0,
    )
    devices = held.shape[0]
    held = held.reshape(devices * highest, HW)
    core, me = (lax.axis_index("copy"), lax.axis_index(("dp", "copy")))
    shared_here, crossed_here = owner_tables()
    gram_matrix = product_left(held, held)
    gram_matrix = gram_matrix + shared_here[me] * swap_core(gram_matrix)
    chips = [(i, i ^ 1) for i in range(lax.axis_size("dp"))]
    near = lax.ppermute(to_low(columns_of(gram_matrix, core)), "dp", chips)
    far = swap_core(near)
    crossed = jnp.concatenate(
        [jnp.where(core == 0, near, far), jnp.where(core == 0, far, near)], axis=1
    )
    gram_matrix = gram_matrix + crossed_here[me] * crossed.astype(jnp.float32)
    rows = lax.broadcasted_iota(jnp.int32, gram_matrix.shape, 0)
    columns = lax.broadcasted_iota(jnp.int32, gram_matrix.shape, 1)
    trace = jnp.sum(jnp.where(rows == columns, gram_matrix, 0.0))
    scale_here = 1.0 / (jnp.sqrt(trace) + 1e-07)
    extra = newton_extra(gram_matrix * (scale_here * scale_here))
    result = to_low(product(held, to_low(extra)) * scale_here)
    back = lax.all_to_all(result.reshape(devices, highest, HW), ("dp", "copy"), 0, 0)
    squares = [
        jnp.sum((member * member).reshape(-1, *member.shape[-2:]), axis=(1, 2))
        for member in moments
    ]
    inverse = 1.0 / (jnp.sqrt(sum_all(jnp.concatenate(squares))) + 1e-07)
    scaled = newton_first * newton_first * inverse
    found, start = ([], first_owner())
    shapes = [moments[i].shape for i in (3, 1, 0, 2, 4)]
    for shape, count in zip(shapes, muon_counts):
        part = back[start : start + count]
        rows = math.prod(shape[:-1]) // count
        found.append(part[:, :rows, : shape[-1]].reshape(shape).astype(jnp.float32))
        start += count
    modulate, expand, attend, dense, condition = found
    return (
        scaled[:8, None, None] * moments[0] + attend,
        scaled[8:12, None, None] * moments[1] + expand,
        scaled[12:14, None, None] * moments[2] + dense,
        scaled[14] * moments[3] + modulate,
        scaled[15] * moments[4] + condition,
    )


def adam_shard(master, first, second, gradient):
    first_new = beta_first * first + (1.0 - beta_first) * gradient
    second_new = beta_second * second + (1.0 - beta_second) * gradient * gradient
    corrected_first = first_new / (1.0 - beta_first**STEP)
    corrected_second = second_new / (1.0 - beta_second**STEP)
    master_new = master - adam_rate * (
        corrected_first / (jnp.sqrt(corrected_second) + adam_floor) + adam_decay * master
    )
    return (master_new, first_new, second_new)


def per_device(
    patches,
    noise_copies,
    image_ids,
    buffer_flags,
    loss_mask,
    timesteps,
    attend_weight,
    attend_velocity,
    expand_weight,
    expand_velocity,
    dense_weight,
    dense_velocity,
    modulate_weight,
    modulate_velocity,
    condition_weight,
    condition_velocity,
    encoder_table,
    encoder_first,
    encoder_second,
    head_table,
    head_first,
    head_second,
):
    everywhere = ("dp", "copy")
    core = lax.axis_index("copy")
    flow = Flow()
    attend_low, expand_low, dense_low = (
        to_low(attend_weight),
        to_low(expand_weight),
        to_low(dense_weight),
    )
    rows, wide = (attend_weight.shape[1], dense_weight.shape[1])
    table_slots = -(-encoder_table.shape[0] // D)
    encoder_turned = padded(to_low(encoder_table).T, rows, table_slots * D)
    encoder_turned = encoder_turned.reshape(rows, table_slots, D).transpose(1, 0, 2)
    expand_slots = expand_low.reshape(expand_low.shape[0], -1, rows, D)
    copies = expand_slots.shape[1]

    def gathered(members):
        return lax.all_gather(jnp.concatenate(members, axis=0), everywhere, axis=1, tiled=True)

    entry_part = gathered([attend_low[:4], encoder_turned])
    later_part = gathered([expand_slots[0], expand_slots[1], attend_low[4:], *expand_slots[2:]])
    modulate_rows = modulate_weight.shape[0]
    head_part = lax.all_gather(
        jnp.concatenate(
            [
                to_low(modulate_weight),
                dense_low[0],
                dense_low[1],
                padded(to_low(condition_weight), wide, HW),
                padded(to_low(head_table).T, wide, HW),
            ],
            axis=0,
        )[None],
        everywhere,
        axis=0,
        tiled=True,
    )

    def rows_of(start, count):
        return head_part[:, start : start + count].reshape(-1, HW)

    attend_all = [entry_part[:4], later_part[2 * copies : 2 * copies + 4]]
    expand_all = [
        (
            member[: copies].reshape(copies * D, D),
            member[copies:].reshape(copies * D, D),
        )
        for member in (later_part[: 2 * copies], later_part[2 * copies + 4 :])
    ]
    encoder_all = jnp.concatenate([entry_part[4 + i] for i in range(table_slots)], axis=1).T[
        : encoder_table.shape[0]
    ]
    modulate_all = rows_of(0, modulate_rows)
    dense_all = [rows_of(modulate_rows, wide), rows_of(modulate_rows + wide, wide)]
    condition_all = rows_of(modulate_rows + 2 * wide, wide)[:, :D]
    head_all = rows_of(modulate_rows + 3 * wide, wide)[:, : head_table.shape[0]].T
    halfway = SEQ // 2
    offset = core * halfway

    def own_first(values):
        return jnp.where(
            core == 0, values, jnp.concatenate([values[halfway:], values[:halfway]], axis=0)
        )

    patch_seq = own_first(patches[0])
    image_row = own_first(image_ids[0])
    buffer_row = own_first(buffer_flags[0])
    masked_row = own_first(loss_mask[0])
    weight_row = (masked_row * (1 - buffer_row)).astype(jnp.float32)
    token_count = sum_all(jnp.sum(weight_row))
    own_patch = patch_seq[:halfway]
    buffer_on = buffer_row[:halfway, None] > 0
    masked_on = masked_row[:halfway, None] > 0
    same_image = image_row[:halfway, None] == image_row[None, :]
    gain_rows = encoder_all[:12].astype(jnp.float32)
    position = lax.dynamic_slice_in_dim(encoder_all, 12 + PATCH + offset, halfway, 0).astype(
        jnp.float32
    )
    embedded = product(own_patch, encoder_all[12 : 12 + PATCH])

    def entry(embedded_rows, token_pair, position_rows):
        return (
            jnp.where(buffer_on, token_pair[1], jnp.where(masked_on, token_pair[0], embedded_rows))
            + position_rows
        )

    entered, entry_back = jax.vjp(entry, embedded, gain_rows[10:12], position)
    state_rows = entered
    kept_all = []
    for depth_index in range(2):
        state_rows, kept = block_forward(
            state_rows,
            attend_all[depth_index],
            expand_all[depth_index],
            flow,
            gain_rows[4 * depth_index : 4 * depth_index + 4],
            same_image,
        )
        kept_all.append(kept)
    latent, third_back = jax.vjp(layer_norm, state_rows, gain_rows[8], gain_rows[9])
    latent_low = to_low(latent)
    condition_own = to_low(product_right(latent_low, condition_all))
    condition_rows = jnp.concatenate([condition_own, swap_core(condition_own)], axis=0)
    step_float = own_first(timesteps[0, 0]).astype(jnp.float32)
    alpha_row = alpha_bar(step_float)[:, None]
    target = own_first(noise_copies[0, 0]).astype(jnp.float32)
    noisy_low = to_low(
        jnp.sqrt(alpha_row) * patch_seq.astype(jnp.float32) + jnp.sqrt(1.0 - alpha_row) * target
    )
    lifted = product(noisy_low, head_all[:PATCH])
    feature_low = to_low(time_features(step_float))
    summed = condition_rows.astype(jnp.float32) + product(
        feature_low, head_all[PATCH : PATCH + FREQ]
    )
    activated, silu_back = jax.vjp(jax.nn.silu, summed)
    activated_low = to_low(activated)
    modulation = product_right(activated_low, modulate_all)
    inner_rows, inner_back = jax.vjp(first_modulate, lifted, modulation)
    inner_low = to_low(inner_rows)
    expanded, dense_back = jax.vjp(jax.nn.gelu, product(inner_low, dense_all[0]))
    expanded_low = to_low(expanded)
    branch = product(expanded_low, dense_all[1])
    outer_rows, outer_back = jax.vjp(last_modulate, lifted, modulation, branch)
    outer_low = to_low(outer_rows)
    predicted = product_right(outer_low, head_all[PATCH + FREQ :])
    residue = predicted - target
    loss_local = jnp.sum(weight_row[:, None] * residue * residue) / PATCH
    predicted_grad = to_low(2.0 * weight_row[:, None] * residue / (PATCH * token_count))
    final_turned = product_left(outer_low, predicted_grad)
    lifted_grad, modulation_grad, branch_grad = outer_back(
        product(predicted_grad, head_all[PATCH + FREQ :])
    )
    branch_low = to_low(branch_grad)
    (expanded_grad,) = dense_back(product_right(branch_low, dense_all[1]))
    expanded_grad_low = to_low(expanded_grad)
    lifted_extra, modulation_extra = inner_back(product_right(expanded_grad_low, dense_all[0]))
    modulation_low = flow.tick(to_low(modulation_grad + modulation_extra))
    flow.begin(
        "spread",
        split_weight_task(modulation_low, activated_low, flow, ("modulate.2", "modulate.3")),
    )
    (summed_grad,) = silu_back(product(modulation_low, modulate_all))
    time_turned = product_left(to_low(summed_grad), feature_low)
    lift_turned = product_left(to_low(lifted_grad + lifted_extra), noisy_low)
    head_turned_grad = jnp.concatenate([lift_turned, time_turned, final_turned], axis=1)
    condition_grad = to_low(
        summed_grad[:halfway] + swap_core(to_low(summed_grad[halfway:])).astype(jnp.float32)
    )
    condition_grad = flow.tick(condition_grad)
    flow.begin(
        "head",
        weight_task(
            [
                (1, inner_low, [expanded_grad_low]),
                (1, expanded_low, [branch_low]),
                (1, condition_grad, [latent_low]),
            ],
            True,
            -1,
            [head_turned_grad],
        ),
    )
    state_grad, gain_nine, gain_ten = third_back(product(condition_grad, condition_all))

    def modulate_whole():
        (left_parts,), (right_parts,) = (flow.results["modulate.2"], flow.results["modulate.3"])
        quarters = [left_parts[0], right_parts[0], left_parts[1], right_parts[1]]
        return jnp.concatenate(quarters, axis=-1)[0]

    def attend_whole(depth):
        lower = flow.results["lower%d" % depth]
        return jnp.concatenate([*flow.results["attend%d" % depth], lower[1]], axis=0)

    def expand_whole(depth):
        lower, upper = (flow.results["lower%d" % depth], flow.results["upper%d" % depth])
        return jnp.stack([lower[0].reshape(-1, D), upper[0].reshape(-1, D)])

    def dense_whole():
        return jnp.concatenate(flow.results["head"][:2], axis=0)

    gain_parts = [None, None]
    for depth_index in (1, 0):
        state_grad, gain_parts[depth_index] = block_backward(
            state_grad,
            kept_all[depth_index],
            attend_all[depth_index],
            flow,
            depth_index,
            image_row,
        )
    embedded_grad, token_grad, position_grad = entry_back(state_grad)
    embed_delta = product_left(own_patch, to_low(embedded_grad))
    small_delta = jnp.concatenate(
        [
            gain_parts[0],
            gain_parts[1],
            jnp.stack([gain_nine, gain_ten]),
            token_grad,
            embed_delta,
        ],
        axis=0,
    )
    small_delta = small_delta + swap_core(small_delta)
    small_half = small_delta.shape[0] // 2
    encoder_half = jnp.concatenate(
        [position_grad, lax.dynamic_slice_in_dim(small_delta, core * small_half, small_half, 0)],
        axis=0,
    ).T
    flow.begin("encoder", scatter_task([encoder_half[None]], True, 0, [True], 1))
    encoder_first_half, encoder_last_half = (m[0] for m in flow.take("encoder")[0][0])
    encoder_delta = jnp.concatenate(
        [
            encoder_first_half[:, halfway:],
            encoder_last_half[:, halfway:],
            encoder_first_half[:, :halfway],
            encoder_last_half[:, :halfway],
        ],
        axis=1,
    ).T
    blocks = [name + str(i) for i in range(2) for name in ("upper", "lower", "attend")]
    flow.take("head", "modulate.2", "modulate.3", *blocks)
    reduced = (
        jnp.concatenate([attend_whole(0), attend_whole(1)], axis=0),
        jnp.concatenate([expand_whole(0), expand_whole(1)], axis=0),
        dense_whole(),
        modulate_whole(),
        flow.results["head"][2][0],
        encoder_delta,
        flow.results["head"][3][0].T,
    )
    velocities = (
        attend_velocity,
        expand_velocity,
        dense_velocity,
        modulate_velocity,
        condition_velocity,
    )

    squares = sum((jnp.sum(member * member) for member in reduced))
    totals = sum_all(jnp.stack([squares, loss_local]))
    square_total, loss_sum = (totals[0], totals[1])
    clip_norm = jnp.sqrt(square_total)
    factor = jnp.minimum(1.0, clip_bound / (clip_norm + 1e-06))
    moments = tuple((muon_keep * velocities[i] + factor * reduced[i] for i in range(5)))
    current = muon_steps(moments)
    devices = lax.axis_size(everywhere)
    masters = (attend_weight, expand_weight, dense_weight, modulate_weight, condition_weight)
    updated = tuple(
        (
            masters[i] * (1.0 - muon_rate * muon_decay)
            - muon_rate
            * max(1.0, current[i].shape[-2] * devices / current[i].shape[-1]) ** 0.5
            * current[i]
            for i in range(5)
        )
    )
    encoder_master, encoder_firsts, encoder_seconds = adam_shard(
        encoder_table, encoder_first, encoder_second, factor * reduced[5]
    )
    table_master, table_firsts, table_seconds = adam_shard(
        head_table, head_first, head_second, factor * reduced[6]
    )
    return (
        loss_sum,
        token_count,
        clip_norm,
        updated[0],
        moments[0],
        updated[1],
        moments[1],
        updated[2],
        moments[2],
        updated[3],
        moments[3],
        updated[4],
        moments[4],
        encoder_master,
        encoder_firsts,
        encoder_seconds,
        table_master,
        table_firsts,
        table_seconds,
    )


def solution(mesh):
    placed = (
        P("dp", None, None),
        P("copy", "dp", None, None),
        P("dp", None),
        P("dp", None),
        P("dp", None),
        P("copy", "dp", None),
        P(None, ("dp", "copy"), None),
        P(None, ("dp", "copy"), None),
        P(None, ("dp", "copy"), None),
        P(None, ("dp", "copy"), None),
        P(None, ("dp", "copy"), None),
        P(None, ("dp", "copy"), None),
        P(("dp", "copy"), None),
        P(("dp", "copy"), None),
        P(("dp", "copy"), None),
        P(("dp", "copy"), None),
        P(None, ("dp", "copy")),
        P(None, ("dp", "copy")),
        P(None, ("dp", "copy")),
        P(None, ("dp", "copy")),
        P(None, ("dp", "copy")),
        P(None, ("dp", "copy")),
    )
    return jax.shard_map(
        per_device,
        mesh=mesh,
        in_specs=placed,
        out_specs=(
            P(),
            P(),
            P(),
            P(None, ("dp", "copy"), None),
            P(None, ("dp", "copy"), None),
            P(None, ("dp", "copy"), None),
            P(None, ("dp", "copy"), None),
            P(None, ("dp", "copy"), None),
            P(None, ("dp", "copy"), None),
            P(("dp", "copy"), None),
            P(("dp", "copy"), None),
            P(("dp", "copy"), None),
            P(("dp", "copy"), None),
            P(None, ("dp", "copy")),
            P(None, ("dp", "copy")),
            P(None, ("dp", "copy")),
            P(None, ("dp", "copy")),
            P(None, ("dp", "copy")),
            P(None, ("dp", "copy")),
        ),
        check_vma=False,
    )
```

```python
import math

import jax
import jax.numpy as jnp
from jax import lax
from jax.experimental import pallas as pl
from jax.experimental.pallas import tpu as pltpu
from jax.sharding import PartitionSpec as P

D = 768
HEADS = 12
HD = 64
HW = 1024
PATCH = 64
FREQ = 256
SEQ = 1024
NS_STEPS = 2
STEP = 10
TSTEPS = 1000


precise_mode = lax.Precision.HIGHEST
norm_floor = 1e-06
score_factor = 0.125
newton_first = 3.4445
newton_second = -4.775
newton_third = 2.0315
muon_rate = 1.0
muon_decay = 0.01
muon_keep = 0.95
clip_bound = 0.001
adam_rate = 0.02
beta_first = 0.9
beta_second = 0.95
adam_floor = 1e-08
adam_decay = 0.1


def product(left_side, right_side):
    return jnp.dot(left_side, right_side, preferred_element_type=jnp.float32)


def product_left(left_side, right_side):
    return lax.dot_general(
        left_side, right_side, (((0,), (0,)), ((), ())), preferred_element_type=jnp.float32
    )


def product_right(left_side, right_side):
    return lax.dot_general(
        left_side, right_side, (((1,), (1,)), ((), ())), preferred_element_type=jnp.float32
    )


def to_low(values):
    return values.astype(jnp.bfloat16)


def layer_norm(values, gain_row, bias_row):
    centered = values - jnp.mean(values, axis=-1, keepdims=True)
    spread = jnp.mean(centered * centered, axis=-1, keepdims=True)
    return centered * lax.rsqrt(spread + norm_floor) * gain_row + bias_row


def plain_norm(values):
    centered = values - jnp.mean(values, axis=-1, keepdims=True)
    spread = jnp.mean(centered * centered, axis=-1, keepdims=True)
    return centered * lax.rsqrt(spread + norm_floor)


def alpha_bar(step_float):
    return jnp.cos(0.5 * math.pi * (step_float + 0.5) / TSTEPS) ** 2


def time_features(step_float):
    halfway = FREQ // 2
    frequency = jnp.exp(-math.log(10000.0) * jnp.arange(halfway).astype(jnp.float32) / halfway)
    angles = step_float[:, None] * frequency[None, :]
    return jnp.concatenate([jnp.cos(angles), jnp.sin(angles)], axis=1)


def first_modulate(lifted, modulation):
    return plain_norm(lifted) * (1.0 + modulation[:, HW : 2 * HW]) + modulation[:, :HW]


def last_modulate(lifted, modulation, branch):
    joined = lifted + modulation[:, 2 * HW : 3 * HW] * branch
    return plain_norm(joined) * (1.0 + modulation[:, 4 * HW :]) + modulation[:, 3 * HW : 4 * HW]


def grid_of(count):
    side = 1
    while 2 * side**3 < count:
        side *= 2
    if 2 * side**3 == count:
        return (2 * side, side, side)
    return (count, 1, 1)


def swap_core(values):
    return lax.ppermute(values, "copy", [(0, 1), (1, 0)])


def sum_all(values):
    values = values + swap_core(values)
    count = lax.axis_size("dp")
    if count & (count - 1):
        return lax.psum(values, "dp")
    step = 1
    while step < count:
        values = values + lax.ppermute(values, "dp", [(i, i ^ step) for i in range(count)])
        step *= 2
    return values


class Flow:
    def __init__(self):
        self.live, self.results = ([], {})

    def begin(self, name, task):
        self.live.append([name, task, *next(task)])

    def tick(self, *carry):
        due = [entry for entry in self.live if entry[3] <= 1]
        for entry in self.live:
            entry[3] -= 1
        carry, arrived = lax.optimization_barrier((carry, [entry[2] for entry in due]))
        for entry, values in zip(due, arrived):
            try:
                entry[2], entry[3] = entry[1].send(values)
            except StopIteration as stop:
                self.results[entry[0]] = stop.value
                self.live.remove(entry)
        return carry if len(carry) > 1 else (carry[0] if carry else None)

    def take(self, *names):
        while any(name not in self.results for name in names):
            self.tick()
        return [self.results[name] for name in names]


def columns_of(values, core):
    half = values.shape[-1] // 2
    return lax.dynamic_slice_in_dim(values, core * half, half, values.ndim - 1)


def joined(parts, axis):
    return parts[0] if len(parts) == 1 else jnp.concatenate(parts, axis=axis)


def bits_in_order(crossed):
    grid = grid_of(lax.axis_size("dp"))
    counts = [size.bit_length() - 1 for size in grid]
    z_bits = list(range(counts[2] + counts[1], sum(counts)))
    y_bits = list(range(counts[2], counts[2] + counts[1]))
    x_bits = list(range(counts[2]))
    return (y_bits + x_bits if crossed else x_bits + y_bits) + z_bits


def scatter_task(parts, crossed, axis, exact, lag=2):
    core = lax.axis_index("copy")
    here = lax.axis_index("dp")
    chips = lax.axis_size("dp")
    sizes = [part.shape[axis] for part in parts]
    order = bits_in_order(crossed)
    parts = [
        part.reshape(
            part.shape[0], *[2] * len(order), part.shape[1] // chips, part.shape[2]
        )
        for part in parts
    ]
    left = sorted(order, reverse=True)
    for bit in order:
        position, mine = (1 + left.index(bit), here // 2**bit % 2)
        sent = []
        for part, keep in zip(parts, exact):
            half = lax.dynamic_index_in_dim(part, 1 - mine, position, keepdims=False)
            if keep:
                near = lax.reduce_precision(half, 8, 7)
                sent += [to_low(near), to_low(half - near)]
            else:
                sent.append(to_low(half))
        pairs = [(i, i ^ 2**bit) for i in range(chips)]
        (arrived,) = yield ([lax.ppermute(joined(sent, axis), "dp", pairs)], lag)
        start, totals = (0, [])
        for part, keep, size in zip(parts, exact, sizes):
            total = lax.dynamic_index_in_dim(part, mine, position, keepdims=False)
            for number in range(2 if keep else 1):
                piece = lax.slice_in_dim(
                    arrived, start, start + size, axis=axis % arrived.ndim
                )
                total = total + piece.astype(jnp.float32)
                start += size
            totals.append(total)
        parts = totals
        left.remove(bit)
    values = joined(parts, axis)
    half = values.shape[1] // 2
    mine = lax.dynamic_slice_in_dim(values, core * half, half, 1)
    (arrived,) = yield (
        [swap_core(lax.dynamic_slice_in_dim(values, (1 - core) * half, half, 1))],
        1,
    )
    first = jnp.where(core == 0, mine, arrived)
    last = jnp.where(core == 0, arrived, mine)
    starts = [sum(sizes[:i]) for i in range(len(sizes))]
    return [
        tuple(lax.slice_in_dim(m, start, start + size, axis=axis % m.ndim) for m in (first, last))
        for start, size in zip(starts, sizes)
    ]


def weight_task(products, crossed, axis, tables=(), lag=2):
    core = lax.axis_index("copy")

    def some(right_sides, which):
        return joined([columns_of(right, which) for right in right_sides], 1)

    sent = [product_left(left, some(rights, 1 - core)) for slots, left, rights in products]
    sent += [columns_of(table, 1 - core) for table in tables]
    arrived = yield ([swap_core(part) for part in sent], 1)
    totals = [
        product_left(left, some(rights, core)) + part
        for (slots, left, rights), part in zip(products, arrived)
    ]
    totals = [
        total.reshape(member[0], total.shape[0] // member[0], total.shape[1])
        for total, member in zip(totals, products)
    ]
    for table, part in zip(tables, arrived[len(products) :]):
        totals.append((columns_of(table, core) + part)[None])
    exact = [False] * len(products) + [True] * len(tables)
    halves = yield from scatter_task(totals, crossed, axis, exact, lag)
    found = []
    counts = [len(member[2]) for member in products] + [1] * len(tables)
    for (first, last), count in zip(halves, counts):
        width = first.shape[-1] // count
        for i in range(count):
            pair = [m[..., i * width : (i + 1) * width] for m in (first, last)]
            found.append(jnp.concatenate(pair, axis=-1))
    return found


def split_weight_task(left_side, right_side, flow, names):
    core = lax.axis_index("copy")
    (arrived,) = yield ([swap_core(product_left(left_side, columns_of(right_side, 1 - core)))], 1)
    total = (product_left(left_side, columns_of(right_side, core)) + arrived)[None]
    quarter = total.shape[-1] // 2
    flow.begin(names[0], scatter_task([total[..., :quarter]], False, 0, [False], 3))
    flow.begin(names[1], scatter_task([total[..., quarter:]], True, 0, [False], 3))
    return None


def attention_back_kernel(
    query_ref, key_ref, value_ref, grad_ref, log_ref, query_id, key_id, dq_ref, dk_ref, dv_ref
):
    same = key_id[...] == query_id[...]
    query, key, value, grad = (query_ref[...], key_ref[...], value_ref[...], grad_ref[...])
    width = query.shape[1]
    lane = lax.broadcasted_iota(jnp.int32, (1, width), 1)
    query_grad, key_grad, value_grad = (None, None, None)
    for head in range(width // HD):
        inside = jnp.where((lane >= head * HD) & (lane < (head + 1) * HD), 1.0, 0.0)
        query_here = to_low(query.astype(jnp.float32) * inside)
        grad_here = to_low(grad.astype(jnp.float32) * inside)
        key_here = to_low(key.astype(jnp.float32) * inside)
        scores = product_right(key, query_here) * score_factor
        chance = jnp.where(same, jnp.exp(scores - log_ref[head]), 0.0)
        soft_grad = product_right(value, grad_here)
        total = jnp.sum(chance * soft_grad, axis=0, keepdims=True)
        score_low = to_low(chance * (soft_grad - total) * score_factor)
        parts = (
            product_left(key_here, score_low),
            product(score_low, query_here),
            product(to_low(chance), grad_here),
        )
        if head == 0:
            query_grad, key_grad, value_grad = parts
        else:
            query_grad, key_grad, value_grad = (
                query_grad + parts[0],
                key_grad + parts[1],
                value_grad + parts[2],
            )
    dq_ref[...] = to_low(query_grad.T)
    first = pl.program_id(1) == 0

    @pl.when(first)
    def _():
        dk_ref[...] = key_grad
        dv_ref[...] = value_grad

    @pl.when(jnp.logical_not(first))
    def _():
        dk_ref[...] += key_grad
        dv_ref[...] += value_grad


def attention_back(query, key, value, grad, log_total, query_ids, key_ids):
    queries, keys = (query.shape[0], key.shape[0])
    width, chunk = (2 * HD, 256)
    own = pl.BlockSpec((chunk, width), lambda pair, part: (part, pair))
    whole = pl.BlockSpec((keys, width), lambda pair, part: (0, pair))
    return pl.pallas_call(
        attention_back_kernel,
        grid=(D // width, queries // chunk),
        in_specs=[
            own,
            whole,
            whole,
            own,
            pl.BlockSpec((2, 1, chunk), lambda pair, part: (pair, 0, part)),
            pl.BlockSpec((1, chunk), lambda pair, part: (0, part)),
            pl.BlockSpec((keys, 1), lambda pair, part: (0, 0)),
        ],
        out_specs=[own, whole, whole],
        out_shape=[
            jax.ShapeDtypeStruct((queries, D), jnp.bfloat16),
            jax.ShapeDtypeStruct((keys, D), jnp.float32),
            jax.ShapeDtypeStruct((keys, D), jnp.float32),
        ],
        compiler_params=pltpu.CompilerParams(vmem_limit_bytes=48 * 2**20),
        cost_estimate=pl.CostEstimate(
            flops=10 * queries * keys * D * 2,
            bytes_accessed=12 * keys * D,
            transcendentals=queries * keys * HEADS,
        ),
    )(query, key, value, grad, log_total, query_ids[None, :], key_ids[:, None])


def attention_scores(query_heads, key_heads, same_image):
    raw_scores = jnp.einsum(
        "qhd,khd->hqk", query_heads, key_heads, preferred_element_type=jnp.float32
    )
    return jnp.where(same_image[None], raw_scores * score_factor, -1e30)


def block_forward(entered, attend_low, expand_low, flow, gain_rows, same_image):
    halfway = entered.shape[0]
    normed, first_back = jax.vjp(layer_norm, entered, gain_rows[0], gain_rows[1])
    normed_low = to_low(normed)
    key_low = to_low(product(normed_low, attend_low[1]))
    value_low = to_low(product(normed_low, attend_low[2]))
    key_all = jnp.concatenate([key_low, swap_core(key_low)], axis=0)
    value_all = jnp.concatenate([value_low, swap_core(value_low)], axis=0)
    query_low = to_low(product(normed_low, attend_low[0]))
    query_heads = query_low.reshape(halfway, HEADS, HD)
    key_heads = key_all.reshape(SEQ, HEADS, HD)
    value_heads = value_all.reshape(SEQ, HEADS, HD)
    scores = attention_scores(query_heads, key_heads, same_image)
    highest = jnp.max(scores, axis=-1, keepdims=True)
    exponent_rows = jnp.exp(scores - highest)
    row_total = jnp.sum(exponent_rows, axis=-1, keepdims=True)
    log_total = highest + jnp.log(row_total)
    attended = to_low(
        jnp.einsum(
            "hqk,khd->qhd",
            to_low(exponent_rows / row_total),
            value_heads,
            preferred_element_type=jnp.float32,
        ).reshape(halfway, D)
    )
    middle = entered + product(attended, attend_low[3])
    normed_two, second_back = jax.vjp(layer_norm, middle, gain_rows[2], gain_rows[3])
    normed_two_low = to_low(normed_two)
    hidden, gelu_back = jax.vjp(jax.nn.gelu, product_right(normed_two_low, expand_low[0]))
    hidden_low = to_low(hidden)
    output_rows = middle + product(hidden_low, expand_low[1])
    kept = (
        first_back,
        normed_low,
        query_low,
        key_all,
        value_all,
        log_total,
        attended,
        second_back,
        normed_two_low,
        gelu_back,
        hidden_low,
        expand_low,
    )
    return (output_rows, kept)


def block_backward(output_grad, kept, attend_low, flow, depth, image_row):
    (
        first_back,
        normed_low,
        query_low,
        key_all,
        value_all,
        log_total,
        attended,
        second_back,
        normed_two_low,
        gelu_back,
        hidden_low,
        expand_low,
    ) = kept
    halfway = attended.shape[0]
    copies = expand_low[0].shape[0] // D
    upper_low = to_low(output_grad)
    flow.begin(
        "upper%d" % depth,
        weight_task([(copies, hidden_low, [upper_low])], False, 0),
    )
    (hidden_grad,) = gelu_back(product_right(upper_low, expand_low[1]))
    hidden_grad_low = flow.tick(to_low(hidden_grad))
    middle_extra, gain_three, gain_four = second_back(product(hidden_grad_low, expand_low[0]))
    middle_grad = flow.tick(output_grad + middle_extra)
    projected_low = to_low(middle_grad)
    flow.begin(
        "lower%d" % depth,
        weight_task(
            [(copies, hidden_grad_low, [normed_two_low]), (1, attended, [projected_low])],
            True,
            0,
        ),
    )
    attended_grad = flow.tick(to_low(product_right(projected_low, attend_low[3])))
    query_grad, key_part, value_part = attention_back(
        query_low,
        key_all,
        value_all,
        attended_grad,
        log_total.reshape(HEADS, 1, halfway),
        image_row[:halfway],
        image_row,
    )
    key_part, value_part = flow.tick(key_part, value_part)
    value_grad = to_low(
        value_part[:halfway] + swap_core(to_low(value_part[halfway:])).astype(jnp.float32)
    )
    key_grad = to_low(
        key_part[:halfway] + swap_core(to_low(key_part[halfway:])).astype(jnp.float32)
    )
    query_grad, key_grad, value_grad = flow.tick(query_grad, key_grad, value_grad)
    flow.begin(
        "attend%d" % depth,
        weight_task([(1, normed_low, [query_grad, key_grad, value_grad])], False, 0, (), 1 + depth),
    )
    normed_grad = (
        product_right(query_grad, attend_low[0])
        + product_right(key_grad, attend_low[1])
        + product_right(value_grad, attend_low[2])
    )
    entered_extra, gain_one, gain_two = first_back(normed_grad)
    gain_delta = jnp.stack([gain_one, gain_two, gain_three, gain_four])
    return (flow.tick(middle_grad + entered_extra), gain_delta)


def newton_extra(gram_matrix):
    gram_low = to_low(gram_matrix)
    first_tail = newton_second * gram_matrix + newton_third * product(gram_low, gram_low)
    tail_low = to_low(first_tail)
    once = newton_first * gram_matrix + product(gram_low, tail_low)
    later = newton_first * once + product(to_low(once), tail_low)
    later_low = to_low(later)
    last_tail = newton_second * later + newton_third * product(later_low, later_low)
    return newton_first * (first_tail + last_tail) + product(tail_low, to_low(last_tail))


def padded(piece, rows, columns):
    lead = [(0, 0)] * (piece.ndim - 2)
    return jnp.pad(
        piece, (*lead, (0, rows - piece.shape[-2]), (0, columns - piece.shape[-1]))
    )


muon_counts = (4, 8, 8, 2, 1)


def first_owner():
    return lax.axis_size(("dp", "copy")) // 4


def owner_tables():
    devices, start = (lax.axis_size(("dp", "copy")), first_owner())

    def table(values, kind):
        return jnp.asarray([0] * start + values + [0] * (devices - start - len(values)), kind)

    return (
        table([1] * 12 + [0] * 11, jnp.float32),
        table([1] * 4 + [0] * 19, jnp.float32),
    )


def owner_buffer(modulate, expand, attend, dense, condition, rows, columns):
    devices, start = (lax.axis_size(("dp", "copy")), first_owner())
    groups = [jnp.zeros((start, rows, columns), jnp.bfloat16)]
    for given, count in zip((modulate, expand, attend, dense, condition), muon_counts):
        held = 0
        for member in given:
            if isinstance(member, int):
                groups.append(jnp.zeros((member, rows, columns), jnp.bfloat16))
                held += member
            else:
                groups.append(padded(to_low(member), rows, columns))
                held += member.shape[0]
        assert held == count
    groups.append(
        jnp.zeros((devices - start - sum(muon_counts), rows, columns), jnp.bfloat16)
    )
    return jnp.concatenate(groups, axis=0)


def in_parts(values, count):
    return values.reshape(-1, values.shape[-2] // count, values.shape[-1])


def muon_steps(moments):
    attend, expand, dense, modulate, condition = moments
    highest = max(
        modulate.shape[0] // 4,
        expand.shape[1] // 2,
        attend.shape[1],
        dense.shape[1],
        condition.shape[0],
    )
    held = lax.all_to_all(
        owner_buffer(
            [in_parts(modulate, 4)],
            [in_parts(expand, 2)],
            [attend],
            [dense],
            [condition[None]],
            highest,
            HW,
        ),
        ("dp", "copy"),
        0,
        0,
    )
    devices = held.shape[0]
    held = held.reshape(devices * highest, HW)
    core, me = (lax.axis_index("copy"), lax.axis_index(("dp", "copy")))
    shared_here, crossed_here = owner_tables()
    gram_matrix = product_left(held, held)
    gram_matrix = gram_matrix + shared_here[me] * swap_core(gram_matrix)
    chips = [(i, i ^ 1) for i in range(lax.axis_size("dp"))]
    near = lax.ppermute(to_low(columns_of(gram_matrix, core)), "dp", chips)
    far = swap_core(near)
    crossed = jnp.concatenate(
        [jnp.where(core == 0, near, far), jnp.where(core == 0, far, near)], axis=1
    )
    gram_matrix = gram_matrix + crossed_here[me] * crossed.astype(jnp.float32)
    rows = lax.broadcasted_iota(jnp.int32, gram_matrix.shape, 0)
    columns = lax.broadcasted_iota(jnp.int32, gram_matrix.shape, 1)
    trace = jnp.sum(jnp.where(rows == columns, gram_matrix, 0.0))
    scale_here = 1.0 / (jnp.sqrt(trace) + 1e-07)
    extra = newton_extra(gram_matrix * (scale_here * scale_here))
    result = to_low(product(held, to_low(extra)) * scale_here)
    back = lax.all_to_all(result.reshape(devices, highest, HW), ("dp", "copy"), 0, 0)
    squares = [
        jnp.sum((member * member).reshape(-1, *member.shape[-2:]), axis=(1, 2))
        for member in moments
    ]
    inverse = 1.0 / (jnp.sqrt(sum_all(jnp.concatenate(squares))) + 1e-07)
    scaled = newton_first * newton_first * inverse
    found, start = ([], first_owner())
    shapes = [moments[i].shape for i in (3, 1, 0, 2, 4)]
    for shape, count in zip(shapes, muon_counts):
        part = back[start : start + count]
        rows = math.prod(shape[:-1]) // count
        found.append(part[:, :rows, : shape[-1]].reshape(shape).astype(jnp.float32))
        start += count
    modulate, expand, attend, dense, condition = found
    return (
        scaled[:8, None, None] * moments[0] + attend,
        scaled[8:12, None, None] * moments[1] + expand,
        scaled[12:14, None, None] * moments[2] + dense,
        scaled[14] * moments[3] + modulate,
        scaled[15] * moments[4] + condition,
    )


def adam_shard(master, first, second, gradient):
    first_new = beta_first * first + (1.0 - beta_first) * gradient
    second_new = beta_second * second + (1.0 - beta_second) * gradient * gradient
    corrected_first = first_new / (1.0 - beta_first**STEP)
    corrected_second = second_new / (1.0 - beta_second**STEP)
    master_new = master - adam_rate * (
        corrected_first / (jnp.sqrt(corrected_second) + adam_floor) + adam_decay * master
    )
    return (master_new, first_new, second_new)


def per_device(
    patches,
    noise_copies,
    image_ids,
    buffer_flags,
    loss_mask,
    timesteps,
    attend_weight,
    attend_velocity,
    expand_weight,
    expand_velocity,
    dense_weight,
    dense_velocity,
    modulate_weight,
    modulate_velocity,
    condition_weight,
    condition_velocity,
    encoder_table,
    encoder_first,
    encoder_second,
    head_table,
    head_first,
    head_second,
):
    everywhere = ("dp", "copy")
    core = lax.axis_index("copy")
    flow = Flow()
    attend_low, expand_low, dense_low = (
        to_low(attend_weight),
        to_low(expand_weight),
        to_low(dense_weight),
    )
    rows, wide = (attend_weight.shape[1], dense_weight.shape[1])
    table_slots = -(-encoder_table.shape[0] // D)
    encoder_turned = padded(to_low(encoder_table).T, rows, table_slots * D)
    encoder_turned = encoder_turned.reshape(rows, table_slots, D).transpose(1, 0, 2)
    expand_slots = expand_low.reshape(expand_low.shape[0], -1, rows, D)
    copies = expand_slots.shape[1]

    def gathered(members):
        return lax.all_gather(jnp.concatenate(members, axis=0), everywhere, axis=1, tiled=True)

    entry_part = gathered([attend_low[:4], encoder_turned])
    later_part = gathered([expand_slots[0], expand_slots[1], attend_low[4:], *expand_slots[2:]])
    modulate_rows = modulate_weight.shape[0]
    head_part = lax.all_gather(
        jnp.concatenate(
            [
                to_low(modulate_weight),
                dense_low[0],
                dense_low[1],
                padded(to_low(condition_weight), wide, HW),
                padded(to_low(head_table).T, wide, HW),
            ],
            axis=0,
        )[None],
        everywhere,
        axis=0,
        tiled=True,
    )

    def rows_of(start, count):
        return head_part[:, start : start + count].reshape(-1, HW)

    attend_all = [entry_part[:4], later_part[2 * copies : 2 * copies + 4]]
    expand_all = [
        (
            member[: copies].reshape(copies * D, D),
            member[copies:].reshape(copies * D, D),
        )
        for member in (later_part[: 2 * copies], later_part[2 * copies + 4 :])
    ]
    encoder_all = jnp.concatenate([entry_part[4 + i] for i in range(table_slots)], axis=1).T[
        : encoder_table.shape[0]
    ]
    halfway = SEQ // 2
    offset = core * halfway

    def own_first(values):
        return jnp.where(
            core == 0, values, jnp.concatenate([values[halfway:], values[:halfway]], axis=0)
        )

    patch_seq = own_first(patches[0])
    image_row = own_first(image_ids[0])
    buffer_row = own_first(buffer_flags[0])
    masked_row = own_first(loss_mask[0])
    weight_row = (masked_row * (1 - buffer_row)).astype(jnp.float32)
    token_count = sum_all(jnp.sum(weight_row))
    step_float = own_first(timesteps[0, 0]).astype(jnp.float32)
    alpha_row = alpha_bar(step_float)[:, None]
    target = own_first(noise_copies[0, 0]).astype(jnp.float32)
    noisy_low = to_low(
        jnp.sqrt(alpha_row) * patch_seq.astype(jnp.float32) + jnp.sqrt(1.0 - alpha_row) * target
    )
    feature_low = to_low(time_features(step_float))
    encoder_all, noisy_low, feature_low, target = lax.optimization_barrier(
        (encoder_all, noisy_low, feature_low, target)
    )
    own_patch = patch_seq[:halfway]
    buffer_on = buffer_row[:halfway, None] > 0
    masked_on = masked_row[:halfway, None] > 0
    same_image = image_row[:halfway, None] == image_row[None, :]
    gain_rows = encoder_all[:12].astype(jnp.float32)
    position = lax.dynamic_slice_in_dim(encoder_all, 12 + PATCH + offset, halfway, 0).astype(
        jnp.float32
    )
    embedded = product(own_patch, encoder_all[12 : 12 + PATCH])

    def entry(embedded_rows, token_pair, position_rows):
        return (
            jnp.where(buffer_on, token_pair[1], jnp.where(masked_on, token_pair[0], embedded_rows))
            + position_rows
        )

    entered, entry_back = jax.vjp(entry, embedded, gain_rows[10:12], position)
    state_rows = entered
    kept_all = []
    for depth_index in range(2):
        state_rows, kept = block_forward(
            state_rows,
            attend_all[depth_index],
            expand_all[depth_index],
            flow,
            gain_rows[4 * depth_index : 4 * depth_index + 4],
            same_image,
        )
        kept_all.append(kept)
    state_rows, head_part = lax.optimization_barrier((state_rows, head_part))
    modulate_all = rows_of(0, modulate_rows)
    dense_all = [rows_of(modulate_rows, wide), rows_of(modulate_rows + wide, wide)]
    condition_all = rows_of(modulate_rows + 2 * wide, wide)[:, :D]
    head_all = rows_of(modulate_rows + 3 * wide, wide)[:, : head_table.shape[0]].T
    latent, third_back = jax.vjp(layer_norm, state_rows, gain_rows[8], gain_rows[9])
    latent_low = to_low(latent)
    condition_own = to_low(product_right(latent_low, condition_all))
    condition_rows = jnp.concatenate([condition_own, swap_core(condition_own)], axis=0)
    lifted = product(noisy_low, head_all[:PATCH])
    summed = condition_rows.astype(jnp.float32) + product(
        feature_low, head_all[PATCH : PATCH + FREQ]
    )
    activated, silu_back = jax.vjp(jax.nn.silu, summed)
    activated_low = to_low(activated)
    modulation = product_right(activated_low, modulate_all)
    inner_rows, inner_back = jax.vjp(first_modulate, lifted, modulation)
    inner_low = to_low(inner_rows)
    expanded, dense_back = jax.vjp(jax.nn.gelu, product(inner_low, dense_all[0]))
    expanded_low = to_low(expanded)
    branch = product(expanded_low, dense_all[1])
    outer_rows, outer_back = jax.vjp(last_modulate, lifted, modulation, branch)
    outer_low = to_low(outer_rows)
    predicted = product_right(outer_low, head_all[PATCH + FREQ :])
    residue = predicted - target
    loss_local = jnp.sum(weight_row[:, None] * residue * residue) / PATCH
    predicted_grad = to_low(2.0 * weight_row[:, None] * residue / (PATCH * token_count))
    final_turned = product_left(outer_low, predicted_grad)
    lifted_grad, modulation_grad, branch_grad = outer_back(
        product(predicted_grad, head_all[PATCH + FREQ :])
    )
    branch_low = to_low(branch_grad)
    (expanded_grad,) = dense_back(product_right(branch_low, dense_all[1]))
    expanded_grad_low = to_low(expanded_grad)
    lifted_extra, modulation_extra = inner_back(product_right(expanded_grad_low, dense_all[0]))
    modulation_low = flow.tick(to_low(modulation_grad + modulation_extra))
    flow.begin(
        "spread",
        split_weight_task(modulation_low, activated_low, flow, ("modulate.2", "modulate.3")),
    )
    (summed_grad,) = silu_back(product(modulation_low, modulate_all))
    time_turned = product_left(to_low(summed_grad), feature_low)
    lift_turned = product_left(to_low(lifted_grad + lifted_extra), noisy_low)
    head_turned_grad = jnp.concatenate([lift_turned, time_turned, final_turned], axis=1)
    condition_grad = to_low(
        summed_grad[:halfway] + swap_core(to_low(summed_grad[halfway:])).astype(jnp.float32)
    )
    condition_grad = flow.tick(condition_grad)
    flow.begin(
        "head",
        weight_task(
            [
                (1, inner_low, [expanded_grad_low]),
                (1, expanded_low, [branch_low]),
                (1, condition_grad, [latent_low]),
            ],
            True,
            -1,
            [head_turned_grad],
            3,
        ),
    )
    state_grad, gain_nine, gain_ten = third_back(product(condition_grad, condition_all))

    def modulate_whole():
        (left_parts,), (right_parts,) = (flow.results["modulate.2"], flow.results["modulate.3"])
        quarters = [left_parts[0], right_parts[0], left_parts[1], right_parts[1]]
        return jnp.concatenate(quarters, axis=-1)[0]

    def attend_whole(depth):
        lower = flow.results["lower%d" % depth]
        return jnp.concatenate([*flow.results["attend%d" % depth], lower[1]], axis=0)

    def expand_whole(depth):
        lower, upper = (flow.results["lower%d" % depth], flow.results["upper%d" % depth])
        return jnp.stack([lower[0].reshape(-1, D), upper[0].reshape(-1, D)])

    def dense_whole():
        return jnp.concatenate(flow.results["head"][:2], axis=0)

    gain_parts = [None, None]
    for depth_index in (1, 0):
        state_grad, gain_parts[depth_index] = block_backward(
            state_grad,
            kept_all[depth_index],
            attend_all[depth_index],
            flow,
            depth_index,
            image_row,
        )
    embedded_grad, token_grad, position_grad = entry_back(state_grad)
    embed_delta = product_left(own_patch, to_low(embedded_grad))
    small_delta = jnp.concatenate(
        [
            gain_parts[0],
            gain_parts[1],
            jnp.stack([gain_nine, gain_ten]),
            token_grad,
            embed_delta,
        ],
        axis=0,
    )
    small_delta = small_delta + swap_core(small_delta)
    small_half = small_delta.shape[0] // 2
    small_own = lax.dynamic_slice_in_dim(small_delta, core * small_half, small_half, 0)
    flow.begin(
        "encoder",
        scatter_task([small_own.T[None], position_grad.T[None]], True, -1, [True, False], 1),
    )
    small_pair, position_pair = flow.take("encoder")[0]
    encoder_delta = jnp.concatenate([*small_pair, *position_pair], axis=-1)[0].T
    blocks = [name + str(i) for i in range(2) for name in ("upper", "lower", "attend")]
    flow.take("head", "modulate.2", "modulate.3", *blocks)
    reduced = (
        jnp.concatenate([attend_whole(0), attend_whole(1)], axis=0),
        jnp.concatenate([expand_whole(0), expand_whole(1)], axis=0),
        dense_whole(),
        modulate_whole(),
        flow.results["head"][2][0],
        encoder_delta,
        flow.results["head"][3][0].T,
    )
    velocities = (
        attend_velocity,
        expand_velocity,
        dense_velocity,
        modulate_velocity,
        condition_velocity,
    )

    squares = sum((jnp.sum(member * member) for member in reduced))
    totals = sum_all(jnp.stack([squares, loss_local]))
    square_total, loss_sum = (totals[0], totals[1])
    clip_norm = jnp.sqrt(square_total)
    factor = jnp.minimum(1.0, clip_bound / (clip_norm + 1e-06))
    moments = tuple((muon_keep * velocities[i] + factor * reduced[i] for i in range(5)))
    current = muon_steps(moments)
    devices = lax.axis_size(everywhere)
    masters = (attend_weight, expand_weight, dense_weight, modulate_weight, condition_weight)
    updated = tuple(
        (
            masters[i] * (1.0 - muon_rate * muon_decay)
            - muon_rate
            * max(1.0, current[i].shape[-2] * devices / current[i].shape[-1]) ** 0.5
            * current[i]
            for i in range(5)
        )
    )
    encoder_master, encoder_firsts, encoder_seconds = adam_shard(
        encoder_table, encoder_first, encoder_second, factor * reduced[5]
    )
    table_master, table_firsts, table_seconds = adam_shard(
        head_table, head_first, head_second, factor * reduced[6]
    )
    return (
        loss_sum,
        token_count,
        clip_norm,
        updated[0],
        moments[0],
        updated[1],
        moments[1],
        updated[2],
        moments[2],
        updated[3],
        moments[3],
        updated[4],
        moments[4],
        encoder_master,
        encoder_firsts,
        encoder_seconds,
        table_master,
        table_firsts,
        table_seconds,
    )


def solution(mesh):
    placed = (
        P("dp", None, None),
        P("copy", "dp", None, None),
        P("dp", None),
        P("dp", None),
        P("dp", None),
        P("copy", "dp", None),
        P(None, ("dp", "copy"), None),
        P(None, ("dp", "copy"), None),
        P(None, ("dp", "copy"), None),
        P(None, ("dp", "copy"), None),
        P(None, ("dp", "copy"), None),
        P(None, ("dp", "copy"), None),
        P(("dp", "copy"), None),
        P(("dp", "copy"), None),
        P(("dp", "copy"), None),
        P(("dp", "copy"), None),
        P(None, ("dp", "copy")),
        P(None, ("dp", "copy")),
        P(None, ("dp", "copy")),
        P(None, ("dp", "copy")),
        P(None, ("dp", "copy")),
        P(None, ("dp", "copy")),
    )
    return jax.shard_map(
        per_device,
        mesh=mesh,
        in_specs=placed,
        out_specs=(
            P(),
            P(),
            P(),
            P(None, ("dp", "copy"), None),
            P(None, ("dp", "copy"), None),
            P(None, ("dp", "copy"), None),
            P(None, ("dp", "copy"), None),
            P(None, ("dp", "copy"), None),
            P(None, ("dp", "copy"), None),
            P(("dp", "copy"), None),
            P(("dp", "copy"), None),
            P(("dp", "copy"), None),
            P(("dp", "copy"), None),
            P(None, ("dp", "copy")),
            P(None, ("dp", "copy")),
            P(None, ("dp", "copy")),
            P(None, ("dp", "copy")),
            P(None, ("dp", "copy")),
            P(None, ("dp", "copy")),
        ),
        check_vma=False,
    )
```

```python
import math

import jax
import jax.numpy as jnp
from jax import lax
from jax.experimental import pallas as pl
from jax.experimental.pallas import tpu as pltpu
from jax.sharding import PartitionSpec as P

D = 768
HEADS = 12
HD = 64
HW = 1024
PATCH = 64
FREQ = 256
SEQ = 1024
NS_STEPS = 2
STEP = 10
TSTEPS = 1000


precise_mode = lax.Precision.HIGHEST
norm_floor = 1e-06
score_factor = 0.125
newton_first = 3.4445
newton_second = -4.775
newton_third = 2.0315
muon_rate = 1.0
muon_decay = 0.01
muon_keep = 0.95
clip_bound = 0.001
adam_rate = 0.02
beta_first = 0.9
beta_second = 0.95
adam_floor = 1e-08
adam_decay = 0.1


def product(left_side, right_side):
    return jnp.dot(left_side, right_side, preferred_element_type=jnp.float32)


def product_left(left_side, right_side):
    return lax.dot_general(
        left_side, right_side, (((0,), (0,)), ((), ())), preferred_element_type=jnp.float32
    )


def product_right(left_side, right_side):
    return lax.dot_general(
        left_side, right_side, (((1,), (1,)), ((), ())), preferred_element_type=jnp.float32
    )


def to_low(values):
    return values.astype(jnp.bfloat16)


def layer_norm(values, gain_row, bias_row):
    centered = values - jnp.mean(values, axis=-1, keepdims=True)
    spread = jnp.mean(centered * centered, axis=-1, keepdims=True)
    return centered * lax.rsqrt(spread + norm_floor) * gain_row + bias_row


def plain_norm(values):
    centered = values - jnp.mean(values, axis=-1, keepdims=True)
    spread = jnp.mean(centered * centered, axis=-1, keepdims=True)
    return centered * lax.rsqrt(spread + norm_floor)


def alpha_bar(step_float):
    return jnp.cos(0.5 * math.pi * (step_float + 0.5) / TSTEPS) ** 2


def time_features(step_float):
    halfway = FREQ // 2
    frequency = jnp.exp(-math.log(10000.0) * jnp.arange(halfway).astype(jnp.float32) / halfway)
    angles = step_float[:, None] * frequency[None, :]
    return jnp.concatenate([jnp.cos(angles), jnp.sin(angles)], axis=1)


def first_modulate(lifted, modulation):
    return plain_norm(lifted) * (1.0 + modulation[:, HW : 2 * HW]) + modulation[:, :HW]


def last_modulate(lifted, modulation, branch):
    joined = lifted + modulation[:, 2 * HW : 3 * HW] * branch
    return plain_norm(joined) * (1.0 + modulation[:, 4 * HW :]) + modulation[:, 3 * HW : 4 * HW]


def grid_of(count):
    side = 1
    while 2 * side**3 < count:
        side *= 2
    if 2 * side**3 == count:
        return (2 * side, side, side)
    return (count, 1, 1)


def swap_core(values):
    return lax.ppermute(values, "copy", [(0, 1), (1, 0)])


def sum_all(values):
    values = values + swap_core(values)
    count = lax.axis_size("dp")
    if count & (count - 1):
        return lax.psum(values, "dp")
    step = 1
    while step < count:
        values = values + lax.ppermute(values, "dp", [(i, i ^ step) for i in range(count)])
        step *= 2
    return values


class Flow:
    def __init__(self):
        self.live, self.results = ([], {})

    def begin(self, name, task):
        self.live.append([name, task, *next(task)])

    def tick(self, *carry):
        due = [entry for entry in self.live if entry[3] <= 1]
        for entry in self.live:
            entry[3] -= 1
        carry, arrived = lax.optimization_barrier((carry, [entry[2] for entry in due]))
        for entry, values in zip(due, arrived):
            try:
                entry[2], entry[3] = entry[1].send(values)
            except StopIteration as stop:
                self.results[entry[0]] = stop.value
                self.live.remove(entry)
        return carry if len(carry) > 1 else (carry[0] if carry else None)

    def take(self, *names):
        while any(name not in self.results for name in names):
            self.tick()
        return [self.results[name] for name in names]


def columns_of(values, core):
    half = values.shape[-1] // 2
    return lax.dynamic_slice_in_dim(values, core * half, half, values.ndim - 1)


def joined(parts, axis):
    return parts[0] if len(parts) == 1 else jnp.concatenate(parts, axis=axis)


def bits_in_order(crossed):
    grid = grid_of(lax.axis_size("dp"))
    counts = [size.bit_length() - 1 for size in grid]
    z_bits = list(range(counts[2] + counts[1], sum(counts)))
    y_bits = list(range(counts[2], counts[2] + counts[1]))
    x_bits = list(range(counts[2]))
    return (y_bits + x_bits if crossed else x_bits + y_bits) + z_bits


def scatter_task(parts, crossed, axis, exact, lag=2):
    core = lax.axis_index("copy")
    here = lax.axis_index("dp")
    chips = lax.axis_size("dp")
    sizes = [part.shape[axis] for part in parts]
    order = bits_in_order(crossed)
    parts = [
        part.reshape(
            part.shape[0], *[2] * len(order), part.shape[1] // chips, part.shape[2]
        )
        for part in parts
    ]
    left = sorted(order, reverse=True)
    for bit in order:
        position, mine = (1 + left.index(bit), here // 2**bit % 2)
        sent = []
        for part, keep in zip(parts, exact):
            half = lax.dynamic_index_in_dim(part, 1 - mine, position, keepdims=False)
            if keep:
                near = lax.reduce_precision(half, 8, 7)
                sent += [to_low(near), to_low(half - near)]
            else:
                sent.append(to_low(half))
        pairs = [(i, i ^ 2**bit) for i in range(chips)]
        (arrived,) = yield ([lax.ppermute(joined(sent, axis), "dp", pairs)], lag)
        start, totals = (0, [])
        for part, keep, size in zip(parts, exact, sizes):
            total = lax.dynamic_index_in_dim(part, mine, position, keepdims=False)
            for number in range(2 if keep else 1):
                piece = lax.slice_in_dim(
                    arrived, start, start + size, axis=axis % arrived.ndim
                )
                total = total + piece.astype(jnp.float32)
                start += size
            totals.append(total)
        parts = totals
        left.remove(bit)
    values = joined(parts, axis)
    half = values.shape[1] // 2
    mine = lax.dynamic_slice_in_dim(values, core * half, half, 1)
    (arrived,) = yield (
        [swap_core(lax.dynamic_slice_in_dim(values, (1 - core) * half, half, 1))],
        1,
    )
    first = jnp.where(core == 0, mine, arrived)
    last = jnp.where(core == 0, arrived, mine)
    starts = [sum(sizes[:i]) for i in range(len(sizes))]
    return [
        tuple(lax.slice_in_dim(m, start, start + size, axis=axis % m.ndim) for m in (first, last))
        for start, size in zip(starts, sizes)
    ]


def weight_task(products, crossed, axis, tables=(), lag=2):
    core = lax.axis_index("copy")

    def some(right_sides, which):
        return joined([columns_of(right, which) for right in right_sides], 1)

    sent = [product_left(left, some(rights, 1 - core)) for slots, left, rights in products]
    sent += [columns_of(table, 1 - core) for table in tables]
    arrived = yield ([swap_core(part) for part in sent], 1)
    totals = [
        product_left(left, some(rights, core)) + part
        for (slots, left, rights), part in zip(products, arrived)
    ]
    totals = [
        total.reshape(member[0], total.shape[0] // member[0], total.shape[1])
        for total, member in zip(totals, products)
    ]
    for table, part in zip(tables, arrived[len(products) :]):
        totals.append((columns_of(table, core) + part)[None])
    exact = [False] * len(products) + [True] * len(tables)
    halves = yield from scatter_task(totals, crossed, axis, exact, lag)
    found = []
    counts = [len(member[2]) for member in products] + [1] * len(tables)
    for (first, last), count in zip(halves, counts):
        width = first.shape[-1] // count
        for i in range(count):
            pair = [m[..., i * width : (i + 1) * width] for m in (first, last)]
            found.append(jnp.concatenate(pair, axis=-1))
    return found


def split_weight_task(left_side, right_side, flow, names):
    core = lax.axis_index("copy")
    (arrived,) = yield ([swap_core(product_left(left_side, columns_of(right_side, 1 - core)))], 1)
    total = (product_left(left_side, columns_of(right_side, core)) + arrived)[None]
    quarter = total.shape[-1] // 2
    flow.begin(names[0], scatter_task([total[..., :quarter]], False, 0, [False], 3))
    flow.begin(names[1], scatter_task([total[..., quarter:]], True, 0, [False], 3))
    return None


def attention_back_kernel(
    query_ref, key_ref, value_ref, grad_ref, log_ref, query_id, key_id, dq_ref, dk_ref, dv_ref
):
    same = key_id[...] == query_id[...]
    query, key, value, grad = (query_ref[...], key_ref[...], value_ref[...], grad_ref[...])
    width = query.shape[1]
    lane = lax.broadcasted_iota(jnp.int32, (1, width), 1)
    query_grad, key_grad, value_grad = (None, None, None)
    for head in range(width // HD):
        inside = jnp.where((lane >= head * HD) & (lane < (head + 1) * HD), 1.0, 0.0)
        query_here = to_low(query.astype(jnp.float32) * inside)
        grad_here = to_low(grad.astype(jnp.float32) * inside)
        key_here = to_low(key.astype(jnp.float32) * inside)
        scores = product_right(key, query_here) * score_factor
        chance = jnp.where(same, jnp.exp(scores - log_ref[head]), 0.0)
        soft_grad = product_right(value, grad_here)
        total = jnp.sum(chance * soft_grad, axis=0, keepdims=True)
        score_low = to_low(chance * (soft_grad - total) * score_factor)
        parts = (
            product_left(key_here, score_low),
            product(score_low, query_here),
            product(to_low(chance), grad_here),
        )
        if head == 0:
            query_grad, key_grad, value_grad = parts
        else:
            query_grad, key_grad, value_grad = (
                query_grad + parts[0],
                key_grad + parts[1],
                value_grad + parts[2],
            )
    dq_ref[...] = to_low(query_grad.T)
    first = pl.program_id(1) == 0

    @pl.when(first)
    def _():
        dk_ref[...] = key_grad
        dv_ref[...] = value_grad

    @pl.when(jnp.logical_not(first))
    def _():
        dk_ref[...] += key_grad
        dv_ref[...] += value_grad


def attention_back(query, key, value, grad, log_total, query_ids, key_ids):
    queries, keys = (query.shape[0], key.shape[0])
    width, chunk = (2 * HD, 256)
    own = pl.BlockSpec((chunk, width), lambda pair, part: (part, pair))
    whole = pl.BlockSpec((keys, width), lambda pair, part: (0, pair))
    return pl.pallas_call(
        attention_back_kernel,
        grid=(D // width, queries // chunk),
        in_specs=[
            own,
            whole,
            whole,
            own,
            pl.BlockSpec((2, 1, chunk), lambda pair, part: (pair, 0, part)),
            pl.BlockSpec((1, chunk), lambda pair, part: (0, part)),
            pl.BlockSpec((keys, 1), lambda pair, part: (0, 0)),
        ],
        out_specs=[own, whole, whole],
        out_shape=[
            jax.ShapeDtypeStruct((queries, D), jnp.bfloat16),
            jax.ShapeDtypeStruct((keys, D), jnp.float32),
            jax.ShapeDtypeStruct((keys, D), jnp.float32),
        ],
        compiler_params=pltpu.CompilerParams(vmem_limit_bytes=48 * 2**20),
        cost_estimate=pl.CostEstimate(
            flops=10 * queries * keys * D * 2,
            bytes_accessed=12 * keys * D,
            transcendentals=queries * keys * HEADS,
        ),
    )(query, key, value, grad, log_total, query_ids[None, :], key_ids[:, None])


def attention_scores(query_heads, key_heads, same_image):
    raw_scores = jnp.einsum(
        "qhd,khd->hqk", query_heads, key_heads, preferred_element_type=jnp.float32
    )
    return jnp.where(same_image[None], raw_scores * score_factor, -1e30)


def block_forward(entered, attend_low, expand_low, flow, gain_rows, same_image):
    halfway = entered.shape[0]
    normed, first_back = jax.vjp(layer_norm, entered, gain_rows[0], gain_rows[1])
    normed_low = to_low(normed)
    key_low = to_low(product(normed_low, attend_low[1]))
    value_low = to_low(product(normed_low, attend_low[2]))
    key_all = jnp.concatenate([key_low, swap_core(key_low)], axis=0)
    value_all = jnp.concatenate([value_low, swap_core(value_low)], axis=0)
    query_low = to_low(product(normed_low, attend_low[0]))
    query_heads = query_low.reshape(halfway, HEADS, HD)
    key_heads = key_all.reshape(SEQ, HEADS, HD)
    value_heads = value_all.reshape(SEQ, HEADS, HD)
    scores = attention_scores(query_heads, key_heads, same_image)
    highest = jnp.max(scores, axis=-1, keepdims=True)
    exponent_rows = jnp.exp(scores - highest)
    row_total = jnp.sum(exponent_rows, axis=-1, keepdims=True)
    log_total = highest + jnp.log(row_total)
    attended = to_low(
        jnp.einsum(
            "hqk,khd->qhd",
            to_low(exponent_rows / row_total),
            value_heads,
            preferred_element_type=jnp.float32,
        ).reshape(halfway, D)
    )
    middle = entered + product(attended, attend_low[3])
    normed_two, second_back = jax.vjp(layer_norm, middle, gain_rows[2], gain_rows[3])
    normed_two_low = to_low(normed_two)
    hidden, gelu_back = jax.vjp(jax.nn.gelu, product_right(normed_two_low, expand_low[0]))
    hidden_low = to_low(hidden)
    output_rows = middle + product(hidden_low, expand_low[1])
    kept = (
        first_back,
        normed_low,
        query_low,
        key_all,
        value_all,
        log_total,
        attended,
        second_back,
        normed_two_low,
        gelu_back,
        hidden_low,
        expand_low,
    )
    return (output_rows, kept)


def block_backward(output_grad, kept, attend_low, flow, depth, image_row):
    (
        first_back,
        normed_low,
        query_low,
        key_all,
        value_all,
        log_total,
        attended,
        second_back,
        normed_two_low,
        gelu_back,
        hidden_low,
        expand_low,
    ) = kept
    halfway = attended.shape[0]
    copies = expand_low[0].shape[0] // D
    upper_low = to_low(output_grad)
    flow.begin(
        "upper%d" % depth,
        weight_task([(copies, hidden_low, [upper_low])], False, 0),
    )
    (hidden_grad,) = gelu_back(product_right(upper_low, expand_low[1]))
    hidden_grad_low = flow.tick(to_low(hidden_grad))
    middle_extra, gain_three, gain_four = second_back(product(hidden_grad_low, expand_low[0]))
    middle_grad = flow.tick(output_grad + middle_extra)
    projected_low = to_low(middle_grad)
    flow.begin(
        "lower%d" % depth,
        weight_task(
            [(copies, hidden_grad_low, [normed_two_low]), (1, attended, [projected_low])],
            False,
            0,
        ),
    )
    attended_grad = flow.tick(to_low(product_right(projected_low, attend_low[3])))
    query_grad, key_part, value_part = attention_back(
        query_low,
        key_all,
        value_all,
        attended_grad,
        log_total.reshape(HEADS, 1, halfway),
        image_row[:halfway],
        image_row,
    )
    key_part, value_part = flow.tick(key_part, value_part)
    value_grad = to_low(
        value_part[:halfway] + swap_core(to_low(value_part[halfway:])).astype(jnp.float32)
    )
    key_grad = to_low(
        key_part[:halfway] + swap_core(to_low(key_part[halfway:])).astype(jnp.float32)
    )
    query_grad, key_grad, value_grad = flow.tick(query_grad, key_grad, value_grad)
    flow.begin(
        "attend%d" % depth,
        weight_task([(1, normed_low, [query_grad, key_grad, value_grad])], False, 0, (), 1 + depth),
    )
    normed_grad = (
        product_right(query_grad, attend_low[0])
        + product_right(key_grad, attend_low[1])
        + product_right(value_grad, attend_low[2])
    )
    entered_extra, gain_one, gain_two = first_back(normed_grad)
    gain_delta = jnp.stack([gain_one, gain_two, gain_three, gain_four])
    return (flow.tick(middle_grad + entered_extra), gain_delta)


def newton_extra(gram_matrix):
    gram_low = to_low(gram_matrix)
    first_tail = newton_second * gram_matrix + newton_third * product(gram_low, gram_low)
    tail_low = to_low(first_tail)
    once = newton_first * gram_matrix + product(gram_low, tail_low)
    later = newton_first * once + product(to_low(once), tail_low)
    later_low = to_low(later)
    last_tail = newton_second * later + newton_third * product(later_low, later_low)
    return newton_first * (first_tail + last_tail) + product(tail_low, to_low(last_tail))


def padded(piece, rows, columns):
    lead = [(0, 0)] * (piece.ndim - 2)
    return jnp.pad(
        piece, (*lead, (0, rows - piece.shape[-2]), (0, columns - piece.shape[-1]))
    )


muon_counts = (4, 8, 8, 2, 1)


def first_owner():
    return lax.axis_size(("dp", "copy")) // 4


def owner_tables():
    devices, start = (lax.axis_size(("dp", "copy")), first_owner())

    def table(values, kind):
        return jnp.asarray([0] * start + values + [0] * (devices - start - len(values)), kind)

    return (
        table([1] * 12 + [0] * 11, jnp.float32),
        table([1] * 4 + [0] * 19, jnp.float32),
    )


def owner_buffer(modulate, expand, attend, dense, condition, rows, columns):
    devices, start = (lax.axis_size(("dp", "copy")), first_owner())
    groups = [jnp.zeros((start, rows, columns), jnp.bfloat16)]
    for given, count in zip((modulate, expand, attend, dense, condition), muon_counts):
        held = 0
        for member in given:
            if isinstance(member, int):
                groups.append(jnp.zeros((member, rows, columns), jnp.bfloat16))
                held += member
            else:
                groups.append(padded(to_low(member), rows, columns))
                held += member.shape[0]
        assert held == count
    groups.append(
        jnp.zeros((devices - start - sum(muon_counts), rows, columns), jnp.bfloat16)
    )
    return jnp.concatenate(groups, axis=0)


def in_parts(values, count):
    return values.reshape(-1, values.shape[-2] // count, values.shape[-1])


def muon_steps(moments):
    attend, expand, dense, modulate, condition = moments
    highest = max(
        modulate.shape[0] // 4,
        expand.shape[1] // 2,
        attend.shape[1],
        dense.shape[1],
        condition.shape[0],
    )
    held = lax.all_to_all(
        owner_buffer(
            [in_parts(modulate, 4)],
            [in_parts(expand, 2)],
            [attend],
            [dense],
            [condition[None]],
            highest,
            HW,
        ),
        ("dp", "copy"),
        0,
        0,
    )
    devices = held.shape[0]
    held = held.reshape(devices * highest, HW)
    core, me = (lax.axis_index("copy"), lax.axis_index(("dp", "copy")))
    shared_here, crossed_here = owner_tables()
    gram_matrix = product_left(held, held)
    gram_matrix = gram_matrix + shared_here[me] * swap_core(gram_matrix)
    chips = [(i, i ^ 1) for i in range(lax.axis_size("dp"))]
    near = lax.ppermute(to_low(columns_of(gram_matrix, core)), "dp", chips)
    far = swap_core(near)
    crossed = jnp.concatenate(
        [jnp.where(core == 0, near, far), jnp.where(core == 0, far, near)], axis=1
    )
    gram_matrix = gram_matrix + crossed_here[me] * crossed.astype(jnp.float32)
    rows = lax.broadcasted_iota(jnp.int32, gram_matrix.shape, 0)
    columns = lax.broadcasted_iota(jnp.int32, gram_matrix.shape, 1)
    trace = jnp.sum(jnp.where(rows == columns, gram_matrix, 0.0))
    scale_here = 1.0 / (jnp.sqrt(trace) + 1e-07)
    extra = newton_extra(gram_matrix * (scale_here * scale_here))
    result = to_low(product(held, to_low(extra)) * scale_here)
    back = lax.all_to_all(result.reshape(devices, highest, HW), ("dp", "copy"), 0, 0)
    squares = [
        jnp.sum((member * member).reshape(-1, *member.shape[-2:]), axis=(1, 2))
        for member in moments
    ]
    inverse = 1.0 / (jnp.sqrt(sum_all(jnp.concatenate(squares))) + 1e-07)
    scaled = newton_first * newton_first * inverse
    found, start = ([], first_owner())
    shapes = [moments[i].shape for i in (3, 1, 0, 2, 4)]
    for shape, count in zip(shapes, muon_counts):
        part = back[start : start + count]
        rows = math.prod(shape[:-1]) // count
        found.append(part[:, :rows, : shape[-1]].reshape(shape).astype(jnp.float32))
        start += count
    modulate, expand, attend, dense, condition = found
    return (
        scaled[:8, None, None] * moments[0] + attend,
        scaled[8:12, None, None] * moments[1] + expand,
        scaled[12:14, None, None] * moments[2] + dense,
        scaled[14] * moments[3] + modulate,
        scaled[15] * moments[4] + condition,
    )


def adam_shard(master, first, second, gradient):
    first_new = beta_first * first + (1.0 - beta_first) * gradient
    second_new = beta_second * second + (1.0 - beta_second) * gradient * gradient
    corrected_first = first_new / (1.0 - beta_first**STEP)
    corrected_second = second_new / (1.0 - beta_second**STEP)
    master_new = master - adam_rate * (
        corrected_first / (jnp.sqrt(corrected_second) + adam_floor) + adam_decay * master
    )
    return (master_new, first_new, second_new)


def per_device(
    patches,
    noise_copies,
    image_ids,
    buffer_flags,
    loss_mask,
    timesteps,
    attend_weight,
    attend_velocity,
    expand_weight,
    expand_velocity,
    dense_weight,
    dense_velocity,
    modulate_weight,
    modulate_velocity,
    condition_weight,
    condition_velocity,
    encoder_table,
    encoder_first,
    encoder_second,
    head_table,
    head_first,
    head_second,
):
    everywhere = ("dp", "copy")
    core = lax.axis_index("copy")
    flow = Flow()
    attend_low, expand_low, dense_low = (
        to_low(attend_weight),
        to_low(expand_weight),
        to_low(dense_weight),
    )
    rows, wide = (attend_weight.shape[1], dense_weight.shape[1])
    table_slots = -(-encoder_table.shape[0] // D)
    encoder_turned = padded(to_low(encoder_table).T, rows, table_slots * D)
    encoder_turned = encoder_turned.reshape(rows, table_slots, D).transpose(1, 0, 2)
    expand_slots = expand_low.reshape(expand_low.shape[0], -1, rows, D)
    copies = expand_slots.shape[1]

    def gathered(members):
        return lax.all_gather(jnp.concatenate(members, axis=0), everywhere, axis=1, tiled=True)

    entry_part = gathered([attend_low[:4], encoder_turned])
    later_part = gathered([expand_slots[0], expand_slots[1], attend_low[4:], *expand_slots[2:]])
    modulate_rows = modulate_weight.shape[0]
    head_part = lax.all_gather(
        jnp.concatenate(
            [
                to_low(modulate_weight),
                dense_low[0],
                dense_low[1],
                padded(to_low(condition_weight), wide, HW),
                padded(to_low(head_table).T, wide, HW),
            ],
            axis=0,
        )[None],
        everywhere,
        axis=0,
        tiled=True,
    )

    def rows_of(start, count):
        return head_part[:, start : start + count].reshape(-1, HW)

    attend_all = [entry_part[:4], later_part[2 * copies : 2 * copies + 4]]
    expand_all = [
        (
            member[: copies].reshape(copies * D, D),
            member[copies:].reshape(copies * D, D),
        )
        for member in (later_part[: 2 * copies], later_part[2 * copies + 4 :])
    ]
    encoder_all = jnp.concatenate([entry_part[4 + i] for i in range(table_slots)], axis=1).T[
        : encoder_table.shape[0]
    ]
    halfway = SEQ // 2
    offset = core * halfway

    def own_first(values):
        return jnp.where(
            core == 0, values, jnp.concatenate([values[halfway:], values[:halfway]], axis=0)
        )

    patch_seq = own_first(patches[0])
    image_row = own_first(image_ids[0])
    buffer_row = own_first(buffer_flags[0])
    masked_row = own_first(loss_mask[0])
    weight_row = (masked_row * (1 - buffer_row)).astype(jnp.float32)
    token_count = sum_all(jnp.sum(weight_row))
    step_float = own_first(timesteps[0, 0]).astype(jnp.float32)
    alpha_row = alpha_bar(step_float)[:, None]
    target = own_first(noise_copies[0, 0]).astype(jnp.float32)
    noisy_low = to_low(
        jnp.sqrt(alpha_row) * patch_seq.astype(jnp.float32) + jnp.sqrt(1.0 - alpha_row) * target
    )
    feature_low = to_low(time_features(step_float))
    encoder_all, noisy_low, feature_low, target = lax.optimization_barrier(
        (encoder_all, noisy_low, feature_low, target)
    )
    own_patch = patch_seq[:halfway]
    buffer_on = buffer_row[:halfway, None] > 0
    masked_on = masked_row[:halfway, None] > 0
    same_image = image_row[:halfway, None] == image_row[None, :]
    gain_rows = encoder_all[:12].astype(jnp.float32)
    position = lax.dynamic_slice_in_dim(encoder_all, 12 + PATCH + offset, halfway, 0).astype(
        jnp.float32
    )
    embedded = product(own_patch, encoder_all[12 : 12 + PATCH])

    def entry(embedded_rows, token_pair, position_rows):
        return (
            jnp.where(buffer_on, token_pair[1], jnp.where(masked_on, token_pair[0], embedded_rows))
            + position_rows
        )

    entered, entry_back = jax.vjp(entry, embedded, gain_rows[10:12], position)
    state_rows = entered
    kept_all = []
    for depth_index in range(2):
        state_rows, kept = block_forward(
            state_rows,
            attend_all[depth_index],
            expand_all[depth_index],
            flow,
            gain_rows[4 * depth_index : 4 * depth_index + 4],
            same_image,
        )
        kept_all.append(kept)
    state_rows, head_part = lax.optimization_barrier((state_rows, head_part))
    modulate_all = rows_of(0, modulate_rows)
    dense_all = [rows_of(modulate_rows, wide), rows_of(modulate_rows + wide, wide)]
    condition_all = rows_of(modulate_rows + 2 * wide, wide)[:, :D]
    head_all = rows_of(modulate_rows + 3 * wide, wide)[:, : head_table.shape[0]].T
    latent, third_back = jax.vjp(layer_norm, state_rows, gain_rows[8], gain_rows[9])
    latent_low = to_low(latent)
    condition_own = to_low(product_right(latent_low, condition_all))
    condition_rows = jnp.concatenate([condition_own, swap_core(condition_own)], axis=0)
    lifted = product(noisy_low, head_all[:PATCH])
    summed = condition_rows.astype(jnp.float32) + product(
        feature_low, head_all[PATCH : PATCH + FREQ]
    )
    activated, silu_back = jax.vjp(jax.nn.silu, summed)
    activated_low = to_low(activated)
    modulation = product_right(activated_low, modulate_all)
    inner_rows, inner_back = jax.vjp(first_modulate, lifted, modulation)
    inner_low = to_low(inner_rows)
    expanded, dense_back = jax.vjp(jax.nn.gelu, product(inner_low, dense_all[0]))
    expanded_low = to_low(expanded)
    branch = product(expanded_low, dense_all[1])
    outer_rows, outer_back = jax.vjp(last_modulate, lifted, modulation, branch)
    outer_low = to_low(outer_rows)
    predicted = product_right(outer_low, head_all[PATCH + FREQ :])
    residue = predicted - target
    loss_local = jnp.sum(weight_row[:, None] * residue * residue) / PATCH
    predicted_grad = to_low(2.0 * weight_row[:, None] * residue / (PATCH * token_count))
    final_turned = product_left(outer_low, predicted_grad)
    lifted_grad, modulation_grad, branch_grad = outer_back(
        product(predicted_grad, head_all[PATCH + FREQ :])
    )
    branch_low = to_low(branch_grad)
    (expanded_grad,) = dense_back(product_right(branch_low, dense_all[1]))
    expanded_grad_low = to_low(expanded_grad)
    lifted_extra, modulation_extra = inner_back(product_right(expanded_grad_low, dense_all[0]))
    modulation_low = flow.tick(to_low(modulation_grad + modulation_extra))
    flow.begin(
        "spread",
        split_weight_task(modulation_low, activated_low, flow, ("modulate.2", "modulate.3")),
    )
    (summed_grad,) = silu_back(product(modulation_low, modulate_all))
    time_turned = product_left(to_low(summed_grad), feature_low)
    lift_turned = product_left(to_low(lifted_grad + lifted_extra), noisy_low)
    head_turned_grad = jnp.concatenate([lift_turned, time_turned, final_turned], axis=1)
    condition_grad = to_low(
        summed_grad[:halfway] + swap_core(to_low(summed_grad[halfway:])).astype(jnp.float32)
    )
    condition_grad = flow.tick(condition_grad)
    flow.begin(
        "head",
        weight_task(
            [
                (1, inner_low, [expanded_grad_low]),
                (1, expanded_low, [branch_low]),
                (1, condition_grad, [latent_low]),
            ],
            True,
            -1,
            [head_turned_grad],
            3,
        ),
    )
    state_grad, gain_nine, gain_ten = third_back(product(condition_grad, condition_all))

    def modulate_whole():
        (left_parts,), (right_parts,) = (flow.results["modulate.2"], flow.results["modulate.3"])
        quarters = [left_parts[0], right_parts[0], left_parts[1], right_parts[1]]
        return jnp.concatenate(quarters, axis=-1)[0]

    def attend_whole(depth):
        lower = flow.results["lower%d" % depth]
        return jnp.concatenate([*flow.results["attend%d" % depth], lower[1]], axis=0)

    def expand_whole(depth):
        lower, upper = (flow.results["lower%d" % depth], flow.results["upper%d" % depth])
        return jnp.stack([lower[0].reshape(-1, D), upper[0].reshape(-1, D)])

    def dense_whole():
        return jnp.concatenate(flow.results["head"][:2], axis=0)

    gain_parts = [None, None]
    for depth_index in (1, 0):
        state_grad, gain_parts[depth_index] = block_backward(
            state_grad,
            kept_all[depth_index],
            attend_all[depth_index],
            flow,
            depth_index,
            image_row,
        )
    embedded_grad, token_grad, position_grad = entry_back(state_grad)
    embed_delta = product_left(own_patch, to_low(embedded_grad))
    small_delta = jnp.concatenate(
        [
            gain_parts[0],
            gain_parts[1],
            jnp.stack([gain_nine, gain_ten]),
            token_grad,
            embed_delta,
        ],
        axis=0,
    )
    small_delta = small_delta + swap_core(small_delta)
    small_half = small_delta.shape[0] // 2
    small_own = lax.dynamic_slice_in_dim(small_delta, core * small_half, small_half, 0)
    flow.begin(
        "encoder",
        scatter_task([small_own.T[None], position_grad.T[None]], True, -1, [True, False], 1),
    )
    small_pair, position_pair = flow.take("encoder")[0]
    encoder_delta = jnp.concatenate([*small_pair, *position_pair], axis=-1)[0].T
    blocks = [name + str(i) for i in range(2) for name in ("upper", "lower", "attend")]
    flow.take("head", "modulate.2", "modulate.3", *blocks)
    reduced = (
        jnp.concatenate([attend_whole(0), attend_whole(1)], axis=0),
        jnp.concatenate([expand_whole(0), expand_whole(1)], axis=0),
        dense_whole(),
        modulate_whole(),
        flow.results["head"][2][0],
        encoder_delta,
        flow.results["head"][3][0].T,
    )
    velocities = (
        attend_velocity,
        expand_velocity,
        dense_velocity,
        modulate_velocity,
        condition_velocity,
    )

    squares = sum((jnp.sum(member * member) for member in reduced))
    totals = sum_all(jnp.stack([squares, loss_local]))
    square_total, loss_sum = (totals[0], totals[1])
    clip_norm = jnp.sqrt(square_total)
    factor = jnp.minimum(1.0, clip_bound / (clip_norm + 1e-06))
    moments = tuple((muon_keep * velocities[i] + factor * reduced[i] for i in range(5)))
    current = muon_steps(moments)
    devices = lax.axis_size(everywhere)
    masters = (attend_weight, expand_weight, dense_weight, modulate_weight, condition_weight)
    updated = tuple(
        (
            masters[i] * (1.0 - muon_rate * muon_decay)
            - muon_rate
            * max(1.0, current[i].shape[-2] * devices / current[i].shape[-1]) ** 0.5
            * current[i]
            for i in range(5)
        )
    )
    encoder_master, encoder_firsts, encoder_seconds = adam_shard(
        encoder_table, encoder_first, encoder_second, factor * reduced[5]
    )
    table_master, table_firsts, table_seconds = adam_shard(
        head_table, head_first, head_second, factor * reduced[6]
    )
    return (
        loss_sum,
        token_count,
        clip_norm,
        updated[0],
        moments[0],
        updated[1],
        moments[1],
        updated[2],
        moments[2],
        updated[3],
        moments[3],
        updated[4],
        moments[4],
        encoder_master,
        encoder_firsts,
        encoder_seconds,
        table_master,
        table_firsts,
        table_seconds,
    )


def solution(mesh):
    placed = (
        P("dp", None, None),
        P("copy", "dp", None, None),
        P("dp", None),
        P("dp", None),
        P("dp", None),
        P("copy", "dp", None),
        P(None, ("dp", "copy"), None),
        P(None, ("dp", "copy"), None),
        P(None, ("dp", "copy"), None),
        P(None, ("dp", "copy"), None),
        P(None, ("dp", "copy"), None),
        P(None, ("dp", "copy"), None),
        P(("dp", "copy"), None),
        P(("dp", "copy"), None),
        P(("dp", "copy"), None),
        P(("dp", "copy"), None),
        P(None, ("dp", "copy")),
        P(None, ("dp", "copy")),
        P(None, ("dp", "copy")),
        P(None, ("dp", "copy")),
        P(None, ("dp", "copy")),
        P(None, ("dp", "copy")),
    )
    return jax.shard_map(
        per_device,
        mesh=mesh,
        in_specs=placed,
        out_specs=(
            P(),
            P(),
            P(),
            P(None, ("dp", "copy"), None),
            P(None, ("dp", "copy"), None),
            P(None, ("dp", "copy"), None),
            P(None, ("dp", "copy"), None),
            P(None, ("dp", "copy"), None),
            P(None, ("dp", "copy"), None),
            P(("dp", "copy"), None),
            P(("dp", "copy"), None),
            P(("dp", "copy"), None),
            P(("dp", "copy"), None),
            P(None, ("dp", "copy")),
            P(None, ("dp", "copy")),
            P(None, ("dp", "copy")),
            P(None, ("dp", "copy")),
            P(None, ("dp", "copy")),
            P(None, ("dp", "copy")),
        ),
        check_vma=False,
    )
```

```python
import math

import jax
import jax.numpy as jnp
from jax import lax
from jax.experimental import pallas as pl
from jax.experimental.pallas import tpu as pltpu
from jax.sharding import PartitionSpec as P

D = 768
HEADS = 12
HD = 64
HW = 1024
PATCH = 64
FREQ = 256
SEQ = 1024
NS_STEPS = 2
STEP = 10
TSTEPS = 1000


precise_mode = lax.Precision.HIGHEST
norm_floor = 1e-06
score_factor = 0.125
newton_first = 3.4445
newton_second = -4.775
newton_third = 2.0315
muon_rate = 1.0
muon_decay = 0.01
muon_keep = 0.95
clip_bound = 0.001
adam_rate = 0.02
beta_first = 0.9
beta_second = 0.95
adam_floor = 1e-08
adam_decay = 0.1


def product(left_side, right_side):
    return jnp.dot(left_side, right_side, preferred_element_type=jnp.float32)


def product_left(left_side, right_side):
    return lax.dot_general(
        left_side, right_side, (((0,), (0,)), ((), ())), preferred_element_type=jnp.float32
    )


def product_right(left_side, right_side):
    return lax.dot_general(
        left_side, right_side, (((1,), (1,)), ((), ())), preferred_element_type=jnp.float32
    )


def to_low(values):
    return values.astype(jnp.bfloat16)


def layer_norm(values, gain_row, bias_row):
    centered = values - jnp.mean(values, axis=-1, keepdims=True)
    spread = jnp.mean(centered * centered, axis=-1, keepdims=True)
    return centered * lax.rsqrt(spread + norm_floor) * gain_row + bias_row


def plain_norm(values):
    centered = values - jnp.mean(values, axis=-1, keepdims=True)
    spread = jnp.mean(centered * centered, axis=-1, keepdims=True)
    return centered * lax.rsqrt(spread + norm_floor)


def alpha_bar(step_float):
    return jnp.cos(0.5 * math.pi * (step_float + 0.5) / TSTEPS) ** 2


def time_features(step_float):
    halfway = FREQ // 2
    frequency = jnp.exp(-math.log(10000.0) * jnp.arange(halfway).astype(jnp.float32) / halfway)
    angles = step_float[:, None] * frequency[None, :]
    return jnp.concatenate([jnp.cos(angles), jnp.sin(angles)], axis=1)


def first_modulate(lifted, modulation):
    return plain_norm(lifted) * (1.0 + modulation[:, HW : 2 * HW]) + modulation[:, :HW]


def last_modulate(lifted, modulation, branch):
    joined = lifted + modulation[:, 2 * HW : 3 * HW] * branch
    return plain_norm(joined) * (1.0 + modulation[:, 4 * HW :]) + modulation[:, 3 * HW : 4 * HW]


def grid_of(count):
    side = 1
    while 2 * side**3 < count:
        side *= 2
    if 2 * side**3 == count:
        return (2 * side, side, side)
    return (count, 1, 1)


def swap_core(values):
    return lax.ppermute(values, "copy", [(0, 1), (1, 0)])


def sum_all(values):
    values = values + swap_core(values)
    count = lax.axis_size("dp")
    if count & (count - 1):
        return lax.psum(values, "dp")
    step = 1
    while step < count:
        values = values + lax.ppermute(values, "dp", [(i, i ^ step) for i in range(count)])
        step *= 2
    return values


class Flow:
    def __init__(self):
        self.live, self.results = ([], {})

    def begin(self, name, task):
        self.live.append([name, task, *next(task)])

    def tick(self, *carry):
        due = [entry for entry in self.live if entry[3] <= 1]
        for entry in self.live:
            entry[3] -= 1
        carry, arrived = lax.optimization_barrier((carry, [entry[2] for entry in due]))
        for entry, values in zip(due, arrived):
            try:
                entry[2], entry[3] = entry[1].send(values)
            except StopIteration as stop:
                self.results[entry[0]] = stop.value
                self.live.remove(entry)
        return carry if len(carry) > 1 else (carry[0] if carry else None)

    def take(self, *names):
        while any(name not in self.results for name in names):
            self.tick()
        return [self.results[name] for name in names]


def columns_of(values, core):
    half = values.shape[-1] // 2
    return lax.dynamic_slice_in_dim(values, core * half, half, values.ndim - 1)


def joined(parts, axis):
    return parts[0] if len(parts) == 1 else jnp.concatenate(parts, axis=axis)


def bits_in_order(crossed):
    grid = grid_of(lax.axis_size("dp"))
    counts = [size.bit_length() - 1 for size in grid]
    z_bits = list(range(counts[2] + counts[1], sum(counts)))
    y_bits = list(range(counts[2], counts[2] + counts[1]))
    x_bits = list(range(counts[2]))
    return (y_bits + x_bits if crossed else x_bits + y_bits) + z_bits


def scatter_task(parts, crossed, axis, exact, lag=2):
    core = lax.axis_index("copy")
    here = lax.axis_index("dp")
    chips = lax.axis_size("dp")
    sizes = [part.shape[axis] for part in parts]
    order = bits_in_order(crossed)
    parts = [
        part.reshape(
            part.shape[0], *[2] * len(order), part.shape[1] // chips, part.shape[2]
        )
        for part in parts
    ]
    left = sorted(order, reverse=True)
    for bit in order:
        position, mine = (1 + left.index(bit), here // 2**bit % 2)
        sent = []
        for part, keep in zip(parts, exact):
            half = lax.dynamic_index_in_dim(part, 1 - mine, position, keepdims=False)
            if keep:
                near = lax.reduce_precision(half, 8, 7)
                sent += [to_low(near), to_low(half - near)]
            else:
                sent.append(to_low(half))
        pairs = [(i, i ^ 2**bit) for i in range(chips)]
        (arrived,) = yield ([lax.ppermute(joined(sent, axis), "dp", pairs)], lag)
        start, totals = (0, [])
        for part, keep, size in zip(parts, exact, sizes):
            total = lax.dynamic_index_in_dim(part, mine, position, keepdims=False)
            for number in range(2 if keep else 1):
                piece = lax.slice_in_dim(
                    arrived, start, start + size, axis=axis % arrived.ndim
                )
                total = total + piece.astype(jnp.float32)
                start += size
            totals.append(total)
        parts = totals
        left.remove(bit)
    values = joined(parts, axis)
    half = values.shape[1] // 2
    mine = lax.dynamic_slice_in_dim(values, core * half, half, 1)
    (arrived,) = yield (
        [swap_core(lax.dynamic_slice_in_dim(values, (1 - core) * half, half, 1))],
        1,
    )
    first = jnp.where(core == 0, mine, arrived)
    last = jnp.where(core == 0, arrived, mine)
    starts = [sum(sizes[:i]) for i in range(len(sizes))]
    return [
        tuple(lax.slice_in_dim(m, start, start + size, axis=axis % m.ndim) for m in (first, last))
        for start, size in zip(starts, sizes)
    ]


def weight_task(products, crossed, axis, tables=(), lag=2):
    core = lax.axis_index("copy")

    def some(right_sides, which):
        return joined([columns_of(right, which) for right in right_sides], 1)

    sent = [product_left(left, some(rights, 1 - core)) for slots, left, rights in products]
    sent += [columns_of(table, 1 - core) for table in tables]
    arrived = yield ([swap_core(part) for part in sent], 1)
    totals = [
        product_left(left, some(rights, core)) + part
        for (slots, left, rights), part in zip(products, arrived)
    ]
    totals = [
        total.reshape(member[0], total.shape[0] // member[0], total.shape[1])
        for total, member in zip(totals, products)
    ]
    for table, part in zip(tables, arrived[len(products) :]):
        totals.append((columns_of(table, core) + part)[None])
    exact = [False] * len(products) + [True] * len(tables)
    halves = yield from scatter_task(totals, crossed, axis, exact, lag)
    found = []
    counts = [len(member[2]) for member in products] + [1] * len(tables)
    for (first, last), count in zip(halves, counts):
        width = first.shape[-1] // count
        for i in range(count):
            pair = [m[..., i * width : (i + 1) * width] for m in (first, last)]
            found.append(jnp.concatenate(pair, axis=-1))
    return found


def split_weight_task(left_side, right_side, flow, names):
    core = lax.axis_index("copy")
    (arrived,) = yield ([swap_core(product_left(left_side, columns_of(right_side, 1 - core)))], 1)
    total = (product_left(left_side, columns_of(right_side, core)) + arrived)[None]
    quarter = total.shape[-1] // 2
    flow.begin(names[0], scatter_task([total[..., :quarter]], False, 0, [False], 3))
    flow.begin(names[1], scatter_task([total[..., quarter:]], True, 0, [False], 3))
    return None


def attention_back_kernel(
    query_ref, key_ref, value_ref, grad_ref, log_ref, query_id, key_id, dq_ref, dk_ref, dv_ref
):
    same = key_id[...] == query_id[...]
    query, key, value, grad = (query_ref[...], key_ref[...], value_ref[...], grad_ref[...])
    width = query.shape[1]
    lane = lax.broadcasted_iota(jnp.int32, (1, width), 1)
    query_grad, key_grad, value_grad = (None, None, None)
    for head in range(width // HD):
        inside = jnp.where((lane >= head * HD) & (lane < (head + 1) * HD), 1.0, 0.0)
        query_here = to_low(query.astype(jnp.float32) * inside)
        grad_here = to_low(grad.astype(jnp.float32) * inside)
        key_here = to_low(key.astype(jnp.float32) * inside)
        scores = product_right(key, query_here) * score_factor
        chance = jnp.where(same, jnp.exp(scores - log_ref[head]), 0.0)
        soft_grad = product_right(value, grad_here)
        total = jnp.sum(chance * soft_grad, axis=0, keepdims=True)
        score_low = to_low(chance * (soft_grad - total) * score_factor)
        parts = (
            product_left(key_here, score_low),
            product(score_low, query_here),
            product(to_low(chance), grad_here),
        )
        if head == 0:
            query_grad, key_grad, value_grad = parts
        else:
            query_grad, key_grad, value_grad = (
                query_grad + parts[0],
                key_grad + parts[1],
                value_grad + parts[2],
            )
    dq_ref[...] = to_low(query_grad.T)
    first = pl.program_id(1) == 0

    @pl.when(first)
    def _():
        dk_ref[...] = key_grad
        dv_ref[...] = value_grad

    @pl.when(jnp.logical_not(first))
    def _():
        dk_ref[...] += key_grad
        dv_ref[...] += value_grad


def attention_back(query, key, value, grad, log_total, query_ids, key_ids):
    queries, keys = (query.shape[0], key.shape[0])
    width, chunk = (2 * HD, 256)
    own = pl.BlockSpec((chunk, width), lambda pair, part: (part, pair))
    whole = pl.BlockSpec((keys, width), lambda pair, part: (0, pair))
    return pl.pallas_call(
        attention_back_kernel,
        grid=(D // width, queries // chunk),
        in_specs=[
            own,
            whole,
            whole,
            own,
            pl.BlockSpec((2, 1, chunk), lambda pair, part: (pair, 0, part)),
            pl.BlockSpec((1, chunk), lambda pair, part: (0, part)),
            pl.BlockSpec((keys, 1), lambda pair, part: (0, 0)),
        ],
        out_specs=[own, whole, whole],
        out_shape=[
            jax.ShapeDtypeStruct((queries, D), jnp.bfloat16),
            jax.ShapeDtypeStruct((keys, D), jnp.float32),
            jax.ShapeDtypeStruct((keys, D), jnp.float32),
        ],
        compiler_params=pltpu.CompilerParams(vmem_limit_bytes=48 * 2**20),
        cost_estimate=pl.CostEstimate(
            flops=10 * queries * keys * D * 2,
            bytes_accessed=12 * keys * D,
            transcendentals=queries * keys * HEADS,
        ),
    )(query, key, value, grad, log_total, query_ids[None, :], key_ids[:, None])


def attention_scores(query_heads, key_heads, same_image):
    raw_scores = jnp.einsum(
        "qhd,khd->hqk", query_heads, key_heads, preferred_element_type=jnp.float32
    )
    return jnp.where(same_image[None], raw_scores * score_factor, -1e30)


def block_forward(entered, attend_low, expand_low, flow, gain_rows, same_image):
    halfway = entered.shape[0]
    normed, first_back = jax.vjp(layer_norm, entered, gain_rows[0], gain_rows[1])
    normed_low = to_low(normed)
    key_low = to_low(product(normed_low, attend_low[1]))
    value_low = to_low(product(normed_low, attend_low[2]))
    key_all = jnp.concatenate([key_low, swap_core(key_low)], axis=0)
    value_all = jnp.concatenate([value_low, swap_core(value_low)], axis=0)
    query_low = to_low(product(normed_low, attend_low[0]))
    query_heads = query_low.reshape(halfway, HEADS, HD)
    key_heads = key_all.reshape(SEQ, HEADS, HD)
    value_heads = value_all.reshape(SEQ, HEADS, HD)
    scores = attention_scores(query_heads, key_heads, same_image)
    highest = jnp.max(scores, axis=-1, keepdims=True)
    exponent_rows = jnp.exp(scores - highest)
    row_total = jnp.sum(exponent_rows, axis=-1, keepdims=True)
    log_total = highest + jnp.log(row_total)
    attended = to_low(
        jnp.einsum(
            "hqk,khd->qhd",
            to_low(exponent_rows / row_total),
            value_heads,
            preferred_element_type=jnp.float32,
        ).reshape(halfway, D)
    )
    middle = entered + product(attended, attend_low[3])
    normed_two, second_back = jax.vjp(layer_norm, middle, gain_rows[2], gain_rows[3])
    normed_two_low = to_low(normed_two)
    hidden, gelu_back = jax.vjp(jax.nn.gelu, product_right(normed_two_low, expand_low[0]))
    hidden_low = to_low(hidden)
    output_rows = middle + product(hidden_low, expand_low[1])
    kept = (
        first_back,
        normed_low,
        query_low,
        key_all,
        value_all,
        log_total,
        attended,
        second_back,
        normed_two_low,
        gelu_back,
        hidden_low,
        expand_low,
    )
    return (output_rows, kept)


def block_backward(output_grad, kept, attend_low, flow, depth, image_row):
    (
        first_back,
        normed_low,
        query_low,
        key_all,
        value_all,
        log_total,
        attended,
        second_back,
        normed_two_low,
        gelu_back,
        hidden_low,
        expand_low,
    ) = kept
    halfway = attended.shape[0]
    copies = expand_low[0].shape[0] // D
    upper_low = to_low(output_grad)
    flow.begin(
        "upper%d" % depth,
        weight_task([(copies, hidden_low, [upper_low])], False, 0, (), 2 + depth),
    )
    (hidden_grad,) = gelu_back(product_right(upper_low, expand_low[1]))
    hidden_grad_low = flow.tick(to_low(hidden_grad))
    middle_extra, gain_three, gain_four = second_back(product(hidden_grad_low, expand_low[0]))
    middle_grad = flow.tick(output_grad + middle_extra)
    projected_low = to_low(middle_grad)
    flow.begin(
        "lower%d" % depth,
        weight_task(
            [(copies, hidden_grad_low, [normed_two_low]), (1, attended, [projected_low])],
            False,
            0,
            (),
            2 + depth,
        ),
    )
    attended_grad = flow.tick(to_low(product_right(projected_low, attend_low[3])))
    query_grad, key_part, value_part = attention_back(
        query_low,
        key_all,
        value_all,
        attended_grad,
        log_total.reshape(HEADS, 1, halfway),
        image_row[:halfway],
        image_row,
    )
    key_part, value_part = flow.tick(key_part, value_part)
    value_grad = to_low(
        value_part[:halfway] + swap_core(to_low(value_part[halfway:])).astype(jnp.float32)
    )
    key_grad = to_low(
        key_part[:halfway] + swap_core(to_low(key_part[halfway:])).astype(jnp.float32)
    )
    query_grad, key_grad, value_grad = flow.tick(query_grad, key_grad, value_grad)
    flow.begin(
        "attend%d" % depth,
        weight_task([(1, normed_low, [query_grad, key_grad, value_grad])], False, 0, (), 1 + depth),
    )
    normed_grad = (
        product_right(query_grad, attend_low[0])
        + product_right(key_grad, attend_low[1])
        + product_right(value_grad, attend_low[2])
    )
    entered_extra, gain_one, gain_two = first_back(normed_grad)
    gain_delta = jnp.stack([gain_one, gain_two, gain_three, gain_four])
    return (flow.tick(middle_grad + entered_extra), gain_delta)


def newton_extra(gram_matrix):
    gram_low = to_low(gram_matrix)
    first_tail = newton_second * gram_matrix + newton_third * product(gram_low, gram_low)
    tail_low = to_low(first_tail)
    once = newton_first * gram_matrix + product(gram_low, tail_low)
    later = newton_first * once + product(to_low(once), tail_low)
    later_low = to_low(later)
    last_tail = newton_second * later + newton_third * product(later_low, later_low)
    return newton_first * (first_tail + last_tail) + product(tail_low, to_low(last_tail))


def padded(piece, rows, columns):
    lead = [(0, 0)] * (piece.ndim - 2)
    return jnp.pad(
        piece, (*lead, (0, rows - piece.shape[-2]), (0, columns - piece.shape[-1]))
    )


muon_counts = (4, 8, 8, 2, 1)


def first_owner():
    return lax.axis_size(("dp", "copy")) // 4


def owner_tables():
    devices, start = (lax.axis_size(("dp", "copy")), first_owner())

    def table(values, kind):
        return jnp.asarray([0] * start + values + [0] * (devices - start - len(values)), kind)

    return (
        table([1] * 12 + [0] * 11, jnp.float32),
        table([1] * 4 + [0] * 19, jnp.float32),
    )


def owner_buffer(modulate, expand, attend, dense, condition, rows, columns):
    devices, start = (lax.axis_size(("dp", "copy")), first_owner())
    groups = [jnp.zeros((start, rows, columns), jnp.bfloat16)]
    for given, count in zip((modulate, expand, attend, dense, condition), muon_counts):
        held = 0
        for member in given:
            if isinstance(member, int):
                groups.append(jnp.zeros((member, rows, columns), jnp.bfloat16))
                held += member
            else:
                groups.append(padded(to_low(member), rows, columns))
                held += member.shape[0]
        assert held == count
    groups.append(
        jnp.zeros((devices - start - sum(muon_counts), rows, columns), jnp.bfloat16)
    )
    return jnp.concatenate(groups, axis=0)


def in_parts(values, count):
    return values.reshape(-1, values.shape[-2] // count, values.shape[-1])


def muon_steps(moments):
    attend, expand, dense, modulate, condition = moments
    highest = max(
        modulate.shape[0] // 4,
        expand.shape[1] // 2,
        attend.shape[1],
        dense.shape[1],
        condition.shape[0],
    )
    held = lax.all_to_all(
        owner_buffer(
            [in_parts(modulate, 4)],
            [in_parts(expand, 2)],
            [attend],
            [dense],
            [condition[None]],
            highest,
            HW,
        ),
        ("dp", "copy"),
        0,
        0,
    )
    devices = held.shape[0]
    held = held.reshape(devices * highest, HW)
    core, me = (lax.axis_index("copy"), lax.axis_index(("dp", "copy")))
    shared_here, crossed_here = owner_tables()
    gram_matrix = product_left(held, held)
    gram_matrix = gram_matrix + shared_here[me] * swap_core(gram_matrix)
    chips = [(i, i ^ 1) for i in range(lax.axis_size("dp"))]
    near = lax.ppermute(to_low(columns_of(gram_matrix, core)), "dp", chips)
    far = swap_core(near)
    crossed = jnp.concatenate(
        [jnp.where(core == 0, near, far), jnp.where(core == 0, far, near)], axis=1
    )
    gram_matrix = gram_matrix + crossed_here[me] * crossed.astype(jnp.float32)
    rows = lax.broadcasted_iota(jnp.int32, gram_matrix.shape, 0)
    columns = lax.broadcasted_iota(jnp.int32, gram_matrix.shape, 1)
    trace = jnp.sum(jnp.where(rows == columns, gram_matrix, 0.0))
    scale_here = 1.0 / (jnp.sqrt(trace) + 1e-07)
    extra = newton_extra(gram_matrix * (scale_here * scale_here))
    result = to_low(product(held, to_low(extra)) * scale_here)
    back = lax.all_to_all(result.reshape(devices, highest, HW), ("dp", "copy"), 0, 0)
    squares = [
        jnp.sum((member * member).reshape(-1, *member.shape[-2:]), axis=(1, 2))
        for member in moments
    ]
    inverse = 1.0 / (jnp.sqrt(sum_all(jnp.concatenate(squares))) + 1e-07)
    scaled = newton_first * newton_first * inverse
    found, start = ([], first_owner())
    shapes = [moments[i].shape for i in (3, 1, 0, 2, 4)]
    for shape, count in zip(shapes, muon_counts):
        part = back[start : start + count]
        rows = math.prod(shape[:-1]) // count
        found.append(part[:, :rows, : shape[-1]].reshape(shape).astype(jnp.float32))
        start += count
    modulate, expand, attend, dense, condition = found
    return (
        scaled[:8, None, None] * moments[0] + attend,
        scaled[8:12, None, None] * moments[1] + expand,
        scaled[12:14, None, None] * moments[2] + dense,
        scaled[14] * moments[3] + modulate,
        scaled[15] * moments[4] + condition,
    )


def adam_shard(master, first, second, gradient):
    first_new = beta_first * first + (1.0 - beta_first) * gradient
    second_new = beta_second * second + (1.0 - beta_second) * gradient * gradient
    corrected_first = first_new / (1.0 - beta_first**STEP)
    corrected_second = second_new / (1.0 - beta_second**STEP)
    master_new = master - adam_rate * (
        corrected_first / (jnp.sqrt(corrected_second) + adam_floor) + adam_decay * master
    )
    return (master_new, first_new, second_new)


def per_device(
    patches,
    noise_copies,
    image_ids,
    buffer_flags,
    loss_mask,
    timesteps,
    attend_weight,
    attend_velocity,
    expand_weight,
    expand_velocity,
    dense_weight,
    dense_velocity,
    modulate_weight,
    modulate_velocity,
    condition_weight,
    condition_velocity,
    encoder_table,
    encoder_first,
    encoder_second,
    head_table,
    head_first,
    head_second,
):
    everywhere = ("dp", "copy")
    core = lax.axis_index("copy")
    flow = Flow()
    attend_low, expand_low, dense_low = (
        to_low(attend_weight),
        to_low(expand_weight),
        to_low(dense_weight),
    )
    rows, wide = (attend_weight.shape[1], dense_weight.shape[1])
    table_slots = -(-encoder_table.shape[0] // D)
    encoder_turned = padded(to_low(encoder_table).T, rows, table_slots * D)
    encoder_turned = encoder_turned.reshape(rows, table_slots, D).transpose(1, 0, 2)
    expand_slots = expand_low.reshape(expand_low.shape[0], -1, rows, D)
    copies = expand_slots.shape[1]

    def gathered(members):
        return lax.all_gather(jnp.concatenate(members, axis=0), everywhere, axis=1, tiled=True)

    entry_part = gathered([attend_low[:4], encoder_turned])
    later_part = gathered([expand_slots[0], expand_slots[1], attend_low[4:], *expand_slots[2:]])
    modulate_rows = modulate_weight.shape[0]
    head_part = lax.all_gather(
        jnp.concatenate(
            [
                to_low(modulate_weight),
                dense_low[0],
                dense_low[1],
                padded(to_low(condition_weight), wide, HW),
                padded(to_low(head_table).T, wide, HW),
            ],
            axis=0,
        )[None],
        everywhere,
        axis=0,
        tiled=True,
    )

    def rows_of(start, count):
        return head_part[:, start : start + count].reshape(-1, HW)

    attend_all = [entry_part[:4], later_part[2 * copies : 2 * copies + 4]]
    expand_all = [
        (
            member[: copies].reshape(copies * D, D),
            member[copies:].reshape(copies * D, D),
        )
        for member in (later_part[: 2 * copies], later_part[2 * copies + 4 :])
    ]
    encoder_all = jnp.concatenate([entry_part[4 + i] for i in range(table_slots)], axis=1).T[
        : encoder_table.shape[0]
    ]
    halfway = SEQ // 2
    offset = core * halfway

    def own_first(values):
        return jnp.where(
            core == 0, values, jnp.concatenate([values[halfway:], values[:halfway]], axis=0)
        )

    patch_seq = own_first(patches[0])
    image_row = own_first(image_ids[0])
    buffer_row = own_first(buffer_flags[0])
    masked_row = own_first(loss_mask[0])
    weight_row = (masked_row * (1 - buffer_row)).astype(jnp.float32)
    token_count = sum_all(jnp.sum(weight_row))
    step_float = own_first(timesteps[0, 0]).astype(jnp.float32)
    alpha_row = alpha_bar(step_float)[:, None]
    target = own_first(noise_copies[0, 0]).astype(jnp.float32)
    noisy_low = to_low(
        jnp.sqrt(alpha_row) * patch_seq.astype(jnp.float32) + jnp.sqrt(1.0 - alpha_row) * target
    )
    feature_low = to_low(time_features(step_float))
    encoder_all, noisy_low, feature_low, target = lax.optimization_barrier(
        (encoder_all, noisy_low, feature_low, target)
    )
    own_patch = patch_seq[:halfway]
    buffer_on = buffer_row[:halfway, None] > 0
    masked_on = masked_row[:halfway, None] > 0
    same_image = image_row[:halfway, None] == image_row[None, :]
    gain_rows = encoder_all[:12].astype(jnp.float32)
    position = lax.dynamic_slice_in_dim(encoder_all, 12 + PATCH + offset, halfway, 0).astype(
        jnp.float32
    )
    embedded = product(own_patch, encoder_all[12 : 12 + PATCH])

    def entry(embedded_rows, token_pair, position_rows):
        return (
            jnp.where(buffer_on, token_pair[1], jnp.where(masked_on, token_pair[0], embedded_rows))
            + position_rows
        )

    entered, entry_back = jax.vjp(entry, embedded, gain_rows[10:12], position)
    state_rows = entered
    kept_all = []
    for depth_index in range(2):
        state_rows, kept = block_forward(
            state_rows,
            attend_all[depth_index],
            expand_all[depth_index],
            flow,
            gain_rows[4 * depth_index : 4 * depth_index + 4],
            same_image,
        )
        kept_all.append(kept)
    state_rows, head_part = lax.optimization_barrier((state_rows, head_part))
    modulate_all = rows_of(0, modulate_rows)
    dense_all = [rows_of(modulate_rows, wide), rows_of(modulate_rows + wide, wide)]
    condition_all = rows_of(modulate_rows + 2 * wide, wide)[:, :D]
    head_all = rows_of(modulate_rows + 3 * wide, wide)[:, : head_table.shape[0]].T
    latent, third_back = jax.vjp(layer_norm, state_rows, gain_rows[8], gain_rows[9])
    latent_low = to_low(latent)
    condition_own = to_low(product_right(latent_low, condition_all))
    condition_rows = jnp.concatenate([condition_own, swap_core(condition_own)], axis=0)
    lifted = product(noisy_low, head_all[:PATCH])
    summed = condition_rows.astype(jnp.float32) + product(
        feature_low, head_all[PATCH : PATCH + FREQ]
    )
    activated, silu_back = jax.vjp(jax.nn.silu, summed)
    activated_low = to_low(activated)
    modulation = product_right(activated_low, modulate_all)
    inner_rows, inner_back = jax.vjp(first_modulate, lifted, modulation)
    inner_low = to_low(inner_rows)
    expanded, dense_back = jax.vjp(jax.nn.gelu, product(inner_low, dense_all[0]))
    expanded_low = to_low(expanded)
    branch = product(expanded_low, dense_all[1])
    outer_rows, outer_back = jax.vjp(last_modulate, lifted, modulation, branch)
    outer_low = to_low(outer_rows)
    predicted = product_right(outer_low, head_all[PATCH + FREQ :])
    residue = predicted - target
    loss_local = jnp.sum(weight_row[:, None] * residue * residue) / PATCH
    predicted_grad = to_low(2.0 * weight_row[:, None] * residue / (PATCH * token_count))
    final_turned = product_left(outer_low, predicted_grad)
    lifted_grad, modulation_grad, branch_grad = outer_back(
        product(predicted_grad, head_all[PATCH + FREQ :])
    )
    branch_low = to_low(branch_grad)
    (expanded_grad,) = dense_back(product_right(branch_low, dense_all[1]))
    expanded_grad_low = to_low(expanded_grad)
    lifted_extra, modulation_extra = inner_back(product_right(expanded_grad_low, dense_all[0]))
    modulation_low = flow.tick(to_low(modulation_grad + modulation_extra))
    flow.begin(
        "spread",
        split_weight_task(modulation_low, activated_low, flow, ("modulate.2", "modulate.3")),
    )
    (summed_grad,) = silu_back(product(modulation_low, modulate_all))
    time_turned = product_left(to_low(summed_grad), feature_low)
    lift_turned = product_left(to_low(lifted_grad + lifted_extra), noisy_low)
    head_turned_grad = jnp.concatenate([lift_turned, time_turned, final_turned], axis=1)
    condition_grad = to_low(
        summed_grad[:halfway] + swap_core(to_low(summed_grad[halfway:])).astype(jnp.float32)
    )
    condition_grad = flow.tick(condition_grad)
    flow.begin(
        "head",
        weight_task(
            [
                (1, inner_low, [expanded_grad_low]),
                (1, expanded_low, [branch_low]),
                (1, condition_grad, [latent_low]),
            ],
            True,
            -1,
            [head_turned_grad],
            3,
        ),
    )
    state_grad, gain_nine, gain_ten = third_back(product(condition_grad, condition_all))

    def modulate_whole():
        (left_parts,), (right_parts,) = (flow.results["modulate.2"], flow.results["modulate.3"])
        quarters = [left_parts[0], right_parts[0], left_parts[1], right_parts[1]]
        return jnp.concatenate(quarters, axis=-1)[0]

    def attend_whole(depth):
        lower = flow.results["lower%d" % depth]
        return jnp.concatenate([*flow.results["attend%d" % depth], lower[1]], axis=0)

    def expand_whole(depth):
        lower, upper = (flow.results["lower%d" % depth], flow.results["upper%d" % depth])
        return jnp.stack([lower[0].reshape(-1, D), upper[0].reshape(-1, D)])

    def dense_whole():
        return jnp.concatenate(flow.results["head"][:2], axis=0)

    gain_parts = [None, None]
    for depth_index in (1, 0):
        state_grad, gain_parts[depth_index] = block_backward(
            state_grad,
            kept_all[depth_index],
            attend_all[depth_index],
            flow,
            depth_index,
            image_row,
        )
    embedded_grad, token_grad, position_grad = entry_back(state_grad)
    embed_delta = product_left(own_patch, to_low(embedded_grad))
    small_delta = jnp.concatenate(
        [
            gain_parts[0],
            gain_parts[1],
            jnp.stack([gain_nine, gain_ten]),
            token_grad,
            embed_delta,
        ],
        axis=0,
    )
    small_delta = small_delta + swap_core(small_delta)
    small_half = small_delta.shape[0] // 2
    small_own = lax.dynamic_slice_in_dim(small_delta, core * small_half, small_half, 0)
    flow.begin(
        "encoder",
        scatter_task([small_own.T[None], position_grad.T[None]], True, -1, [True, False], 1),
    )
    small_pair, position_pair = flow.take("encoder")[0]
    encoder_delta = jnp.concatenate([*small_pair, *position_pair], axis=-1)[0].T
    blocks = [name + str(i) for i in range(2) for name in ("upper", "lower", "attend")]
    flow.take("head", "modulate.2", "modulate.3", *blocks)
    reduced = (
        jnp.concatenate([attend_whole(0), attend_whole(1)], axis=0),
        jnp.concatenate([expand_whole(0), expand_whole(1)], axis=0),
        dense_whole(),
        modulate_whole(),
        flow.results["head"][2][0],
        encoder_delta,
        flow.results["head"][3][0].T,
    )
    velocities = (
        attend_velocity,
        expand_velocity,
        dense_velocity,
        modulate_velocity,
        condition_velocity,
    )

    squares = sum((jnp.sum(member * member) for member in reduced))
    totals = sum_all(jnp.stack([squares, loss_local]))
    square_total, loss_sum = (totals[0], totals[1])
    clip_norm = jnp.sqrt(square_total)
    factor = jnp.minimum(1.0, clip_bound / (clip_norm + 1e-06))
    moments = tuple((muon_keep * velocities[i] + factor * reduced[i] for i in range(5)))
    current = muon_steps(moments)
    devices = lax.axis_size(everywhere)
    masters = (attend_weight, expand_weight, dense_weight, modulate_weight, condition_weight)
    updated = tuple(
        (
            masters[i] * (1.0 - muon_rate * muon_decay)
            - muon_rate
            * max(1.0, current[i].shape[-2] * devices / current[i].shape[-1]) ** 0.5
            * current[i]
            for i in range(5)
        )
    )
    encoder_master, encoder_firsts, encoder_seconds = adam_shard(
        encoder_table, encoder_first, encoder_second, factor * reduced[5]
    )
    table_master, table_firsts, table_seconds = adam_shard(
        head_table, head_first, head_second, factor * reduced[6]
    )
    return (
        loss_sum,
        token_count,
        clip_norm,
        updated[0],
        moments[0],
        updated[1],
        moments[1],
        updated[2],
        moments[2],
        updated[3],
        moments[3],
        updated[4],
        moments[4],
        encoder_master,
        encoder_firsts,
        encoder_seconds,
        table_master,
        table_firsts,
        table_seconds,
    )


def solution(mesh):
    placed = (
        P("dp", None, None),
        P("copy", "dp", None, None),
        P("dp", None),
        P("dp", None),
        P("dp", None),
        P("copy", "dp", None),
        P(None, ("dp", "copy"), None),
        P(None, ("dp", "copy"), None),
        P(None, ("dp", "copy"), None),
        P(None, ("dp", "copy"), None),
        P(None, ("dp", "copy"), None),
        P(None, ("dp", "copy"), None),
        P(("dp", "copy"), None),
        P(("dp", "copy"), None),
        P(("dp", "copy"), None),
        P(("dp", "copy"), None),
        P(None, ("dp", "copy")),
        P(None, ("dp", "copy")),
        P(None, ("dp", "copy")),
        P(None, ("dp", "copy")),
        P(None, ("dp", "copy")),
        P(None, ("dp", "copy")),
    )
    return jax.shard_map(
        per_device,
        mesh=mesh,
        in_specs=placed,
        out_specs=(
            P(),
            P(),
            P(),
            P(None, ("dp", "copy"), None),
            P(None, ("dp", "copy"), None),
            P(None, ("dp", "copy"), None),
            P(None, ("dp", "copy"), None),
            P(None, ("dp", "copy"), None),
            P(None, ("dp", "copy"), None),
            P(("dp", "copy"), None),
            P(("dp", "copy"), None),
            P(("dp", "copy"), None),
            P(("dp", "copy"), None),
            P(None, ("dp", "copy")),
            P(None, ("dp", "copy")),
            P(None, ("dp", "copy")),
            P(None, ("dp", "copy")),
            P(None, ("dp", "copy")),
            P(None, ("dp", "copy")),
        ),
        check_vma=False,
    )
```
